256 devices in a mesh: seq: 64 (over x, z, y_lo), head: 4 (over y_hi, core).
Axes of the slice: x: 4, y: 4 (y_hi: 2, y_lo: 2; y = y_hi * 2 + y_lo), z: 8, core: 2. Of those that a mesh axis runs over, the one named last changes fastest.
Arguments:
- inputs: bfloat16 [131072, 1024], P('seq'), may hold values from -32 to 32
- latent_array: bfloat16 [2048, 1024], P('seq'), may hold values from -16 to 16
- w_query: bfloat16 [1024, 1024], P(None, 'head'), may hold values from -4 to 4
- w_key: bfloat16 [1024, 1024], P(None, 'head'), may hold values from -4 to 4
- w_value: bfloat16 [1024, 1024], P(None, 'head'), may hold values from -0.1875 to 0.1875
- w_out: bfloat16 [1024, 1024], P('head'), may hold values from -0.1875 to 0.1875
- w_up: bfloat16 [1024, 4096], P(None, 'head'), may hold values from -0.1875 to 0.1875
- w_down: bfloat16 [4096, 1024], P('head'), may hold values from -0.09375 to 0.09375
Outputs:
- latent_out: bfloat16 [2048, 1024], P('seq', 'head')
The draws below stay inside these ranges and needn't reach their ends.
All inputs are finite; a program needn't handle non-finite values.
Results may differ from the reference program's by a relative error of at most 0.01355.
The reference program's roundings to bfloat16 on the way count: a program that leaves them out, or rounds other values in their place, can miss the bound.
Values may be sent and summed in bfloat16 or wider, within the bound.
No kernel may reach another device: no remote copies, remote signals or barrier semaphores. Data moves between devices by JAX's collectives and lax.ppermute only.
A program may use at most 320 MiB of HBM per device.

```python
import math
import jax
import jax.numpy as jnp
from jax import lax

D_IN = 1024
D_LAT = 1024
HEADS = 16
HEAD_DIM = 64
MLP_WIDTH = 4096
TOK_DEV = 2048
INNER = 1024
TOKENS = 131072
LATENTS = 2048
N_SEQ = 64


def latent_base(key):
    base_key = jax.random.fold_in(key, 101)
    split_keys = jax.random.split(base_key, 3)
    entries = jax.random.truncated_normal(split_keys[0], -4.0, 4.0, (LATENTS, D_LAT), jnp.float32)
    row_scale = 3.0 ** (jax.random.uniform(split_keys[1], (LATENTS, 1), jnp.float32) - 0.5)
    column_rise = 3.0 ** (jnp.arange(D_LAT, dtype=jnp.float32) / D_LAT - 0.5)
    column_scale = column_rise[None, :] * jax.random.uniform(split_keys[2], (1, D_LAT), jnp.float32, 0.7, 1.3)
    return entries * row_scale * column_scale


def draw_latent_array(key, part):
    return latent_base(key).astype(jnp.bfloat16)


def draw_inputs(key, part):
    key = jax.random.fold_in(key, 2)
    entries = jax.random.truncated_normal(key, -5.0, 5.0, (TOKENS, D_IN), jnp.float32)
    return entries.astype(jnp.bfloat16)


def draw_w_query(key, part):
    key = jax.random.fold_in(key, 3)
    own_part = jax.random.truncated_normal(key, -4.0, 4.0, (D_LAT, INNER), jnp.float32)
    weights = own_part * math.sqrt(3.0 / D_LAT)
    return weights.astype(jnp.bfloat16)


def draw_w_key(key, part):
    key = jax.random.fold_in(key, 4)
    own_part = jax.random.truncated_normal(key, -4.0, 4.0, (D_IN, INNER), jnp.float32)
    weights = own_part * math.sqrt(3.0 / D_IN)
    return weights.astype(jnp.bfloat16)


def block_levels(stream_key, extent, shards, least, high):
    def one(dim, shards_of):
        steps = jax.random.uniform(jax.random.fold_in(jax.random.fold_in(stream_key, 6), dim), (shards_of,), jnp.float32, least / len(shards), high / len(shards))
        return jnp.repeat(jnp.exp(steps), extent[dim] // shards_of).reshape((-1,) + (1,) * (len(extent) - dim - 1))

    loudness = one(*shards[0])
    for cut in shards[1:]:
        loudness = loudness * one(*cut)
    return loudness


def normal_values(stream_key, extent, deviation, reach, cuts=(), kind=jnp.bfloat16):
    loudness = block_levels(stream_key, extent, cuts, -0.22, 0.18) if cuts else 1.0
    values = jax.random.normal(stream_key, extent, jnp.float32) * deviation * loudness
    return jnp.minimum(jnp.maximum(values, -reach), reach).astype(kind)


def setup_inputs(seed: int = 0) -> dict:
    splits = jax.random.split(jax.random.key(seed), 9)
    inputs = draw_inputs(jax.random.fold_in(splits[8], 71), 0)
    latent_array = draw_latent_array(jax.random.fold_in(splits[8], 71), 0)
    w_query = draw_w_query(jax.random.fold_in(splits[8], 71), 0)
    w_key = draw_w_key(jax.random.fold_in(splits[8], 71), 0)
    w_value = normal_values(splits[4], (D_IN, INNER), D_IN ** -0.5, 0.1875, ((1, 4),))
    w_out = normal_values(splits[5], (INNER, D_LAT), INNER ** -0.5, 0.1875, ((0, 4),))
    w_up = normal_values(splits[6], (D_LAT, MLP_WIDTH), D_LAT ** -0.5, 0.1875, ((1, 4),))
    w_down = normal_values(splits[7], (MLP_WIDTH, D_LAT), MLP_WIDTH ** -0.5, 0.09375, ((0, 4),))
    return dict(inputs=inputs, latent_array=latent_array, w_query=w_query, w_key=w_key, w_value=w_value, w_out=w_out, w_up=w_up, w_down=w_down)


def layer_norm(entries):
    widened = entries.astype(jnp.float32)
    width = widened.shape[-1]
    row_mean = lax.optimization_barrier(jnp.sum(widened, axis=-1, keepdims=True)) / width
    row_square = lax.optimization_barrier(jnp.sum(widened * widened, axis=-1, keepdims=True)) / width
    row_var = row_square - row_mean * row_mean
    return (widened - row_mean) * lax.rsqrt(row_var + 1e-05)

def softmax_merge(earlier, later):
    high_one, sum_one, acc_one = earlier
    high_two, sum_two, acc_two = later
    highest = jnp.maximum(high_one, high_two)
    factor_one = jnp.exp(high_one - highest)
    factor_two = jnp.exp(high_two - highest)
    total = factor_one * sum_one + factor_two * sum_two
    accum = factor_one[..., None] * acc_one + factor_two[..., None] * acc_two
    return (highest, total, accum)

def reference(inputs, latent_array, w_query, w_key, w_value, w_out, w_up, w_down):
    score_scale = HEAD_DIM ** (-0.5)
    normed_latent = layer_norm(latent_array).astype(jnp.bfloat16)
    queries = (jnp.dot(normed_latent, w_query, preferred_element_type=jnp.float32) * score_scale).astype(jnp.bfloat16)
    query_heads = queries.reshape(LATENTS, HEADS, HEAD_DIM).astype(jnp.float32)

    def shard_step(carried, shard_index):
        start_row = (shard_index * TOK_DEV).astype(jnp.int32)
        input_piece = lax.dynamic_slice_in_dim(inputs, start_row, TOK_DEV, 0)
        normed = layer_norm(input_piece).astype(jnp.bfloat16)
        key_heads = jnp.dot(normed, w_key, preferred_element_type=jnp.float32).astype(jnp.bfloat16)
        value_heads = jnp.dot(normed, w_value, preferred_element_type=jnp.float32).astype(jnp.bfloat16)
        key_heads = key_heads.reshape(TOK_DEV, HEADS, HEAD_DIM).astype(jnp.float32)
        value_heads = value_heads.reshape(TOK_DEV, HEADS, HEAD_DIM).astype(jnp.float32)
        scores = jnp.einsum('lhd,thd->lht', query_heads, key_heads)
        shard_max = lax.optimization_barrier(jnp.max(scores, axis=2))
        weights = jnp.exp(scores - shard_max[..., None]).astype(jnp.bfloat16).astype(jnp.float32)
        shard_sum = lax.optimization_barrier(jnp.sum(weights, axis=2))
        shard_acc = jnp.einsum('lht,thd->lhd', weights, value_heads)
        return (softmax_merge(carried, (shard_max, shard_sum, shard_acc)), None)
    start_state = (jnp.full((LATENTS, HEADS), -1e+30, jnp.float32), jnp.zeros((LATENTS, HEADS), jnp.float32), jnp.zeros((LATENTS, HEADS, HEAD_DIM), jnp.float32))
    merged, unused = lax.scan(shard_step, start_state, jnp.arange(N_SEQ, dtype=jnp.int32))
    highest, total, accum = merged
    attended = (accum / total[..., None]).reshape(LATENTS, INNER).astype(jnp.bfloat16)
    residual = (latent_array.astype(jnp.float32) + jnp.dot(attended, w_out, preferred_element_type=jnp.float32)).astype(jnp.bfloat16)
    normed_resid = layer_norm(residual).astype(jnp.bfloat16)
    hidden_units = jax.nn.gelu(jnp.dot(normed_resid, w_up, preferred_element_type=jnp.float32), approximate=False).astype(jnp.bfloat16)
    return (residual.astype(jnp.float32) + jnp.dot(hidden_units, w_down, preferred_element_type=jnp.float32)).astype(jnp.bfloat16)
```

```python
import functools

import jax
import jax.numpy as jnp
from jax import lax
from jax.experimental import pallas as pl
from jax.experimental.pallas import tpu as pltpu
from jax.sharding import Mesh
from jax.sharding import PartitionSpec as P

HEAD_DIM = 64
HEADS_HERE = 4
LANES = 128
SEQ = ("x", "z", "ylo")
HEAD = ("yhi", "core")
BF16 = jnp.bfloat16
F32 = jnp.float32
NT = (((1,), (1,)), ((), ()))
NN = (((1,), (0,)), ((), ()))


def product(left, right, numbers=NN):
    return lax.dot_general(left, right, numbers, preferred_element_type=F32)


def params(mib):
    return pltpu.CompilerParams(vmem_limit_bytes=mib * 2**20)


def norm_rows(widened):
    width = widened.shape[-1]
    row_mean = jnp.sum(widened, axis=-1, keepdims=True) / width
    row_square = jnp.sum(widened * widened, axis=-1, keepdims=True) / width
    row_var = row_square - row_mean * row_mean
    return (widened - row_mean) * lax.rsqrt(row_var + 1e-05)


def query_kernel(latent_ref, w_ref, out_ref):
    normed = norm_rows(latent_ref[...].astype(F32)).astype(BF16)
    out_ref[...] = (product(normed, w_ref[...]) * HEAD_DIM ** (-0.5)).astype(BF16)


def make_queries(latent, w_query):
    return pl.pallas_call(
        query_kernel,
        out_shape=jax.ShapeDtypeStruct((latent.shape[0], w_query.shape[1]), BF16),
        compiler_params=params(8),
        name="make_queries",
    )(latent, w_query)


def key_value_kernel(x_ref, w_key_ref, w_value_ref, key_ref, value_ref):
    normed = norm_rows(x_ref[...].astype(F32)).astype(BF16)
    keys = product(normed, w_key_ref[...]).astype(BF16)
    vals = product(normed, w_value_ref[...])
    lane = lax.broadcasted_iota(jnp.int32, (vals.shape[0], LANES), 1)
    low = lane < HEAD_DIM
    for head in range(HEADS_HERE):
        key_ref[head] = keys[:, head * HEAD_DIM : (head + 1) * HEAD_DIM]
        pair = vals[:, head // 2 * LANES : (head // 2 + 1) * LANES]
        one = jnp.where(lane == (HEAD_DIM if head % 2 == 0 else 0), 1.0, 0.0)
        kept = jnp.where(low, pair, one) if head % 2 == 0 else jnp.where(low, one, pair)
        value_ref[head] = kept.astype(BF16)


def make_keys_values(x, w_key, w_value):
    tokens, width = x.shape
    block = 512
    inner = w_key.shape[1]
    return pl.pallas_call(
        key_value_kernel,
        grid=(tokens // block,),
        in_specs=[
            pl.BlockSpec((block, width), lambda i: (i, 0)),
            pl.BlockSpec((width, inner), lambda i: (0, 0)),
            pl.BlockSpec((width, inner), lambda i: (0, 0)),
        ],
        out_specs=[
            pl.BlockSpec((HEADS_HERE, block, HEAD_DIM), lambda i: (0, i, 0)),
            pl.BlockSpec((HEADS_HERE, block, LANES), lambda i: (0, i, 0)),
        ],
        out_shape=[
            jax.ShapeDtypeStruct((HEADS_HERE, tokens, HEAD_DIM), BF16),
            jax.ShapeDtypeStruct((HEADS_HERE, tokens, LANES), BF16),
        ],
        compiler_params=params(24),
        name="make_keys_values",
    )(x, w_key, w_value)


def split_levels(levels, lane):
    first = levels.astype(BF16).astype(F32)
    rest = levels - first
    second = rest.astype(BF16).astype(F32)
    third = rest - second
    parts = jnp.where(lane < 4, first, jnp.where(lane < 8, second, third))
    return jnp.where(lane < 12, parts, 0.0).astype(BF16)


def attend_kernel(count, *refs):
    query_refs, (key_ref, value_ref) = refs[:count], refs[count : count + 2]
    out_refs = refs[count + 2 :]
    rows = query_refs[0].shape[0]
    total_rows = rows * count

    def scores_of(head):
        columns = slice(head * HEAD_DIM, (head + 1) * HEAD_DIM)
        parts = [ref[:, columns] for ref in query_refs]
        part = parts[0] if count == 1 else jnp.concatenate(parts, axis=0)
        return product(part, key_ref[head], NT)

    lane = lax.broadcasted_iota(jnp.int32, (total_rows, LANES), 1)
    levels = jnp.zeros((total_rows, LANES), F32)
    following = scores_of(0)
    even = None
    for head in range(HEADS_HERE):
        scores = following
        if head + 1 < HEADS_HERE:
            following = scores_of(head + 1)
        highest = jnp.max(scores, axis=1, keepdims=True)
        weights = jnp.exp(scores - highest).astype(BF16)
        accum = product(weights, value_ref[head])
        place = HEAD_DIM if head % 2 == 0 else 0
        total = accum[:, place : place + 1]
        mean = accum * (1.0 / total)
        levels = jnp.where(lane % 4 == head, highest + jnp.log(total), levels)
        if head % 2 == 0:
            even = mean
        else:
            both = jnp.where(lane < HEAD_DIM, even, mean).astype(BF16)
            for i, ref in enumerate(out_refs):
                columns = slice(head // 2 * LANES, (head // 2 + 1) * LANES)
                ref[:, columns] = both[i * rows : (i + 1) * rows]
    packed = split_levels(levels, lane)
    for i, ref in enumerate(out_refs):
        ref[:, 2 * LANES :] = packed[i * rows : (i + 1) * rows]


def attend(chunks, keys, values):
    count = len(chunks)
    rows = chunks[0].shape[0]
    return pl.pallas_call(
        functools.partial(attend_kernel, count),
        out_shape=[jax.ShapeDtypeStruct((rows, 3 * LANES), BF16)] * count,
        compiler_params=params(40),
        name="attend",
    )(*chunks, keys, values)


def spread_matrix():
    source = lax.broadcasted_iota(jnp.int32, (LANES, 2 * LANES), 0)
    target = lax.broadcasted_iota(jnp.int32, (LANES, 2 * LANES), 1)
    hit = (source < 12) & (source % 4 == target // HEAD_DIM)
    return jnp.where(hit, 1.0, 0.0).astype(BF16)


def merged(pieces):
    spread = spread_matrix()
    levels = [product(piece[:, 2 * LANES :], spread) for piece in pieces]
    highest = functools.reduce(jnp.maximum, levels)
    total, accum = None, None
    for piece, level in zip(pieces, levels):
        factor = jnp.exp(level - highest)
        term = factor * piece[:, : 2 * LANES].astype(F32)
        total = factor if total is None else total + factor
        accum = term if accum is None else accum + term
    return accum / total, highest, total


def merge_kernel(*refs):
    pieces = [ref[...] for ref in refs[:-1]]
    out_ref = refs[-1]
    mean, highest, total = merged(pieces)
    out_ref[:, : 2 * LANES] = mean.astype(BF16)
    levels = highest + jnp.log(total)
    lane = lax.broadcasted_iota(jnp.int32, (levels.shape[0], LANES), 1)
    one, two = levels[:, :LANES], levels[:, LANES:]
    one_other, two_other = pltpu.roll(one, HEAD_DIM, 1), pltpu.roll(two, HEAD_DIM, 1)
    head = lane % 4
    picked = jnp.where(
        head == 0, one, jnp.where(head == 1, one_other, jnp.where(head == 2, two, two_other))
    )
    out_ref[:, 2 * LANES :] = split_levels(picked, lane)


def merge(pieces):
    return pl.pallas_call(
        merge_kernel,
        out_shape=jax.ShapeDtypeStruct(pieces[0].shape, BF16),
        compiler_params=params(24),
        name="merge",
    )(*pieces)


def finish_kernel(pieces_ref, out_ref):
    mean, highest, total = merged([pieces_ref[i] for i in range(pieces_ref.shape[0])])
    out_ref[...] = mean.astype(BF16)


def finish(pieces):
    return pl.pallas_call(
        finish_kernel,
        out_shape=jax.ShapeDtypeStruct((pieces.shape[1], 2 * LANES), BF16),
        compiler_params=params(8),
        name="finish",
    )(pieces)


def mlp_kernel(att_ref, latent_ref, w_out_ref, w_up_ref, w_down_ref, resid_ref, share_ref):
    count, _, inner = att_ref.shape
    projected = latent_ref[...].astype(F32) + functools.reduce(
        jnp.add,
        [product(att_ref[i], w_out_ref[i * inner : (i + 1) * inner]) for i in range(count)],
    )
    residual = projected.astype(BF16)
    normed = norm_rows(residual.astype(F32)).astype(BF16)
    raised = product(normed, w_up_ref[...])
    hidden = (0.5 * raised * (1.0 + lax.erf(raised * 0.5**0.5))).astype(BF16)
    share = product(hidden, w_down_ref[...]).astype(BF16)
    columns = share.shape[1] // count
    for i in range(count):
        resid_ref[i] = residual[:, i * columns : (i + 1) * columns]
        share_ref[i] = share[:, i * columns : (i + 1) * columns]


def mlp(att, latent, w_out, w_up, w_down):
    count, rows, _ = att.shape
    out = jax.ShapeDtypeStruct((count, rows, latent.shape[1] // count), BF16)
    return pl.pallas_call(
        mlp_kernel,
        out_shape=[out, out],
        compiler_params=params(24),
        name="mlp",
    )(att, latent, w_out, w_up, w_down)


def close_kernel(place_ref, resid_ref, share_ref, out_ref):
    total = functools.reduce(jnp.add, [share_ref[i].astype(F32) for i in range(share_ref.shape[0])])
    out_ref[...] = (resid_ref[place_ref[0]].astype(F32) + total).astype(BF16)


def close(place, resid, shares):
    return pl.pallas_call(
        close_kernel,
        in_specs=[
            pl.BlockSpec(memory_space=pltpu.SMEM),
            pl.BlockSpec(memory_space=pltpu.VMEM),
            pl.BlockSpec(memory_space=pltpu.VMEM),
        ],
        out_shape=jax.ShapeDtypeStruct(resid.shape[1:], BF16),
        compiler_params=params(8),
        name="close",
    )(place, resid, shares)


def moved(value, by_x, by_y):
    size_x, size_y = lax.axis_size("x"), lax.axis_size("ylo")
    pairs = []
    for x in range(size_x):
        for y in range(size_y):
            target = (x + by_x) % size_x * size_y + (y + by_y) % size_y
            pairs.append((x * size_y + y, target))
    return lax.ppermute(value, ("x", "ylo"), pairs)


def along(value, axis, by):
    size = lax.axis_size(axis)
    return lax.ppermute(value, axis, [(i, (i + by) % size) for i in range(size)])


def on_device(inputs, latent, w_query, w_key, w_value, w_out, w_up, w_down):
    rows = latent.shape[0]
    size_z = lax.axis_size("z")
    w_out_all = lax.all_gather(w_out, HEAD, axis=0, tiled=True)
    queries = make_queries(latent, w_query)
    wide = jnp.broadcast_to(queries[None], (size_z,) + queries.shape)
    column = lax.all_to_all(wide, "z", 0, 0, tiled=True).reshape(size_z * rows, -1)
    keys, values = make_keys_values(inputs, w_key, w_value)
    shifts = [(1, 0), (3, 0), (2, 0), (2, 1), (1, 1), (3, 1), (0, 1)]
    arrived = {shift: moved(column, *shift) for shift in shifts}
    pieces = []
    groups = [[None], shifts[0:2], shifts[2:4], shifts[4:6], shifts[6:7]]
    for group in groups:
        chunks = [column if shift is None else arrived[shift] for shift in group]
        outs = attend(chunks, keys, values)
        for shift, out in zip(group, outs):
            if shift is not None:
                out = moved(out, -shift[0], -shift[1])
            pieces.append(out)
    block = merge(pieces)
    parts = lax.all_to_all(block.reshape(size_z, rows, -1), "z", 0, 0, tiled=True)
    attended = finish(parts)
    att = lax.all_gather(attended, HEAD, axis=0)
    resid, shares = mlp(att, latent, w_out_all, w_up, w_down)
    shares = lax.all_to_all(shares, HEAD, 0, 0, tiled=True)
    place = lax.axis_index(HEAD).astype(jnp.int32).reshape(1)
    return close(place, resid, shares)


def solution(mesh):
    fine = Mesh(mesh.devices.reshape(4, 8, 2, 2, 2), SEQ + HEAD)
    placed = (
        P(SEQ, None),
        P(SEQ, None),
        P(None, HEAD),
        P(None, HEAD),
        P(None, HEAD),
        P(HEAD, None),
        P(None, HEAD),
        P(HEAD, None),
    )
    return jax.shard_map(
        on_device, mesh=fine, in_specs=placed, out_specs=P(SEQ, HEAD), check_vma=False
    )
```

```python
import functools

import jax
import jax.numpy as jnp
from jax import lax
from jax.experimental import pallas as pl
from jax.experimental.pallas import tpu as pltpu
from jax.sharding import Mesh
from jax.sharding import PartitionSpec as P

HEAD_DIM = 64
HEADS_HERE = 4
LANES = 128
SEQ = ("xhi", "xlo", "z", "ylo")
FAR = ("xhi", "z")
HEAD = ("yhi", "core")
BF16 = jnp.bfloat16
F32 = jnp.float32
NT = (((1,), (1,)), ((), ()))
NN = (((1,), (0,)), ((), ()))


def product(left, right, numbers=NN):
    return lax.dot_general(left, right, numbers, preferred_element_type=F32)


def params(mib):
    return pltpu.CompilerParams(vmem_limit_bytes=mib * 2**20)


def norm_rows(widened):
    width = widened.shape[-1]
    row_mean = jnp.sum(widened, axis=-1, keepdims=True) / width
    row_square = jnp.sum(widened * widened, axis=-1, keepdims=True) / width
    row_var = row_square - row_mean * row_mean
    return (widened - row_mean) * lax.rsqrt(row_var + 1e-05)


def query_kernel(latent_hbm, w_hbm, out_ref, latent_ref, w_ref, sems):
    copies = [
        pltpu.make_async_copy(latent_hbm, latent_ref, sems.at[0]),
        pltpu.make_async_copy(w_hbm, w_ref, sems.at[1]),
    ]
    for copy in copies:
        copy.start()
    copies[0].wait()
    normed = norm_rows(latent_ref[...].astype(F32)).astype(BF16)
    copies[1].wait()
    out_ref[...] = (product(normed, w_ref[...]) * HEAD_DIM ** (-0.5)).astype(BF16)


def make_queries(latent, w_query):
    return pl.pallas_call(
        query_kernel,
        in_specs=[pl.BlockSpec(memory_space=pltpu.HBM)] * 2,
        out_shape=jax.ShapeDtypeStruct((latent.shape[0], w_query.shape[1]), BF16),
        scratch_shapes=[
            pltpu.VMEM(latent.shape, BF16),
            pltpu.VMEM(w_query.shape, BF16),
            pltpu.SemaphoreType.DMA((2,)),
        ],
        compiler_params=params(8),
        name="make_queries",
    )(latent, w_query)


def key_value_kernel(
    block, x_hbm, w_key_hbm, w_value_hbm, key_ref, value_ref, x_ref, w_key_ref, w_value_ref, sems
):
    tokens = x_ref.shape[0]
    weights = [
        pltpu.make_async_copy(w_key_hbm, w_key_ref, sems.at[0]),
        pltpu.make_async_copy(w_value_hbm, w_value_ref, sems.at[1]),
    ]
    spans = [slice(start, start + block) for start in range(0, tokens, block)]
    copies = [
        pltpu.make_async_copy(x_hbm.at[span], x_ref.at[span], sems.at[2 + i])
        for i, span in enumerate(spans)
    ]
    for copy in copies[:1] + weights + copies[1:]:
        copy.start()
    lane = lax.broadcasted_iota(jnp.int32, (block, LANES), 1)
    low = lane < HEAD_DIM
    for i, span in enumerate(spans):
        copies[i].wait()
        normed = norm_rows(x_ref[span].astype(F32)).astype(BF16)
        if i == 0:
            weights[0].wait()
            weights[1].wait()
        keys = product(normed, w_key_ref[...]).astype(BF16)
        vals = product(normed, w_value_ref[...])
        for head in range(HEADS_HERE):
            key_ref[head, span] = keys[:, head * HEAD_DIM : (head + 1) * HEAD_DIM]
            pair = vals[:, head // 2 * LANES : (head // 2 + 1) * LANES]
            one = jnp.where(lane == (HEAD_DIM if head % 2 == 0 else 0), 1.0, 0.0)
            kept = jnp.where(low, pair, one) if head % 2 == 0 else jnp.where(low, one, pair)
            value_ref[head, span] = kept.astype(BF16)


def make_keys_values(x, w_key, w_value):
    tokens = x.shape[0]
    block = 512
    return pl.pallas_call(
        functools.partial(key_value_kernel, block),
        in_specs=[pl.BlockSpec(memory_space=pltpu.HBM)] * 3,
        out_shape=[
            jax.ShapeDtypeStruct((HEADS_HERE, tokens, HEAD_DIM), BF16),
            jax.ShapeDtypeStruct((HEADS_HERE, tokens, LANES), BF16),
        ],
        scratch_shapes=[
            pltpu.VMEM(x.shape, BF16),
            pltpu.VMEM(w_key.shape, BF16),
            pltpu.VMEM(w_value.shape, BF16),
            pltpu.SemaphoreType.DMA((2 + tokens // block,)),
        ],
        compiler_params=params(32),
        name="make_keys_values",
    )(x, w_key, w_value)


def split_levels(levels, lane):
    first = levels.astype(BF16).astype(F32)
    rest = levels - first
    second = rest.astype(BF16).astype(F32)
    third = rest - second
    parts = jnp.where(lane < 4, first, jnp.where(lane < 8, second, third))
    return jnp.where(lane < 12, parts, 0.0).astype(BF16)


def attend_kernel(count, *refs):
    query_refs, (key_ref, value_ref) = refs[:count], refs[count : count + 2]
    out_refs = refs[count + 2 :]
    rows = query_refs[0].shape[0]
    total_rows = rows * count

    def scores_of(head):
        columns = slice(head * HEAD_DIM, (head + 1) * HEAD_DIM)
        parts = [ref[:, columns] for ref in query_refs]
        part = parts[0] if count == 1 else jnp.concatenate(parts, axis=0)
        return product(part, key_ref[head], NT)

    lane = lax.broadcasted_iota(jnp.int32, (total_rows, LANES), 1)
    levels = jnp.zeros((total_rows, LANES), F32)
    following = scores_of(0)
    even = None
    for head in range(HEADS_HERE):
        scores = following
        if head + 1 < HEADS_HERE:
            following = scores_of(head + 1)
        highest = jnp.max(scores, axis=1, keepdims=True)
        weights = jnp.exp(scores - highest).astype(BF16)
        accum = product(weights, value_ref[head])
        place = HEAD_DIM if head % 2 == 0 else 0
        total = accum[:, place : place + 1]
        mean = accum * (1.0 / total)
        levels = jnp.where(lane % 4 == head, highest + jnp.log(total), levels)
        if head % 2 == 0:
            even = mean
        else:
            both = jnp.where(lane < HEAD_DIM, even, mean).astype(BF16)
            for i, ref in enumerate(out_refs):
                columns = slice(head // 2 * LANES, (head // 2 + 1) * LANES)
                ref[:, columns] = both[i * rows : (i + 1) * rows]
    packed = split_levels(levels, lane)
    for i, ref in enumerate(out_refs):
        ref[:, 2 * LANES :] = packed[i * rows : (i + 1) * rows]


def attend(chunks, keys, values):
    count = len(chunks)
    rows = chunks[0].shape[0]
    return pl.pallas_call(
        functools.partial(attend_kernel, count),
        out_shape=[jax.ShapeDtypeStruct((rows, 3 * LANES), BF16)] * count,
        compiler_params=params(40),
        name="attend",
    )(*chunks, keys, values)


def spread_matrix():
    source = lax.broadcasted_iota(jnp.int32, (LANES, 2 * LANES), 0)
    target = lax.broadcasted_iota(jnp.int32, (LANES, 2 * LANES), 1)
    hit = (source < 12) & (source % 4 == target // HEAD_DIM)
    return jnp.where(hit, 1.0, 0.0).astype(BF16)


def merged(pieces):
    spread = spread_matrix()
    levels = [product(piece[:, 2 * LANES :], spread) for piece in pieces]
    highest = functools.reduce(jnp.maximum, levels)
    total, accum = None, None
    for piece, level in zip(pieces, levels):
        factor = jnp.exp(level - highest)
        term = factor * piece[:, : 2 * LANES].astype(F32)
        total = factor if total is None else total + factor
        accum = term if accum is None else accum + term
    return accum / total, highest, total


def merge_kernel(*refs):
    pieces = [ref[...] for ref in refs[:-1]]
    out_ref = refs[-1]
    mean, highest, total = merged(pieces)
    out_ref[:, : 2 * LANES] = mean.astype(BF16)
    levels = highest + jnp.log(total)
    lane = lax.broadcasted_iota(jnp.int32, (levels.shape[0], LANES), 1)
    one, two = levels[:, :LANES], levels[:, LANES:]
    one_other, two_other = pltpu.roll(one, HEAD_DIM, 1), pltpu.roll(two, HEAD_DIM, 1)
    head = lane % 4
    picked = jnp.where(
        head == 0, one, jnp.where(head == 1, one_other, jnp.where(head == 2, two, two_other))
    )
    out_ref[:, 2 * LANES :] = split_levels(picked, lane)


def merge(pieces):
    return pl.pallas_call(
        merge_kernel,
        out_shape=jax.ShapeDtypeStruct(pieces[0].shape, BF16),
        compiler_params=params(24),
        name="merge",
    )(*pieces)


def finish_kernel(pieces_ref, out_ref):
    mean, highest, total = merged([pieces_ref[i] for i in range(pieces_ref.shape[0])])
    out_ref[...] = mean.astype(BF16)


def finish(pieces):
    return pl.pallas_call(
        finish_kernel,
        out_shape=jax.ShapeDtypeStruct((pieces.shape[1], 2 * LANES), BF16),
        compiler_params=params(8),
        name="finish",
    )(pieces)


def mlp_kernel(one_ref, other_ref, latent_ref, wide_one_ref, wide_other_ref, w_up_ref, w_down_ref, resid_ref, share_ref):
    count, _, columns = resid_ref.shape
    projected = latent_ref[...].astype(F32)
    for att_ref, w_ref in ((one_ref, wide_one_ref), (other_ref, wide_other_ref)):
        for i in range(att_ref.shape[0]):
            projected += product(att_ref[i], w_ref[i])
    residual = projected.astype(BF16)
    normed = norm_rows(residual.astype(F32)).astype(BF16)
    raised = product(normed, w_up_ref[...])
    hidden = (0.5 * raised * (1.0 + lax.erf(raised * 0.5**0.5))).astype(BF16)
    share = product(hidden, w_down_ref[...]).astype(BF16)
    for i in range(count):
        resid_ref[i] = residual[:, i * columns : (i + 1) * columns]
        share_ref[i] = share[:, i * columns : (i + 1) * columns]


def mlp(one, other, latent, wide_one, wide_other, w_up, w_down):
    rows = latent.shape[0]
    count = 2 * one.shape[0]
    out = jax.ShapeDtypeStruct((count, rows, latent.shape[1] // count), BF16)
    return pl.pallas_call(
        mlp_kernel,
        out_shape=[out, out],
        compiler_params=params(24),
        name="mlp",
    )(one, other, latent, wide_one, wide_other, w_up, w_down)


def close_kernel(place_ref, resid_ref, kept_ref, *refs):
    out_ref = refs[-1]
    place = place_ref[0]
    total = kept_ref[place].astype(F32)
    for ref in refs[:-1]:
        total += ref[...].astype(F32)
    out_ref[...] = (resid_ref[place].astype(F32) + total).astype(BF16)


def close(place, resid, kept, *others):
    return pl.pallas_call(
        close_kernel,
        in_specs=[pl.BlockSpec(memory_space=pltpu.SMEM)]
        + [pl.BlockSpec(memory_space=pltpu.VMEM)] * (2 + len(others)),
        out_shape=jax.ShapeDtypeStruct(resid.shape[1:], BF16),
        compiler_params=params(8),
        name="close",
    )(place, resid, kept, *others)


def swapped(value, axis):
    return lax.ppermute(value, axis, [(0, 1), (1, 0)])


def crossed(value, by_x, by_y):
    pairs = [(i, i ^ (by_x * 2 + by_y)) for i in range(4)]
    return lax.ppermute(value, ("xlo", "ylo"), pairs)


def on_device(inputs, latent, w_query, w_key, w_value, w_out, w_up, w_down):
    rows = latent.shape[0]
    far = lax.axis_size(FAR)
    wide_one = jnp.stack([w_out, swapped(w_out, "yhi")])
    wide_other = swapped(wide_one, "core")
    queries = make_queries(latent, w_query)
    wide = jnp.broadcast_to(queries[None], (far,) + queries.shape)
    column = lax.all_to_all(wide, FAR, 0, 0, tiled=True).reshape(far * rows, -1)
    keys, values = make_keys_values(inputs, w_key, w_value)
    shifts = [(0, 1), (1, 1), (1, 0)]
    arrived = [crossed(column, *shift) for shift in shifts]
    pieces = []
    for shift, chunk in zip(shifts, arrived):
        pieces.append(crossed(attend([chunk], keys, values)[0], *shift))
    pieces.append(attend([column], keys, values)[0])
    block = merge(pieces)
    parts = lax.all_to_all(block.reshape(far, rows, -1), FAR, 0, 0, tiled=True)
    attended = finish(parts)
    att_one = jnp.stack([attended, swapped(attended, "yhi")])
    att_other = swapped(att_one, "core")
    resid, shares = mlp(att_one, att_other, latent, wide_one, wide_other, w_up, w_down)
    yhi, core = lax.axis_index("yhi"), lax.axis_index("core")

    def block_of(high, low):
        return lax.dynamic_index_in_dim(shares, high * 2 + low, 0, keepdims=False)

    by_core = swapped(block_of(yhi, 1 - core), "core")
    by_high = swapped(block_of(1 - yhi, core), "yhi")
    by_both = lax.ppermute(block_of(1 - yhi, 1 - core), HEAD, [(i, 3 - i) for i in range(4)])
    place = (yhi * 2 + core).astype(jnp.int32).reshape(1)
    return close(place, resid, shares, by_core, by_high, by_both)


def solution(mesh):
    fine = Mesh(mesh.devices.reshape(2, 2, 8, 2, 2, 2), SEQ + HEAD)
    placed = (
        P(SEQ, None),
        P(SEQ, None),
        P(None, HEAD),
        P(None, HEAD),
        P(None, HEAD),
        P(HEAD, None),
        P(None, HEAD),
        P(HEAD, None),
    )
    return jax.shard_map(
        on_device, mesh=fine, in_specs=placed, out_specs=P(SEQ, HEAD), check_vma=False
    )
```

```python
import functools

import jax
import jax.numpy as jnp
from jax import lax
from jax.experimental import pallas as pl
from jax.experimental.pallas import tpu as pltpu
from jax.sharding import Mesh
from jax.sharding import PartitionSpec as P

HEAD_DIM = 64
HEADS_HERE = 4
LANES = 128
SEQ = ("x", "zhi", "zlo", "ylo")
HEAD = ("yhi", "core")
BF16 = jnp.bfloat16
F32 = jnp.float32
NT = (((1,), (1,)), ((), ()))
NN = (((1,), (0,)), ((), ()))


def product(left, right, numbers=NN):
    return lax.dot_general(left, right, numbers, preferred_element_type=F32)


def params(mib):
    return pltpu.CompilerParams(vmem_limit_bytes=mib * 2**20)


def norm_rows(widened):
    width = widened.shape[-1]
    row_mean = jnp.sum(widened, axis=-1, keepdims=True) / width
    row_square = jnp.sum(widened * widened, axis=-1, keepdims=True) / width
    row_var = row_square - row_mean * row_mean
    return (widened - row_mean) * lax.rsqrt(row_var + 1e-05)


def in_hbm(value):
    return pltpu.with_memory_space_constraint(value, pltpu.HBM)


def query_kernel(latent_hbm, w_hbm, out_ref, latent_ref, w_ref, sems):
    copies = [
        pltpu.make_async_copy(latent_hbm, latent_ref, sems.at[0]),
        pltpu.make_async_copy(w_hbm, w_ref, sems.at[1]),
    ]
    for copy in copies:
        copy.start()
    copies[0].wait()
    normed = norm_rows(latent_ref[...].astype(F32)).astype(BF16)
    copies[1].wait()
    out_ref[...] = (product(normed, w_ref[...]) * HEAD_DIM ** (-0.5)).astype(BF16)


def make_queries(latent, w_query):
    return pl.pallas_call(
        query_kernel,
        in_specs=[pl.BlockSpec(memory_space=pltpu.HBM)] * 2,
        out_shape=jax.ShapeDtypeStruct((latent.shape[0], w_query.shape[1]), BF16),
        scratch_shapes=[
            pltpu.VMEM(latent.shape, BF16),
            pltpu.VMEM(w_query.shape, BF16),
            pltpu.SemaphoreType.DMA((2,)),
        ],
        compiler_params=params(8),
        name="make_queries",
    )(in_hbm(latent), in_hbm(w_query))


def key_value_kernel(
    block, x_hbm, w_key_hbm, w_value_hbm, key_ref, value_ref, x_ref, w_key_ref, w_value_ref, sems
):
    tokens = x_ref.shape[0]
    weights = [
        pltpu.make_async_copy(w_key_hbm, w_key_ref, sems.at[0]),
        pltpu.make_async_copy(w_value_hbm, w_value_ref, sems.at[1]),
    ]
    spans = [slice(start, start + block) for start in range(0, tokens, block)]
    copies = [
        pltpu.make_async_copy(x_hbm.at[span], x_ref.at[span], sems.at[2 + i])
        for i, span in enumerate(spans)
    ]
    for copy in copies[:1] + weights + copies[1:]:
        copy.start()
    lane = lax.broadcasted_iota(jnp.int32, (block, LANES), 1)
    low = lane < HEAD_DIM
    for i, span in enumerate(spans):
        copies[i].wait()
        normed = norm_rows(x_ref[span].astype(F32)).astype(BF16)
        if i == 0:
            weights[0].wait()
            weights[1].wait()
        keys = product(normed, w_key_ref[...]).astype(BF16)
        vals = product(normed, w_value_ref[...])
        for head in range(HEADS_HERE):
            key_ref[head, span] = keys[:, head * HEAD_DIM : (head + 1) * HEAD_DIM]
            pair = vals[:, head // 2 * LANES : (head // 2 + 1) * LANES]
            one = jnp.where(lane == (HEAD_DIM if head % 2 == 0 else 0), 1.0, 0.0)
            kept = jnp.where(low, pair, one) if head % 2 == 0 else jnp.where(low, one, pair)
            value_ref[head, span] = kept.astype(BF16)


def make_keys_values(x, w_key, w_value):
    tokens = x.shape[0]
    block = 512
    return pl.pallas_call(
        functools.partial(key_value_kernel, block),
        in_specs=[pl.BlockSpec(memory_space=pltpu.HBM)] * 3,
        out_shape=[
            jax.ShapeDtypeStruct((HEADS_HERE, tokens, HEAD_DIM), BF16),
            jax.ShapeDtypeStruct((HEADS_HERE, tokens, LANES), BF16),
        ],
        scratch_shapes=[
            pltpu.VMEM(x.shape, BF16),
            pltpu.VMEM(w_key.shape, BF16),
            pltpu.VMEM(w_value.shape, BF16),
            pltpu.SemaphoreType.DMA((2 + tokens // block,)),
        ],
        compiler_params=params(32),
        name="make_keys_values",
    )(in_hbm(x), in_hbm(w_key), in_hbm(w_value))


def split_levels(levels, lane):
    first = levels.astype(BF16).astype(F32)
    rest = levels - first
    second = rest.astype(BF16).astype(F32)
    third = rest - second
    parts = jnp.where(lane < 4, first, jnp.where(lane < 8, second, third))
    return jnp.where(lane < 12, parts, 0.0).astype(BF16)


def attend_kernel(count, *refs):
    query_refs, (key_ref, value_ref) = refs[:count], refs[count : count + 2]
    out_refs = refs[count + 2 :]
    rows = query_refs[0].shape[0]
    total_rows = rows * count

    def scores_of(head):
        columns = slice(head * HEAD_DIM, (head + 1) * HEAD_DIM)
        parts = [ref[:, columns] for ref in query_refs]
        part = parts[0] if count == 1 else jnp.concatenate(parts, axis=0)
        return product(part, key_ref[head], NT)

    lane = lax.broadcasted_iota(jnp.int32, (total_rows, LANES), 1)
    levels = jnp.zeros((total_rows, LANES), F32)
    following = scores_of(0)
    even = None
    for head in range(HEADS_HERE):
        scores = following
        if head + 1 < HEADS_HERE:
            following = scores_of(head + 1)
        highest = jnp.max(scores, axis=1, keepdims=True)
        weights = jnp.exp(scores - highest).astype(BF16)
        accum = product(weights, value_ref[head])
        place = HEAD_DIM if head % 2 == 0 else 0
        total = accum[:, place : place + 1]
        mean = accum * (1.0 / total)
        levels = jnp.where(lane % 4 == head, highest + jnp.log(total), levels)
        if head % 2 == 0:
            even = mean
        else:
            both = jnp.where(lane < HEAD_DIM, even, mean).astype(BF16)
            for i, ref in enumerate(out_refs):
                columns = slice(head // 2 * LANES, (head // 2 + 1) * LANES)
                ref[:, columns] = both[i * rows : (i + 1) * rows]
    packed = split_levels(levels, lane)
    for i, ref in enumerate(out_refs):
        ref[:, 2 * LANES :] = packed[i * rows : (i + 1) * rows]


def attend(chunks, keys, values):
    count = len(chunks)
    rows = chunks[0].shape[0]
    return pl.pallas_call(
        functools.partial(attend_kernel, count),
        out_shape=[jax.ShapeDtypeStruct((rows, 3 * LANES), BF16)] * count,
        compiler_params=params(40),
        name="attend",
    )(*chunks, keys, values)


def spread_matrix():
    source = lax.broadcasted_iota(jnp.int32, (LANES, 2 * LANES), 0)
    target = lax.broadcasted_iota(jnp.int32, (LANES, 2 * LANES), 1)
    hit = (source < 12) & (source % 4 == target // HEAD_DIM)
    return jnp.where(hit, 1.0, 0.0).astype(BF16)


def merged(pieces):
    spread = spread_matrix()
    levels = [product(piece[:, 2 * LANES :], spread) for piece in pieces]
    highest = functools.reduce(jnp.maximum, levels)
    total, accum = None, None
    for piece, level in zip(pieces, levels):
        factor = jnp.exp(level - highest)
        term = factor * piece[:, : 2 * LANES].astype(F32)
        total = factor if total is None else total + factor
        accum = term if accum is None else accum + term
    return accum / total, highest, total


def merge_kernel(count, *refs):
    out_refs = refs[count:]
    mean, highest, total = merged([ref[...] for ref in refs[:count]])
    levels = highest + jnp.log(total)
    lane = lax.broadcasted_iota(jnp.int32, (levels.shape[0], LANES), 1)
    one, two = levels[:, :LANES], levels[:, LANES:]
    one_other, two_other = pltpu.roll(one, HEAD_DIM, 1), pltpu.roll(two, HEAD_DIM, 1)
    head = lane % 4
    picked = jnp.where(
        head == 0, one, jnp.where(head == 1, one_other, jnp.where(head == 2, two, two_other))
    )
    packed = split_levels(picked, lane)
    rows = out_refs[0].shape[0]
    for i, ref in enumerate(out_refs):
        span = slice(i * rows, (i + 1) * rows)
        ref[:, : 2 * LANES] = mean[span].astype(BF16)
        ref[:, 2 * LANES :] = packed[span]


def merge(pieces, parts):
    rows, width = pieces[0].shape
    return pl.pallas_call(
        functools.partial(merge_kernel, len(pieces)),
        out_shape=[jax.ShapeDtypeStruct((rows // parts, width), BF16)] * parts,
        compiler_params=params(24),
        name="merge",
    )(*pieces)


def finish_kernel(*refs):
    mean, highest, total = merged([ref[...] for ref in refs[:-1]])
    refs[-1][...] = mean.astype(BF16)


def finish(pieces):
    return pl.pallas_call(
        finish_kernel,
        out_shape=jax.ShapeDtypeStruct((pieces[0].shape[0], 2 * LANES), BF16),
        compiler_params=params(8),
        name="finish",
    )(*pieces)


def mlp_kernel(count, *refs):
    att_refs, w_out_refs = refs[:count], refs[count : 2 * count]
    latent_ref, w_up_hbm, w_down_hbm, resid_ref, share_ref, w_up_ref, w_down_ref, sems = refs[
        2 * count :
    ]
    copies = [
        pltpu.make_async_copy(w_up_hbm, w_up_ref, sems.at[0]),
        pltpu.make_async_copy(w_down_hbm, w_down_ref, sems.at[1]),
    ]
    for copy in copies:
        copy.start()
    columns = resid_ref.shape[2]
    projected = latent_ref[...].astype(F32)
    for att_ref, w_ref in zip(att_refs, w_out_refs):
        projected += product(att_ref[...], w_ref[...])
    residual = projected.astype(BF16)
    normed = norm_rows(residual.astype(F32)).astype(BF16)
    copies[0].wait()
    raised = product(normed, w_up_ref[...])
    hidden = (0.5 * raised * (1.0 + lax.erf(raised * 0.5**0.5))).astype(BF16)
    copies[1].wait()
    share = product(hidden, w_down_ref[...]).astype(BF16)
    for i in range(count):
        resid_ref[i] = residual[:, i * columns : (i + 1) * columns]
        share_ref[i] = share[:, i * columns : (i + 1) * columns]


def mlp(att, w_out, latent, w_up, w_down):
    rows, width = latent.shape
    count = len(att)
    out = jax.ShapeDtypeStruct((count, rows, width // count), BF16)
    vmem, hbm = pl.BlockSpec(memory_space=pltpu.VMEM), pl.BlockSpec(memory_space=pltpu.HBM)
    return pl.pallas_call(
        functools.partial(mlp_kernel, count),
        in_specs=[vmem] * (2 * count + 1) + [hbm] * 2,
        out_shape=[out, out],
        scratch_shapes=[
            pltpu.VMEM(w_up.shape, BF16),
            pltpu.VMEM(w_down.shape, BF16),
            pltpu.SemaphoreType.DMA((2,)),
        ],
        compiler_params=params(24),
        name="mlp",
    )(*att, *w_out, latent, in_hbm(w_up), in_hbm(w_down))


def close_kernel(place_ref, resid_ref, kept_ref, *refs):
    out_ref = refs[-1]
    place = place_ref[0]
    total = kept_ref[place].astype(F32)
    for ref in refs[:-1]:
        total += ref[...].astype(F32)
    out_ref[...] = (resid_ref[place].astype(F32) + total).astype(BF16)


def close(place, resid, kept, *others):
    return pl.pallas_call(
        close_kernel,
        in_specs=[pl.BlockSpec(memory_space=pltpu.SMEM)]
        + [pl.BlockSpec(memory_space=pltpu.VMEM)] * (2 + len(others)),
        out_shape=jax.ShapeDtypeStruct(resid.shape[1:], BF16),
        compiler_params=params(8),
        name="close",
    )(place, resid, kept, *others)


def along(value, axis, by):
    size = lax.axis_size(axis)
    return lax.ppermute(value, axis, [(i, (i + by) % size) for i in range(size)])


def swapped(value, axes, bits):
    size = lax.axis_size(axes)
    return lax.ppermute(value, axes, [(i, i ^ bits) for i in range(size)])


NEAR = ("zlo", "ylo")
STEPS = (1, 3, 2)


def on_device(inputs, latent, w_query, w_key, w_value, w_out, w_up, w_down):
    w_high = swapped(w_out, HEAD, 2)
    w_blocks = [w_out, swapped(w_out, HEAD, 1), w_high, swapped(w_high, HEAD, 1)]
    part = make_queries(latent, w_query)
    for axis in ("x", "zhi"):
        part = jnp.concatenate([part] + [along(part, axis, by) for by in STEPS], axis=0)
    keys, values = make_keys_values(inputs, w_key, w_value)
    masks = (1, 3, 2)
    arrived = [swapped(part, NEAR, bits) for bits in masks]
    pieces = []
    for bits, chunk in zip(masks, arrived):
        pieces.append(swapped(attend([chunk], keys, values)[0], NEAR, bits))
    pieces.append(attend([part], keys, values)[0])
    for axis in ("zhi", "x"):
        parts = merge(pieces, 1 + len(STEPS))
        pieces = [parts[0]] + [along(p, axis, -by) for p, by in zip(parts[1:], STEPS)]
    attended = finish(pieces)
    att = [attended] + [swapped(attended, HEAD, bits) for bits in (1, 2, 3)]
    resid, shares = mlp(att, w_blocks, latent, w_up, w_down)
    place = lax.axis_index(HEAD).astype(jnp.int32)
    moved = [
        swapped(lax.dynamic_index_in_dim(shares, place ^ bits, 0, keepdims=False), HEAD, bits)
        for bits in (1, 2, 3)
    ]
    return close(place.reshape(1), resid, shares, *moved)


def solution(mesh):
    fine = Mesh(mesh.devices.reshape(4, 4, 2, 2, 2, 2), SEQ + HEAD)
    placed = (
        P(SEQ, None),
        P(SEQ, None),
        P(None, HEAD),
        P(None, HEAD),
        P(None, HEAD),
        P(HEAD, None),
        P(None, HEAD),
        P(HEAD, None),
    )
    return jax.shard_map(
        on_device, mesh=fine, in_specs=placed, out_specs=P(SEQ, HEAD), check_vma=False
    )
```

```python
import functools

import jax
import jax.numpy as jnp
from jax import lax
from jax.experimental import pallas as pl
from jax.experimental.pallas import tpu as pltpu
from jax.sharding import Mesh
from jax.sharding import PartitionSpec as P

HEAD_DIM = 64
HEADS_HERE = 4
LEVEL_ROWS = 16
LANES = 128
SEQ = ("x", "zhi", "zlo", "ylo")
HEAD = ("yhi", "core")
BF16 = jnp.bfloat16
F32 = jnp.float32
NT = (((1,), (1,)), ((), ()))
NN = (((1,), (0,)), ((), ()))
TN = (((0,), (0,)), ((), ()))


def product(left, right, numbers=NN):
    return lax.dot_general(left, right, numbers, preferred_element_type=F32)


def params(mib):
    return pltpu.CompilerParams(vmem_limit_bytes=mib * 2**20)


def norm_rows(widened):
    width = widened.shape[-1]
    row_mean = jnp.sum(widened, axis=-1, keepdims=True) / width
    row_square = jnp.sum(widened * widened, axis=-1, keepdims=True) / width
    row_var = row_square - row_mean * row_mean
    return (widened - row_mean) * lax.rsqrt(row_var + 1e-05)


def in_hbm(value):
    return pltpu.with_memory_space_constraint(value, pltpu.HBM)


def query_kernel(latent_hbm, w_hbm, out_ref, latent_ref, w_ref, sems):
    copies = [
        pltpu.make_async_copy(latent_hbm, latent_ref, sems.at[0]),
        pltpu.make_async_copy(w_hbm, w_ref, sems.at[1]),
    ]
    for copy in copies:
        copy.start()
    copies[0].wait()
    normed = norm_rows(latent_ref[...].astype(F32)).astype(BF16)
    copies[1].wait()
    out_ref[...] = (product(normed, w_ref[...]) * HEAD_DIM ** (-0.5)).astype(BF16)


def make_queries(latent, w_query):
    return pl.pallas_call(
        query_kernel,
        in_specs=[pl.BlockSpec(memory_space=pltpu.HBM)] * 2,
        out_shape=jax.ShapeDtypeStruct((latent.shape[0], w_query.shape[1]), BF16),
        scratch_shapes=[
            pltpu.VMEM(latent.shape, BF16),
            pltpu.VMEM(w_query.shape, BF16),
            pltpu.SemaphoreType.DMA((2,)),
        ],
        compiler_params=params(8),
        name="make_queries",
    )(in_hbm(latent), in_hbm(w_query))


def key_value_kernel(
    block, x_hbm, w_key_hbm, w_value_hbm, key_ref, value_ref, x_ref, w_key_ref, w_value_ref, sems
):
    tokens = x_ref.shape[0]
    weights = [
        pltpu.make_async_copy(w_key_hbm, w_key_ref, sems.at[0]),
        pltpu.make_async_copy(w_value_hbm, w_value_ref, sems.at[1]),
    ]
    spans = [slice(start, start + block) for start in range(0, tokens, block)]
    copies = [
        pltpu.make_async_copy(x_hbm.at[span], x_ref.at[span], sems.at[2 + i])
        for i, span in enumerate(spans)
    ]
    for copy in copies[:1] + weights + copies[1:]:
        copy.start()
    lane = lax.broadcasted_iota(jnp.int32, (block, LANES), 1)
    low = lane < HEAD_DIM
    for i, span in enumerate(spans):
        copies[i].wait()
        normed = norm_rows(x_ref[span].astype(F32)).astype(BF16)
        if i == 0:
            weights[0].wait()
            weights[1].wait()
        keys = product(normed, w_key_ref[...]).astype(BF16)
        vals = product(normed, w_value_ref[...])
        for head in range(HEADS_HERE):
            key_ref[head, span] = keys[:, head * HEAD_DIM : (head + 1) * HEAD_DIM]
            pair = vals[:, head // 2 * LANES : (head // 2 + 1) * LANES]
            one = jnp.where(lane == (HEAD_DIM if head % 2 == 0 else 0), 1.0, 0.0)
            kept = jnp.where(low, pair, one) if head % 2 == 0 else jnp.where(low, one, pair)
            value_ref[head, span] = kept.astype(BF16)


def make_keys_values(x, w_key, w_value):
    tokens = x.shape[0]
    block = 512
    return pl.pallas_call(
        functools.partial(key_value_kernel, block),
        in_specs=[pl.BlockSpec(memory_space=pltpu.HBM)] * 3,
        out_shape=[
            jax.ShapeDtypeStruct((HEADS_HERE, tokens, HEAD_DIM), BF16),
            jax.ShapeDtypeStruct((HEADS_HERE, tokens, LANES), BF16),
        ],
        scratch_shapes=[
            pltpu.VMEM(x.shape, BF16),
            pltpu.VMEM(w_key.shape, BF16),
            pltpu.VMEM(w_value.shape, BF16),
            pltpu.SemaphoreType.DMA((2 + tokens // block,)),
        ],
        compiler_params=params(32),
        name="make_keys_values",
    )(in_hbm(x), in_hbm(w_key), in_hbm(w_value))


def split_levels(levels, lane):
    first = levels.astype(BF16).astype(F32)
    rest = levels - first
    second = rest.astype(BF16).astype(F32)
    third = rest - second
    parts = jnp.where(lane < 4, first, jnp.where(lane < 8, second, third))
    return jnp.where(lane < 12, parts, 0.0)


def level_rows(rows):
    return rows // (2 * LANES) * LEVEL_ROWS


def attend_kernel(count, *refs):
    query_refs, (key_ref, value_ref) = refs[:count], refs[count : count + 2]
    out_refs = refs[count + 2 :]
    rows = query_refs[0].shape[0]
    total_rows = rows * count

    def scores_of(head):
        columns = slice(head * HEAD_DIM, (head + 1) * HEAD_DIM)
        parts = [ref[:, columns] for ref in query_refs]
        part = parts[0] if count == 1 else jnp.concatenate(parts, axis=0)
        return product(part, key_ref[head], NT)

    lane = lax.broadcasted_iota(jnp.int32, (total_rows, LANES), 1)
    levels = jnp.zeros((total_rows, LANES), F32)
    following = scores_of(0)
    even = None
    for head in range(HEADS_HERE):
        scores = following
        if head + 1 < HEADS_HERE:
            following = scores_of(head + 1)
        highest = jnp.max(scores, axis=1, keepdims=True)
        weights = jnp.exp(scores - highest).astype(BF16)
        accum = product(weights, value_ref[head])
        place = HEAD_DIM if head % 2 == 0 else 0
        total = accum[:, place : place + 1]
        mean = accum * (1.0 / total)
        levels = jnp.where(lane % 4 == head, highest + jnp.log(total), levels)
        if head % 2 == 0:
            even = mean
        else:
            both = jnp.where(lane < HEAD_DIM, even, mean).astype(BF16)
            for i, ref in enumerate(out_refs):
                columns = slice(head // 2 * LANES, (head // 2 + 1) * LANES)
                ref[:rows, columns] = both[i * rows : (i + 1) * rows]
    packed = jnp.transpose(split_levels(levels, lane))[:LEVEL_ROWS].astype(BF16)
    for i, ref in enumerate(out_refs):
        for j in range(rows // (2 * LANES)):
            start = i * rows + j * 2 * LANES
            span = slice(rows + j * LEVEL_ROWS, rows + (j + 1) * LEVEL_ROWS)
            ref[span] = packed[:, start : start + 2 * LANES]


def attend(chunks, keys, values):
    count = len(chunks)
    rows = chunks[0].shape[0]
    return pl.pallas_call(
        functools.partial(attend_kernel, count),
        out_shape=[jax.ShapeDtypeStruct((rows + level_rows(rows), 2 * LANES), BF16)] * count,
        compiler_params=params(40),
        name="attend",
    )(*chunks, keys, values)


def spread_matrix(count):
    source = lax.broadcasted_iota(jnp.int32, (count, 2 * LANES), 0)
    target = lax.broadcasted_iota(jnp.int32, (count, 2 * LANES), 1)
    hit = (source < 12) & (source % 4 == target // HEAD_DIM)
    return jnp.where(hit, 1.0, 0.0).astype(BF16)


def side_levels(piece):
    return piece[:, : 2 * LANES], product(piece[:, 2 * LANES :], spread_matrix(LANES))


def under_levels(piece):
    rows = piece.shape[0] * 2 * LANES // (2 * LANES + LEVEL_ROWS)
    spread = spread_matrix(LEVEL_ROWS)
    levels = [
        product(piece[start : start + LEVEL_ROWS], spread, TN)
        for start in range(rows, piece.shape[0], LEVEL_ROWS)
    ]
    return piece[:rows], jnp.concatenate(levels, axis=0)


def merged(pieces, read):
    means, levels = zip(*[read(piece) for piece in pieces])
    highest = functools.reduce(jnp.maximum, levels)
    total, accum = None, None
    for mean, level in zip(means, levels):
        factor = jnp.exp(level - highest)
        term = factor * mean.astype(F32)
        total = factor if total is None else total + factor
        accum = term if accum is None else accum + term
    return accum / total, highest, total


def merge_kernel(count, read, *refs):
    out_refs = refs[count:]
    mean, highest, total = merged([ref[...] for ref in refs[:count]], read)
    levels = highest + jnp.log(total)
    lane = lax.broadcasted_iota(jnp.int32, (levels.shape[0], LANES), 1)
    one, two = levels[:, :LANES], levels[:, LANES:]
    one_other, two_other = pltpu.roll(one, HEAD_DIM, 1), pltpu.roll(two, HEAD_DIM, 1)
    head = lane % 4
    picked = jnp.where(
        head == 0, one, jnp.where(head == 1, one_other, jnp.where(head == 2, two, two_other))
    )
    packed = split_levels(picked, lane).astype(BF16)
    rows = out_refs[0].shape[0]
    for i, ref in enumerate(out_refs):
        span = slice(i * rows, (i + 1) * rows)
        ref[:, : 2 * LANES] = mean[span].astype(BF16)
        ref[:, 2 * LANES :] = packed[span]


def merge(pieces, read, rows, parts):
    return pl.pallas_call(
        functools.partial(merge_kernel, len(pieces), read),
        out_shape=[jax.ShapeDtypeStruct((rows // parts, 3 * LANES), BF16)] * parts,
        compiler_params=params(24),
        name="merge",
    )(*pieces)


def finish_kernel(*refs):
    mean, highest, total = merged([ref[...] for ref in refs[:-1]], side_levels)
    refs[-1][...] = mean.astype(BF16)


def finish(pieces):
    return pl.pallas_call(
        finish_kernel,
        out_shape=jax.ShapeDtypeStruct((pieces[0].shape[0], 2 * LANES), BF16),
        compiler_params=params(8),
        name="finish",
    )(*pieces)


def mlp_kernel(count, *refs):
    att_refs, w_out_refs = refs[:count], refs[count : 2 * count]
    latent_ref, w_up_hbm, w_down_hbm, resid_ref, share_ref, w_up_ref, w_down_ref, sems = refs[
        2 * count :
    ]
    copies = [
        pltpu.make_async_copy(w_up_hbm, w_up_ref, sems.at[0]),
        pltpu.make_async_copy(w_down_hbm, w_down_ref, sems.at[1]),
    ]
    for copy in copies:
        copy.start()
    columns = resid_ref.shape[2]
    projected = latent_ref[...].astype(F32)
    for att_ref, w_ref in zip(att_refs, w_out_refs):
        projected += product(att_ref[...], w_ref[...])
    residual = projected.astype(BF16)
    normed = norm_rows(residual.astype(F32)).astype(BF16)
    copies[0].wait()
    raised = product(normed, w_up_ref[...])
    hidden = (0.5 * raised * (1.0 + lax.erf(raised * 0.5**0.5))).astype(BF16)
    copies[1].wait()
    share = product(hidden, w_down_ref[...]).astype(BF16)
    for i in range(count):
        resid_ref[i] = residual[:, i * columns : (i + 1) * columns]
        share_ref[i] = share[:, i * columns : (i + 1) * columns]


def mlp(att, w_out, latent, w_up, w_down):
    rows, width = latent.shape
    count = len(att)
    out = jax.ShapeDtypeStruct((count, rows, width // count), BF16)
    vmem, hbm = pl.BlockSpec(memory_space=pltpu.VMEM), pl.BlockSpec(memory_space=pltpu.HBM)
    return pl.pallas_call(
        functools.partial(mlp_kernel, count),
        in_specs=[vmem] * (2 * count + 1) + [hbm] * 2,
        out_shape=[out, out],
        scratch_shapes=[
            pltpu.VMEM(w_up.shape, BF16),
            pltpu.VMEM(w_down.shape, BF16),
            pltpu.SemaphoreType.DMA((2,)),
        ],
        compiler_params=params(24),
        name="mlp",
    )(*att, *w_out, latent, in_hbm(w_up), in_hbm(w_down))


def close_kernel(place_ref, resid_ref, kept_ref, *refs):
    out_ref = refs[-1]
    place = place_ref[0]
    total = kept_ref[place].astype(F32)
    for ref in refs[:-1]:
        total += ref[...].astype(F32)
    out_ref[...] = (resid_ref[place].astype(F32) + total).astype(BF16)


def close(place, resid, kept, *others):
    return pl.pallas_call(
        close_kernel,
        in_specs=[pl.BlockSpec(memory_space=pltpu.SMEM)]
        + [pl.BlockSpec(memory_space=pltpu.VMEM)] * (2 + len(others)),
        out_shape=jax.ShapeDtypeStruct(resid.shape[1:], BF16),
        compiler_params=params(8),
        name="close",
    )(place, resid, kept, *others)


def along(value, axis, by):
    size = lax.axis_size(axis)
    return lax.ppermute(value, axis, [(i, (i + by) % size) for i in range(size)])


def swapped(value, axes, bits):
    size = lax.axis_size(axes)
    return lax.ppermute(value, axes, [(i, i ^ bits) for i in range(size)])


NEAR = ("zlo", "ylo")
STEPS = (1, 3, 2)
MASKS = (3, 1, 2)
OTHERS = (1, 2, 3)


def on_device(inputs, latent, w_query, w_key, w_value, w_out, w_up, w_down):
    w_high = swapped(w_out, HEAD, 2)
    part = make_queries(latent, w_query)
    for axis in ("x", "zhi"):
        part = jnp.concatenate([part] + [along(part, axis, by) for by in STEPS], axis=0)
    arrived = [swapped(part, NEAR, bits) for bits in MASKS]
    inputs, w_low, w_both, part = lax.optimization_barrier((inputs, w_out, w_high, part))
    w_low, w_both = swapped(w_low, HEAD, 1), swapped(w_both, HEAD, 1)
    keys, values = make_keys_values(inputs, w_key, w_value)
    pieces = []
    for i, bits in enumerate(MASKS):
        chunk = arrived[i]
        if i == 1:
            chunk, w_low, w_both = lax.optimization_barrier((chunk, w_low, w_both))
        pieces.append(swapped(attend([chunk], keys, values)[0], NEAR, bits))
    pieces.append(attend([part], keys, values)[0])
    rows, read = part.shape[0], under_levels
    for axis in ("zhi", "x"):
        parts = merge(pieces, read, rows, 1 + len(STEPS))
        sent = list(zip(parts[1:], STEPS))[::-1]
        pieces = [parts[0]] + [along(p, axis, -by) for p, by in sent]
        rows, read = parts[0].shape[0], side_levels
    attended = finish(pieces)
    att = [attended] + [swapped(attended, HEAD, bits) for bits in OTHERS]
    resid, shares = mlp(att, [w_out, w_low, w_high, w_both], latent, w_up, w_down)
    place = lax.axis_index(HEAD).astype(jnp.int32)
    moved = [
        swapped(lax.dynamic_index_in_dim(shares, place ^ bits, 0, keepdims=False), HEAD, bits)
        for bits in OTHERS
    ]
    return close(place.reshape(1), resid, shares, *moved)


def solution(mesh):
    fine = Mesh(mesh.devices.reshape(4, 4, 2, 2, 2, 2), SEQ + HEAD)
    placed = (
        P(SEQ, None),
        P(SEQ, None),
        P(None, HEAD),
        P(None, HEAD),
        P(None, HEAD),
        P(HEAD, None),
        P(None, HEAD),
        P(HEAD, None),
    )
    return jax.shard_map(
        on_device, mesh=fine, in_specs=placed, out_specs=P(SEQ, HEAD), check_vma=False
    )
```

```python
import functools

import jax
import jax.numpy as jnp
from jax import lax
from jax.experimental import pallas as pl
from jax.experimental.pallas import tpu as pltpu
from jax.sharding import Mesh
from jax.sharding import PartitionSpec as P

HEAD_DIM = 64
HEADS_HERE = 4
LEVEL_ROWS = 16
LANES = 128
SEQ = ("x", "zhi", "zlo", "ylo")
HEAD = ("yhi", "core")
BF16 = jnp.bfloat16
F32 = jnp.float32
NT = (((1,), (1,)), ((), ()))
NN = (((1,), (0,)), ((), ()))
TN = (((0,), (0,)), ((), ()))


def product(left, right, numbers=NN):
    return lax.dot_general(left, right, numbers, preferred_element_type=F32)


def params(mib):
    return pltpu.CompilerParams(vmem_limit_bytes=mib * 2**20)


def norm_rows(widened):
    width = widened.shape[-1]
    row_mean = jnp.sum(widened, axis=-1, keepdims=True) / width
    row_square = jnp.sum(widened * widened, axis=-1, keepdims=True) / width
    row_var = row_square - row_mean * row_mean
    return (widened - row_mean) * lax.rsqrt(row_var + 1e-05)


def in_hbm(value):
    return pltpu.with_memory_space_constraint(value, pltpu.HBM)


def query_kernel(latent_hbm, w_hbm, out_ref, latent_ref, w_ref, sems):
    copies = [
        pltpu.make_async_copy(latent_hbm, latent_ref, sems.at[0]),
        pltpu.make_async_copy(w_hbm, w_ref, sems.at[1]),
    ]
    for copy in copies:
        copy.start()
    copies[0].wait()
    normed = norm_rows(latent_ref[...].astype(F32)).astype(BF16)
    copies[1].wait()
    out_ref[...] = (product(normed, w_ref[...]) * HEAD_DIM ** (-0.5)).astype(BF16)


def make_queries(latent, w_query):
    return pl.pallas_call(
        query_kernel,
        in_specs=[pl.BlockSpec(memory_space=pltpu.HBM)] * 2,
        out_shape=jax.ShapeDtypeStruct((latent.shape[0], w_query.shape[1]), BF16),
        scratch_shapes=[
            pltpu.VMEM(latent.shape, BF16),
            pltpu.VMEM(w_query.shape, BF16),
            pltpu.SemaphoreType.DMA((2,)),
        ],
        compiler_params=params(8),
        name="make_queries",
    )(in_hbm(latent), in_hbm(w_query))


def key_value_kernel(
    block, x_hbm, w_key_hbm, w_value_hbm, key_ref, value_ref, x_ref, w_key_ref, w_value_ref, sems
):
    tokens = x_ref.shape[0]
    weights = [
        pltpu.make_async_copy(w_key_hbm, w_key_ref, sems.at[0]),
        pltpu.make_async_copy(w_value_hbm, w_value_ref, sems.at[1]),
    ]
    spans = [slice(start, start + block) for start in range(0, tokens, block)]
    copies = [
        pltpu.make_async_copy(x_hbm.at[span], x_ref.at[span], sems.at[2 + i])
        for i, span in enumerate(spans)
    ]
    for copy in copies[:1] + weights + copies[1:]:
        copy.start()
    lane = lax.broadcasted_iota(jnp.int32, (block, LANES), 1)
    low = lane < HEAD_DIM
    for i, span in enumerate(spans):
        copies[i].wait()
        normed = norm_rows(x_ref[span].astype(F32)).astype(BF16)
        if i == 0:
            weights[0].wait()
            weights[1].wait()
        keys = product(normed, w_key_ref[...]).astype(BF16)
        vals = product(normed, w_value_ref[...])
        for head in range(HEADS_HERE):
            key_ref[head, span] = keys[:, head * HEAD_DIM : (head + 1) * HEAD_DIM]
            pair = vals[:, head // 2 * LANES : (head // 2 + 1) * LANES]
            one = jnp.where(lane == (HEAD_DIM if head % 2 == 0 else 0), 1.0, 0.0)
            kept = jnp.where(low, pair, one) if head % 2 == 0 else jnp.where(low, one, pair)
            value_ref[head, span] = kept.astype(BF16)


def make_keys_values(x, w_key, w_value):
    tokens = x.shape[0]
    block = 512
    return pl.pallas_call(
        functools.partial(key_value_kernel, block),
        in_specs=[pl.BlockSpec(memory_space=pltpu.HBM)] * 3,
        out_shape=[
            jax.ShapeDtypeStruct((HEADS_HERE, tokens, HEAD_DIM), BF16),
            jax.ShapeDtypeStruct((HEADS_HERE, tokens, LANES), BF16),
        ],
        scratch_shapes=[
            pltpu.VMEM(x.shape, BF16),
            pltpu.VMEM(w_key.shape, BF16),
            pltpu.VMEM(w_value.shape, BF16),
            pltpu.SemaphoreType.DMA((2 + tokens // block,)),
        ],
        compiler_params=params(16),
        name="make_keys_values",
    )(in_hbm(x), in_hbm(w_key), in_hbm(w_value))


def split_levels(levels, lane):
    first = levels.astype(BF16).astype(F32)
    rest = levels - first
    second = rest.astype(BF16).astype(F32)
    third = rest - second
    parts = jnp.where(lane < 4, first, jnp.where(lane < 8, second, third))
    return jnp.where(lane < 12, parts, 0.0)


def level_rows(rows):
    return rows // (2 * LANES) * LEVEL_ROWS


def attend_kernel(count, *refs):
    query_refs, (key_ref, value_ref) = refs[:count], refs[count : count + 2]
    out_refs = refs[count + 2 :]
    rows = query_refs[0].shape[0]
    total_rows = rows * count

    def scores_of(head):
        columns = slice(head * HEAD_DIM, (head + 1) * HEAD_DIM)
        parts = [ref[:, columns] for ref in query_refs]
        part = parts[0] if count == 1 else jnp.concatenate(parts, axis=0)
        return product(part, key_ref[head], NT)

    lane = lax.broadcasted_iota(jnp.int32, (total_rows, LANES), 1)
    levels = jnp.zeros((total_rows, LANES), F32)
    following = scores_of(0)
    even = None
    for head in range(HEADS_HERE):
        scores = following
        if head + 1 < HEADS_HERE:
            following = scores_of(head + 1)
        highest = jnp.max(scores, axis=1, keepdims=True)
        weights = jnp.exp(scores - highest).astype(BF16)
        accum = product(weights, value_ref[head])
        place = HEAD_DIM if head % 2 == 0 else 0
        total = accum[:, place : place + 1]
        mean = accum * (1.0 / total)
        levels = jnp.where(lane % 4 == head, highest + jnp.log(total), levels)
        if head % 2 == 0:
            even = mean
        else:
            both = jnp.where(lane < HEAD_DIM, even, mean).astype(BF16)
            for i, ref in enumerate(out_refs):
                columns = slice(head // 2 * LANES, (head // 2 + 1) * LANES)
                ref[:rows, columns] = both[i * rows : (i + 1) * rows]
    packed = jnp.transpose(split_levels(levels, lane))[:LEVEL_ROWS].astype(BF16)
    for i, ref in enumerate(out_refs):
        for j in range(rows // (2 * LANES)):
            start = i * rows + j * 2 * LANES
            span = slice(rows + j * LEVEL_ROWS, rows + (j + 1) * LEVEL_ROWS)
            ref[span] = packed[:, start : start + 2 * LANES]


def attend(chunks, keys, values):
    count = len(chunks)
    rows = chunks[0].shape[0]
    return pl.pallas_call(
        functools.partial(attend_kernel, count),
        out_shape=[jax.ShapeDtypeStruct((rows + level_rows(rows), 2 * LANES), BF16)] * count,
        compiler_params=params(20),
        name="attend",
    )(*chunks, keys, values)


def spread_matrix(count):
    source = lax.broadcasted_iota(jnp.int32, (count, 2 * LANES), 0)
    target = lax.broadcasted_iota(jnp.int32, (count, 2 * LANES), 1)
    hit = (source < 12) & (source % 4 == target // HEAD_DIM)
    return jnp.where(hit, 1.0, 0.0).astype(BF16)


def side_levels(piece):
    return piece[:, : 2 * LANES], product(piece[:, 2 * LANES :], spread_matrix(LANES))


def under_levels(piece):
    rows = piece.shape[0] * 2 * LANES // (2 * LANES + LEVEL_ROWS)
    spread = spread_matrix(LEVEL_ROWS)
    levels = [
        product(piece[start : start + LEVEL_ROWS], spread, TN)
        for start in range(rows, piece.shape[0], LEVEL_ROWS)
    ]
    return piece[:rows], jnp.concatenate(levels, axis=0)


def merged(pieces, read):
    means, levels = zip(*[read(piece) for piece in pieces])
    highest = functools.reduce(jnp.maximum, levels)
    total, accum = None, None
    for mean, level in zip(means, levels):
        factor = jnp.exp(level - highest)
        term = factor * mean.astype(F32)
        total = factor if total is None else total + factor
        accum = term if accum is None else accum + term
    return accum / total, highest, total


def merge_kernel(count, read, *refs):
    out_refs = refs[count:]
    mean, highest, total = merged([ref[...] for ref in refs[:count]], read)
    levels = highest + jnp.log(total)
    lane = lax.broadcasted_iota(jnp.int32, (levels.shape[0], LANES), 1)
    one, two = levels[:, :LANES], levels[:, LANES:]
    one_other, two_other = pltpu.roll(one, HEAD_DIM, 1), pltpu.roll(two, HEAD_DIM, 1)
    head = lane % 4
    picked = jnp.where(
        head == 0, one, jnp.where(head == 1, one_other, jnp.where(head == 2, two, two_other))
    )
    packed = split_levels(picked, lane).astype(BF16)
    rows = out_refs[0].shape[0]
    for i, ref in enumerate(out_refs):
        span = slice(i * rows, (i + 1) * rows)
        ref[:, : 2 * LANES] = mean[span].astype(BF16)
        ref[:, 2 * LANES :] = packed[span]


def merge(pieces, read, rows, parts):
    return pl.pallas_call(
        functools.partial(merge_kernel, len(pieces), read),
        out_shape=[jax.ShapeDtypeStruct((rows // parts, 3 * LANES), BF16)] * parts,
        compiler_params=params(24),
        name="merge",
    )(*pieces)


def finish_kernel(*refs):
    mean, highest, total = merged([ref[...] for ref in refs[:-1]], side_levels)
    refs[-1][...] = mean.astype(BF16)


def finish(pieces):
    return pl.pallas_call(
        finish_kernel,
        out_shape=jax.ShapeDtypeStruct((pieces[0].shape[0], 2 * LANES), BF16),
        compiler_params=params(8),
        name="finish",
    )(*pieces)


def mlp_kernel(count, *refs):
    att_refs, w_out_refs = refs[:count], refs[count : 2 * count]
    latent_ref, w_up_hbm, w_down_hbm, resid_ref, share_ref, w_up_ref, w_down_ref, sems = refs[
        2 * count :
    ]
    copies = [
        pltpu.make_async_copy(w_up_hbm, w_up_ref, sems.at[0]),
        pltpu.make_async_copy(w_down_hbm, w_down_ref, sems.at[1]),
    ]
    for copy in copies:
        copy.start()
    columns = resid_ref.shape[2]
    projected = latent_ref[...].astype(F32)
    for att_ref, w_ref in zip(att_refs, w_out_refs):
        projected += product(att_ref[...], w_ref[...])
    residual = projected.astype(BF16)
    normed = norm_rows(residual.astype(F32)).astype(BF16)
    copies[0].wait()
    raised = product(normed, w_up_ref[...])
    hidden = (0.5 * raised * (1.0 + lax.erf(raised * 0.5**0.5))).astype(BF16)
    copies[1].wait()
    share = product(hidden, w_down_ref[...]).astype(BF16)
    for i in range(count):
        resid_ref[i] = residual[:, i * columns : (i + 1) * columns]
        share_ref[i] = share[:, i * columns : (i + 1) * columns]


def mlp(att, w_out, latent, w_up, w_down):
    rows, width = latent.shape
    count = len(att)
    out = jax.ShapeDtypeStruct((count, rows, width // count), BF16)
    vmem, hbm = pl.BlockSpec(memory_space=pltpu.VMEM), pl.BlockSpec(memory_space=pltpu.HBM)
    return pl.pallas_call(
        functools.partial(mlp_kernel, count),
        in_specs=[vmem] * (2 * count + 1) + [hbm] * 2,
        out_shape=[out, out],
        scratch_shapes=[
            pltpu.VMEM(w_up.shape, BF16),
            pltpu.VMEM(w_down.shape, BF16),
            pltpu.SemaphoreType.DMA((2,)),
        ],
        compiler_params=params(24),
        name="mlp",
    )(*att, *w_out, latent, in_hbm(w_up), in_hbm(w_down))


def close_kernel(place_ref, resid_ref, kept_ref, *refs):
    out_ref = refs[-1]
    place = place_ref[0]
    total = kept_ref[place].astype(F32)
    for ref in refs[:-1]:
        total += ref[...].astype(F32)
    out_ref[...] = (resid_ref[place].astype(F32) + total).astype(BF16)


def close(place, resid, kept, *others):
    return pl.pallas_call(
        close_kernel,
        in_specs=[pl.BlockSpec(memory_space=pltpu.SMEM)]
        + [pl.BlockSpec(memory_space=pltpu.VMEM)] * (2 + len(others)),
        out_shape=jax.ShapeDtypeStruct(resid.shape[1:], BF16),
        compiler_params=params(8),
        name="close",
    )(place, resid, kept, *others)


def along(value, axis, by):
    size = lax.axis_size(axis)
    return lax.ppermute(value, axis, [(i, (i + by) % size) for i in range(size)])


def swapped(value, axes, bits):
    size = lax.axis_size(axes)
    return lax.ppermute(value, axes, [(i, i ^ bits) for i in range(size)])


NEAR = ("zlo", "ylo")
STEPS = (1, 3, 2)
MASKS = (3, 1, 2)
OTHERS = (1, 2, 3)


def on_device(inputs, latent, w_query, w_key, w_value, w_out, w_up, w_down):
    w_high = swapped(w_out, HEAD, 2)
    part = make_queries(latent, w_query)
    for axis in ("zhi", "x"):
        part = jnp.concatenate([part] + [along(part, axis, by) for by in STEPS], axis=0)
    arrived = [swapped(part, NEAR, bits) for bits in MASKS]
    inputs, w_low, w_both, part = lax.optimization_barrier((inputs, w_out, w_high, part))
    w_low, w_both = swapped(w_low, HEAD, 1), swapped(w_both, HEAD, 1)
    keys, values = make_keys_values(inputs, w_key, w_value)
    pieces = []
    for i, bits in enumerate(MASKS):
        chunk = arrived[i]
        if i == 1:
            chunk, w_low, w_both = lax.optimization_barrier((chunk, w_low, w_both))
        pieces.append(swapped(attend([chunk], keys, values)[0], NEAR, bits))
    pieces.append(attend([part], keys, values)[0])
    rows, read = part.shape[0], under_levels
    for axis in ("x", "zhi"):
        parts = merge(pieces, read, rows, 1 + len(STEPS))
        sent = list(zip(parts[1:], STEPS))[::-1]
        pieces = [parts[0]] + [along(p, axis, -by) for p, by in sent]
        rows, read = parts[0].shape[0], side_levels
    attended = finish(pieces)
    att = [attended] + [swapped(attended, HEAD, bits) for bits in OTHERS]
    resid, shares = mlp(att, [w_out, w_low, w_high, w_both], latent, w_up, w_down)
    place = lax.axis_index(HEAD).astype(jnp.int32)
    moved = [
        swapped(lax.dynamic_index_in_dim(shares, place ^ bits, 0, keepdims=False), HEAD, bits)
        for bits in OTHERS
    ]
    return close(place.reshape(1), resid, shares, *moved)


def solution(mesh):
    fine = Mesh(mesh.devices.reshape(4, 4, 2, 2, 2, 2), SEQ + HEAD)
    placed = (
        P(SEQ, None),
        P(SEQ, None),
        P(None, HEAD),
        P(None, HEAD),
        P(None, HEAD),
        P(HEAD, None),
        P(None, HEAD),
        P(HEAD, None),
    )
    return jax.shard_map(
        on_device, mesh=fine, in_specs=placed, out_specs=P(SEQ, HEAD), check_vma=False
    )
```

```python
import functools

import jax
import jax.numpy as jnp
from jax import lax
from jax.experimental import pallas as pl
from jax.experimental.pallas import tpu as pltpu
from jax.sharding import Mesh
from jax.sharding import PartitionSpec as P

HEAD_DIM = 64
HEADS_HERE = 4
LEVEL_ROWS = 16
LANES = 128
SEQ = ("x", "zhi", "zlo", "ylo")
HEAD = ("yhi", "core")
BF16 = jnp.bfloat16
F32 = jnp.float32
NT = (((1,), (1,)), ((), ()))
NN = (((1,), (0,)), ((), ()))
TN = (((0,), (0,)), ((), ()))


def product(left, right, numbers=NN):
    return lax.dot_general(left, right, numbers, preferred_element_type=F32)


def params(mib):
    return pltpu.CompilerParams(vmem_limit_bytes=mib * 2**20)


def norm_rows(widened):
    width = widened.shape[-1]
    row_mean = jnp.sum(widened, axis=-1, keepdims=True) / width
    row_square = jnp.sum(widened * widened, axis=-1, keepdims=True) / width
    row_var = row_square - row_mean * row_mean
    return (widened - row_mean) * lax.rsqrt(row_var + 1e-05)


def in_hbm(value):
    return pltpu.with_memory_space_constraint(value, pltpu.HBM)


def query_kernel(latent_hbm, w_hbm, out_ref, latent_ref, w_ref, sems):
    copies = [
        pltpu.make_async_copy(latent_hbm, latent_ref, sems.at[0]),
        pltpu.make_async_copy(w_hbm, w_ref, sems.at[1]),
    ]
    for copy in copies:
        copy.start()
    copies[0].wait()
    normed = norm_rows(latent_ref[...].astype(F32)).astype(BF16)
    copies[1].wait()
    out_ref[...] = (product(normed, w_ref[...]) * HEAD_DIM ** (-0.5)).astype(BF16)


def make_queries(latent, w_query):
    return pl.pallas_call(
        query_kernel,
        in_specs=[pl.BlockSpec(memory_space=pltpu.HBM)] * 2,
        out_shape=jax.ShapeDtypeStruct((latent.shape[0], w_query.shape[1]), BF16),
        scratch_shapes=[
            pltpu.VMEM(latent.shape, BF16),
            pltpu.VMEM(w_query.shape, BF16),
            pltpu.SemaphoreType.DMA((2,)),
        ],
        compiler_params=params(8),
        name="make_queries",
    )(in_hbm(latent), in_hbm(w_query))


def key_value_kernel(
    block, x_hbm, w_key_hbm, w_value_hbm, key_ref, value_ref, x_ref, w_key_ref, w_value_ref, sems
):
    tokens = x_ref.shape[0]
    weights = [
        pltpu.make_async_copy(w_key_hbm, w_key_ref, sems.at[0]),
        pltpu.make_async_copy(w_value_hbm, w_value_ref, sems.at[1]),
    ]
    spans = [slice(start, start + block) for start in range(0, tokens, block)]
    copies = [
        pltpu.make_async_copy(x_hbm.at[span], x_ref.at[span], sems.at[2 + i])
        for i, span in enumerate(spans)
    ]
    for copy in copies[:1] + weights + copies[1:]:
        copy.start()
    lane = lax.broadcasted_iota(jnp.int32, (block, LANES), 1)
    low = lane < HEAD_DIM
    for i, span in enumerate(spans):
        copies[i].wait()
        normed = norm_rows(x_ref[span].astype(F32)).astype(BF16)
        if i == 0:
            weights[0].wait()
            weights[1].wait()
        keys = product(normed, w_key_ref[...]).astype(BF16)
        vals = product(normed, w_value_ref[...])
        for head in range(HEADS_HERE):
            key_ref[head, span] = keys[:, head * HEAD_DIM : (head + 1) * HEAD_DIM]
            pair = vals[:, head // 2 * LANES : (head // 2 + 1) * LANES]
            one = jnp.where(lane == (HEAD_DIM if head % 2 == 0 else 0), 1.0, 0.0)
            kept = jnp.where(low, pair, one) if head % 2 == 0 else jnp.where(low, one, pair)
            value_ref[head, span] = kept.astype(BF16)


def make_keys_values(x, w_key, w_value):
    tokens = x.shape[0]
    block = 512
    return pl.pallas_call(
        functools.partial(key_value_kernel, block),
        in_specs=[pl.BlockSpec(memory_space=pltpu.HBM)] * 3,
        out_shape=[
            jax.ShapeDtypeStruct((HEADS_HERE, tokens, HEAD_DIM), BF16),
            jax.ShapeDtypeStruct((HEADS_HERE, tokens, LANES), BF16),
        ],
        scratch_shapes=[
            pltpu.VMEM(x.shape, BF16),
            pltpu.VMEM(w_key.shape, BF16),
            pltpu.VMEM(w_value.shape, BF16),
            pltpu.SemaphoreType.DMA((2 + tokens // block,)),
        ],
        compiler_params=params(16),
        name="make_keys_values",
    )(in_hbm(x), in_hbm(w_key), in_hbm(w_value))


def split_levels(levels, lane):
    first = levels.astype(BF16).astype(F32)
    rest = levels - first
    second = rest.astype(BF16).astype(F32)
    third = rest - second
    parts = jnp.where(lane < 4, first, jnp.where(lane < 8, second, third))
    return jnp.where(lane < 12, parts, 0.0)


def level_rows(rows):
    return rows // (2 * LANES) * LEVEL_ROWS


def attend_kernel(count, *refs):
    query_refs, (key_ref, value_ref) = refs[:count], refs[count : count + 2]
    out_refs = refs[count + 2 :]
    rows = query_refs[0].shape[0]
    total_rows = rows * count

    def scores_of(head):
        columns = slice(head * HEAD_DIM, (head + 1) * HEAD_DIM)
        parts = [ref[:, columns] for ref in query_refs]
        part = parts[0] if count == 1 else jnp.concatenate(parts, axis=0)
        return product(part, key_ref[head], NT)

    lane = lax.broadcasted_iota(jnp.int32, (total_rows, LANES), 1)
    levels = jnp.zeros((total_rows, LANES), F32)
    following = scores_of(0)
    even = None
    for head in range(HEADS_HERE):
        scores = following
        if head + 1 < HEADS_HERE:
            following = scores_of(head + 1)
        highest = jnp.max(scores, axis=1, keepdims=True)
        weights = jnp.exp(scores - highest).astype(BF16)
        accum = product(weights, value_ref[head])
        place = HEAD_DIM if head % 2 == 0 else 0
        total = accum[:, place : place + 1]
        mean = accum * (1.0 / total)
        levels = jnp.where(lane % 4 == head, highest + jnp.log(total), levels)
        if head % 2 == 0:
            even = mean
        else:
            both = jnp.where(lane < HEAD_DIM, even, mean).astype(BF16)
            for i, ref in enumerate(out_refs):
                columns = slice(head // 2 * LANES, (head // 2 + 1) * LANES)
                ref[:rows, columns] = both[i * rows : (i + 1) * rows]
    packed = jnp.transpose(split_levels(levels, lane))[:LEVEL_ROWS].astype(BF16)
    for i, ref in enumerate(out_refs):
        for j in range(rows // (2 * LANES)):
            start = i * rows + j * 2 * LANES
            span = slice(rows + j * LEVEL_ROWS, rows + (j + 1) * LEVEL_ROWS)
            ref[span] = packed[:, start : start + 2 * LANES]


def attend(chunks, keys, values):
    count = len(chunks)
    rows = chunks[0].shape[0]
    return pl.pallas_call(
        functools.partial(attend_kernel, count),
        out_shape=[jax.ShapeDtypeStruct((rows + level_rows(rows), 2 * LANES), BF16)] * count,
        compiler_params=params(20),
        name="attend",
    )(*chunks, keys, values)


def spread_matrix(count):
    source = lax.broadcasted_iota(jnp.int32, (count, 2 * LANES), 0)
    target = lax.broadcasted_iota(jnp.int32, (count, 2 * LANES), 1)
    hit = (source < 12) & (source % 4 == target // HEAD_DIM)
    return jnp.where(hit, 1.0, 0.0).astype(BF16)


def side_levels(piece):
    return piece[:, : 2 * LANES], product(piece[:, 2 * LANES :], spread_matrix(LANES))


def under_levels(piece):
    rows = piece.shape[0] * 2 * LANES // (2 * LANES + LEVEL_ROWS)
    spread = spread_matrix(LEVEL_ROWS)
    levels = [
        product(piece[start : start + LEVEL_ROWS], spread, TN)
        for start in range(rows, piece.shape[0], LEVEL_ROWS)
    ]
    return piece[:rows], jnp.concatenate(levels, axis=0)


def merged(pieces, read):
    means, levels = zip(*[read(piece) for piece in pieces])
    highest = functools.reduce(jnp.maximum, levels)
    total, accum = None, None
    for mean, level in zip(means, levels):
        factor = jnp.exp(level - highest)
        term = factor * mean.astype(F32)
        total = factor if total is None else total + factor
        accum = term if accum is None else accum + term
    return accum / total, highest, total


def merge_kernel(count, read, *refs):
    out_refs = refs[count:]
    mean, highest, total = merged([ref[...] for ref in refs[:count]], read)
    levels = highest + jnp.log(total)
    lane = lax.broadcasted_iota(jnp.int32, (levels.shape[0], LANES), 1)
    one, two = levels[:, :LANES], levels[:, LANES:]
    one_other, two_other = pltpu.roll(one, HEAD_DIM, 1), pltpu.roll(two, HEAD_DIM, 1)
    head = lane % 4
    picked = jnp.where(
        head == 0, one, jnp.where(head == 1, one_other, jnp.where(head == 2, two, two_other))
    )
    packed = split_levels(picked, lane).astype(BF16)
    rows = out_refs[0].shape[0]
    for i, ref in enumerate(out_refs):
        span = slice(i * rows, (i + 1) * rows)
        ref[:, : 2 * LANES] = mean[span].astype(BF16)
        ref[:, 2 * LANES :] = packed[span]


def merge(pieces, read, rows, parts):
    return pl.pallas_call(
        functools.partial(merge_kernel, len(pieces), read),
        out_shape=[jax.ShapeDtypeStruct((rows // parts, 3 * LANES), BF16)] * parts,
        compiler_params=params(24),
        name="merge",
    )(*pieces)


def project_kernel(count, *refs):
    w_ref, out_ref = refs[count:]
    mean, highest, total = merged([ref[...] for ref in refs[:count]], side_levels)
    projected = product(mean.astype(BF16), w_ref[...])
    columns = out_ref.shape[2]
    for i in range(out_ref.shape[0]):
        out_ref[i] = projected[:, i * columns : (i + 1) * columns]


def project(pieces, w_out):
    rows, width = pieces[0].shape[0], w_out.shape[1]
    return pl.pallas_call(
        functools.partial(project_kernel, len(pieces)),
        out_shape=jax.ShapeDtypeStruct((2, rows, width // 2), F32),
        compiler_params=params(8),
        name="project",
    )(*pieces, w_out)


def placed_call(kernel, name, out_shape, place, *operands):
    return pl.pallas_call(
        kernel,
        in_specs=[pl.BlockSpec(memory_space=pltpu.SMEM)]
        + [pl.BlockSpec(memory_space=pltpu.VMEM)] * len(operands),
        out_shape=out_shape,
        compiler_params=params(8),
        name=name,
    )(place, *operands)


def add_kernel(core_ref, halves_ref, other_ref, out_ref):
    out_ref[...] = halves_ref[core_ref[0]] + other_ref[...]


def residual_kernel(core_ref, one_ref, two_ref, latent_ref, out_ref):
    columns = out_ref.shape[1]
    own = latent_ref[:, pl.ds(pl.multiple_of(core_ref[0] * columns, LANES), columns)]
    out_ref[...] = (own.astype(F32) + (one_ref[...] + two_ref[...])).astype(BF16)


def mlp_kernel(core_ref, own_ref, other_ref, w_up_hbm, w_down_hbm, *refs):
    resid_ref, share_ref, w_up_ref, w_down_ref, sems = refs
    copies = [
        pltpu.make_async_copy(w_up_hbm, w_up_ref, sems.at[0]),
        pltpu.make_async_copy(w_down_hbm, w_down_ref, sems.at[1]),
    ]
    for copy in copies:
        copy.start()
    columns = resid_ref.shape[2]
    own, other = own_ref[...], other_ref[...]
    low = core_ref[0] == 0
    residual = jnp.concatenate([jnp.where(low, own, other), jnp.where(low, other, own)], axis=1)
    normed = norm_rows(residual.astype(F32)).astype(BF16)
    copies[0].wait()
    raised = product(normed, w_up_ref[...])
    hidden = (0.5 * raised * (1.0 + lax.erf(raised * 0.5**0.5))).astype(BF16)
    copies[1].wait()
    share = product(hidden, w_down_ref[...]).astype(BF16)
    for high in range(2):
        for core in range(2):
            i = high * 2 + core
            resid_ref[i] = residual[:, i * columns : (i + 1) * columns]
            share_ref[core, high] = share[:, i * columns : (i + 1) * columns]


def mlp(core, own, other, w_up, w_down):
    rows, half = own.shape
    vmem, hbm = pl.BlockSpec(memory_space=pltpu.VMEM), pl.BlockSpec(memory_space=pltpu.HBM)
    return pl.pallas_call(
        mlp_kernel,
        in_specs=[pl.BlockSpec(memory_space=pltpu.SMEM), vmem, vmem, hbm, hbm],
        out_shape=[
            jax.ShapeDtypeStruct((4, rows, half // 2), BF16),
            jax.ShapeDtypeStruct((2, 2, rows, half // 2), BF16),
        ],
        scratch_shapes=[
            pltpu.VMEM(w_up.shape, BF16),
            pltpu.VMEM(w_down.shape, BF16),
            pltpu.SemaphoreType.DMA((2,)),
        ],
        compiler_params=params(16),
        name="mlp",
    )(core, own, other, in_hbm(w_up), in_hbm(w_down))


def pair_kernel(place_ref, shares_ref, other_ref, kept_ref, sent_ref):
    high, core = place_ref[0], place_ref[1]
    for ref, index in ((kept_ref, high), (sent_ref, 1 - high)):
        ref[...] = shares_ref[core, index].astype(F32) + other_ref[index].astype(F32)


def close_kernel(place_ref, resid_ref, kept_ref, other_ref, out_ref):
    own = resid_ref[place_ref[0] * 2 + place_ref[1]]
    out_ref[...] = (own.astype(F32) + (kept_ref[...] + other_ref[...])).astype(BF16)


def along(value, axis, by):
    size = lax.axis_size(axis)
    return lax.ppermute(value, axis, [(i, (i + by) % size) for i in range(size)])


def swapped(value, axes, bits):
    size = lax.axis_size(axes)
    return lax.ppermute(value, axes, [(i, i ^ bits) for i in range(size)])


NEAR = ("zlo", "ylo")
STEPS = (1, 3, 2)
MASKS = (3, 1, 2)


def on_device(inputs, latent, w_query, w_key, w_value, w_out, w_up, w_down):
    part = make_queries(latent, w_query)
    for axis in ("zhi", "x"):
        part = jnp.concatenate([part] + [along(part, axis, by) for by in STEPS], axis=0)
    arrived = [swapped(part, NEAR, bits) for bits in MASKS]
    inputs, part = lax.optimization_barrier((inputs, part))
    keys, values = make_keys_values(inputs, w_key, w_value)
    pieces = []
    for bits, chunk in zip(MASKS, arrived):
        pieces.append(swapped(attend([chunk], keys, values)[0], NEAR, bits))
    pieces.append(attend([part], keys, values)[0])
    rows, read = part.shape[0], under_levels
    for axis in ("x", "zhi"):
        parts = merge(pieces, read, rows, 1 + len(STEPS))
        sent = list(zip(parts[1:], STEPS))[::-1]
        pieces = [parts[0]] + [along(p, axis, -by) for p, by in sent]
        rows, read = parts[0].shape[0], side_levels
    high, core = lax.axis_index("yhi"), lax.axis_index("core")
    place = jnp.stack([high, core]).astype(jnp.int32)
    core_place = place[1:]
    rows, width = latent.shape
    half = jax.ShapeDtypeStruct((rows, width // 2), F32)
    quarter = jax.ShapeDtypeStruct((rows, width // 4), F32)
    halves = project(pieces, w_out)
    other = swapped(lax.dynamic_index_in_dim(halves, 1 - core, 0, keepdims=False), HEAD, 1)
    pair = placed_call(add_kernel, "pair_sum", half, core_place, halves, other)
    across = swapped(pair, HEAD, 2)
    resid_half = placed_call(
        residual_kernel,
        "residual",
        jax.ShapeDtypeStruct(half.shape, BF16),
        core_place,
        pair,
        across,
        latent,
    )
    resid, shares = mlp(core_place, resid_half, swapped(resid_half, HEAD, 1), w_up, w_down)
    other = swapped(lax.dynamic_index_in_dim(shares, 1 - core, 0, keepdims=False), HEAD, 1)
    kept, sent = placed_call(pair_kernel, "pair_shares", [quarter] * 2, place, shares, other)
    return placed_call(
        close_kernel,
        "close",
        jax.ShapeDtypeStruct(quarter.shape, BF16),
        place,
        resid,
        kept,
        swapped(sent, HEAD, 2),
    )


def solution(mesh):
    fine = Mesh(mesh.devices.reshape(4, 4, 2, 2, 2, 2), SEQ + HEAD)
    placed = (
        P(SEQ, None),
        P(SEQ, None),
        P(None, HEAD),
        P(None, HEAD),
        P(None, HEAD),
        P(HEAD, None),
        P(None, HEAD),
        P(HEAD, None),
    )
    return jax.shard_map(
        on_device, mesh=fine, in_specs=placed, out_specs=P(SEQ, HEAD), check_vma=False
    )
```

```python
import functools

import jax
import jax.numpy as jnp
from jax import lax
from jax.experimental import pallas as pl
from jax.experimental.pallas import tpu as pltpu
from jax.sharding import Mesh
from jax.sharding import PartitionSpec as P

HEAD_DIM = 64
HEADS_HERE = 4
LEVEL_ROWS = 16
LANES = 128
SEQ = ("x", "z", "ylo")
HEAD = ("yhi", "core")
BF16 = jnp.bfloat16
F32 = jnp.float32
NT = (((1,), (1,)), ((), ()))
NN = (((1,), (0,)), ((), ()))
TN = (((0,), (0,)), ((), ()))


def product(left, right, numbers=NN):
    return lax.dot_general(left, right, numbers, preferred_element_type=F32)


def params(mib):
    return pltpu.CompilerParams(vmem_limit_bytes=mib * 2**20)


def norm_rows(widened):
    width = widened.shape[-1]
    row_mean = jnp.sum(widened, axis=-1, keepdims=True) / width
    row_square = jnp.sum(widened * widened, axis=-1, keepdims=True) / width
    row_var = row_square - row_mean * row_mean
    return (widened - row_mean) * lax.rsqrt(row_var + 1e-05)


def in_hbm(value):
    return pltpu.with_memory_space_constraint(value, pltpu.HBM)


def query_kernel(latent_hbm, w_hbm, out_ref, latent_ref, w_ref, sems):
    copies = [
        pltpu.make_async_copy(latent_hbm, latent_ref, sems.at[0]),
        pltpu.make_async_copy(w_hbm, w_ref, sems.at[1]),
    ]
    for copy in copies:
        copy.start()
    copies[0].wait()
    normed = norm_rows(latent_ref[...].astype(F32)).astype(BF16)
    copies[1].wait()
    out_ref[...] = (product(normed, w_ref[...]) * HEAD_DIM ** (-0.5)).astype(BF16)


def make_queries(latent, w_query):
    return pl.pallas_call(
        query_kernel,
        in_specs=[pl.BlockSpec(memory_space=pltpu.HBM)] * 2,
        out_shape=jax.ShapeDtypeStruct((latent.shape[0], w_query.shape[1]), BF16),
        scratch_shapes=[
            pltpu.VMEM(latent.shape, BF16),
            pltpu.VMEM(w_query.shape, BF16),
            pltpu.SemaphoreType.DMA((2,)),
        ],
        compiler_params=params(8),
        name="make_queries",
    )(in_hbm(latent), in_hbm(w_query))


def key_value_kernel(
    block, x_hbm, w_key_hbm, w_value_hbm, key_ref, value_ref, x_ref, w_key_ref, w_value_ref, sems
):
    tokens = x_ref.shape[0]
    weights = [
        pltpu.make_async_copy(w_key_hbm, w_key_ref, sems.at[0]),
        pltpu.make_async_copy(w_value_hbm, w_value_ref, sems.at[1]),
    ]
    spans = [slice(start, start + block) for start in range(0, tokens, block)]
    copies = [
        pltpu.make_async_copy(x_hbm.at[span], x_ref.at[span], sems.at[2 + i])
        for i, span in enumerate(spans)
    ]
    for copy in copies[:1] + weights + copies[1:]:
        copy.start()
    lane = lax.broadcasted_iota(jnp.int32, (block, LANES), 1)
    low = lane < HEAD_DIM
    for i, span in enumerate(spans):
        copies[i].wait()
        normed = norm_rows(x_ref[span].astype(F32)).astype(BF16)
        if i == 0:
            weights[0].wait()
            weights[1].wait()
        keys = product(normed, w_key_ref[...]).astype(BF16)
        vals = product(normed, w_value_ref[...])
        for head in range(HEADS_HERE):
            key_ref[head, span] = keys[:, head * HEAD_DIM : (head + 1) * HEAD_DIM]
            pair = vals[:, head // 2 * LANES : (head // 2 + 1) * LANES]
            one = jnp.where(lane == (HEAD_DIM if head % 2 == 0 else 0), 1.0, 0.0)
            kept = jnp.where(low, pair, one) if head % 2 == 0 else jnp.where(low, one, pair)
            value_ref[head, span] = kept.astype(BF16)


def make_keys_values(x, w_key, w_value):
    tokens = x.shape[0]
    block = 512
    return pl.pallas_call(
        functools.partial(key_value_kernel, block),
        in_specs=[pl.BlockSpec(memory_space=pltpu.HBM)] * 3,
        out_shape=[
            jax.ShapeDtypeStruct((HEADS_HERE, tokens, HEAD_DIM), BF16),
            jax.ShapeDtypeStruct((HEADS_HERE, tokens, LANES), BF16),
        ],
        scratch_shapes=[
            pltpu.VMEM(x.shape, BF16),
            pltpu.VMEM(w_key.shape, BF16),
            pltpu.VMEM(w_value.shape, BF16),
            pltpu.SemaphoreType.DMA((2 + tokens // block,)),
        ],
        compiler_params=params(16),
        name="make_keys_values",
    )(in_hbm(x), in_hbm(w_key), in_hbm(w_value))


def split_levels(levels, lane):
    first = levels.astype(BF16).astype(F32)
    rest = levels - first
    second = rest.astype(BF16).astype(F32)
    third = rest - second
    parts = jnp.where(lane < 4, first, jnp.where(lane < 8, second, third))
    return jnp.where(lane < 12, parts, 0.0)


def level_rows(rows):
    return rows // (2 * LANES) * LEVEL_ROWS


def attend_kernel(count, *refs):
    query_refs, (key_ref, value_ref) = refs[:count], refs[count : count + 2]
    out_refs = refs[count + 2 :]
    rows = query_refs[0].shape[0]
    total_rows = rows * count

    def scores_of(head):
        columns = slice(head * HEAD_DIM, (head + 1) * HEAD_DIM)
        parts = [ref[:, columns] for ref in query_refs]
        part = parts[0] if count == 1 else jnp.concatenate(parts, axis=0)
        return product(part, key_ref[head], NT)

    lane = lax.broadcasted_iota(jnp.int32, (total_rows, LANES), 1)
    levels = jnp.zeros((total_rows, LANES), F32)
    following = scores_of(0)
    even = None
    for head in range(HEADS_HERE):
        scores = following
        if head + 1 < HEADS_HERE:
            following = scores_of(head + 1)
        highest = jnp.max(scores, axis=1, keepdims=True)
        weights = jnp.exp(scores - highest).astype(BF16)
        accum = product(weights, value_ref[head])
        place = HEAD_DIM if head % 2 == 0 else 0
        total = accum[:, place : place + 1]
        mean = accum * (1.0 / total)
        levels = jnp.where(lane % 4 == head, highest + jnp.log(total), levels)
        if head % 2 == 0:
            even = mean
        else:
            both = jnp.where(lane < HEAD_DIM, even, mean).astype(BF16)
            for i, ref in enumerate(out_refs):
                columns = slice(head // 2 * LANES, (head // 2 + 1) * LANES)
                ref[:rows, columns] = both[i * rows : (i + 1) * rows]
    packed = jnp.transpose(split_levels(levels, lane))[:LEVEL_ROWS].astype(BF16)
    for i, ref in enumerate(out_refs):
        for j in range(rows // (2 * LANES)):
            start = i * rows + j * 2 * LANES
            span = slice(rows + j * LEVEL_ROWS, rows + (j + 1) * LEVEL_ROWS)
            ref[span] = packed[:, start : start + 2 * LANES]


def attend(chunks, keys, values):
    count = len(chunks)
    rows = chunks[0].shape[0]
    return pl.pallas_call(
        functools.partial(attend_kernel, count),
        out_shape=[jax.ShapeDtypeStruct((rows + level_rows(rows), 2 * LANES), BF16)] * count,
        compiler_params=params(20),
        name="attend",
    )(*chunks, keys, values)


def spread_matrix(count):
    source = lax.broadcasted_iota(jnp.int32, (count, 2 * LANES), 0)
    target = lax.broadcasted_iota(jnp.int32, (count, 2 * LANES), 1)
    hit = (source < 12) & (source % 4 == target // HEAD_DIM)
    return jnp.where(hit, 1.0, 0.0).astype(BF16)


def side_levels(piece):
    return piece[:, : 2 * LANES], product(piece[:, 2 * LANES :], spread_matrix(LANES))


def under_levels(piece):
    rows = piece.shape[0] * 2 * LANES // (2 * LANES + LEVEL_ROWS)
    spread = spread_matrix(LEVEL_ROWS)
    levels = [
        product(piece[start : start + LEVEL_ROWS], spread, TN)
        for start in range(rows, piece.shape[0], LEVEL_ROWS)
    ]
    return piece[:rows], jnp.concatenate(levels, axis=0)


def merged(pieces, read):
    means, levels = zip(*[read(piece) for piece in pieces])
    highest = functools.reduce(jnp.maximum, levels)
    total, accum = None, None
    for mean, level in zip(means, levels):
        factor = jnp.exp(level - highest)
        term = factor * mean.astype(F32)
        total = factor if total is None else total + factor
        accum = term if accum is None else accum + term
    return accum / total, highest, total


def merge_kernel(count, read, *refs):
    out_refs = refs[count:]
    pieces = [ref[...] for ref in refs[:count]]
    if count == 1:
        pieces = [pieces[0][i] for i in range(pieces[0].shape[0])]
    mean, highest, total = merged(pieces, read)
    levels = highest + jnp.log(total)
    lane = lax.broadcasted_iota(jnp.int32, (levels.shape[0], LANES), 1)
    one, two = levels[:, :LANES], levels[:, LANES:]
    one_other, two_other = pltpu.roll(one, HEAD_DIM, 1), pltpu.roll(two, HEAD_DIM, 1)
    head = lane % 4
    picked = jnp.where(
        head == 0, one, jnp.where(head == 1, one_other, jnp.where(head == 2, two, two_other))
    )
    packed = split_levels(picked, lane).astype(BF16)
    rows = out_refs[0].shape[0]
    for i, ref in enumerate(out_refs):
        span = slice(i * rows, (i + 1) * rows)
        ref[:, : 2 * LANES] = mean[span].astype(BF16)
        ref[:, 2 * LANES :] = packed[span]


def merge(pieces, read, rows, parts):
    return pl.pallas_call(
        functools.partial(merge_kernel, len(pieces), read),
        out_shape=[jax.ShapeDtypeStruct((rows // parts, 3 * LANES), BF16)] * parts,
        compiler_params=params(24),
        name="merge",
    )(*pieces)


def project_kernel(count, *refs):
    w_ref, out_ref = refs[count:]
    mean, highest, total = merged([ref[...] for ref in refs[:count]], side_levels)
    projected = product(mean.astype(BF16), w_ref[...])
    columns = out_ref.shape[2]
    for i in range(out_ref.shape[0]):
        out_ref[i] = projected[:, i * columns : (i + 1) * columns]


def project(pieces, w_out):
    rows, width = pieces[0].shape[0], w_out.shape[1]
    return pl.pallas_call(
        functools.partial(project_kernel, len(pieces)),
        out_shape=jax.ShapeDtypeStruct((2, rows, width // 2), F32),
        compiler_params=params(8),
        name="project",
    )(*pieces, w_out)


def placed_call(kernel, name, out_shape, place, *operands):
    return pl.pallas_call(
        kernel,
        in_specs=[pl.BlockSpec(memory_space=pltpu.SMEM)]
        + [pl.BlockSpec(memory_space=pltpu.VMEM)] * len(operands),
        out_shape=out_shape,
        compiler_params=params(8),
        name=name,
    )(place, *operands)


def add_kernel(core_ref, halves_ref, other_ref, out_ref):
    out_ref[...] = halves_ref[core_ref[0]] + other_ref[...]


def residual_kernel(core_ref, one_ref, two_ref, latent_ref, out_ref):
    columns = out_ref.shape[1]
    own = latent_ref[:, pl.ds(pl.multiple_of(core_ref[0] * columns, LANES), columns)]
    out_ref[...] = (own.astype(F32) + (one_ref[...] + two_ref[...])).astype(BF16)


def mlp_kernel(core_ref, own_ref, other_ref, w_up_hbm, w_down_hbm, *refs):
    resid_ref, share_ref, w_up_ref, w_down_ref, sems = refs
    copies = [
        pltpu.make_async_copy(w_up_hbm, w_up_ref, sems.at[0]),
        pltpu.make_async_copy(w_down_hbm, w_down_ref, sems.at[1]),
    ]
    for copy in copies:
        copy.start()
    columns = resid_ref.shape[2]
    own, other = own_ref[...], other_ref[...]
    low = core_ref[0] == 0
    residual = jnp.concatenate([jnp.where(low, own, other), jnp.where(low, other, own)], axis=1)
    normed = norm_rows(residual.astype(F32)).astype(BF16)
    copies[0].wait()
    raised = product(normed, w_up_ref[...])
    hidden = (0.5 * raised * (1.0 + lax.erf(raised * 0.5**0.5))).astype(BF16)
    copies[1].wait()
    share = product(hidden, w_down_ref[...]).astype(BF16)
    for high in range(2):
        for core in range(2):
            i = high * 2 + core
            resid_ref[i] = residual[:, i * columns : (i + 1) * columns]
            share_ref[core, high] = share[:, i * columns : (i + 1) * columns]


def mlp(core, own, other, w_up, w_down):
    rows, half = own.shape
    vmem, hbm = pl.BlockSpec(memory_space=pltpu.VMEM), pl.BlockSpec(memory_space=pltpu.HBM)
    return pl.pallas_call(
        mlp_kernel,
        in_specs=[pl.BlockSpec(memory_space=pltpu.SMEM), vmem, vmem, hbm, hbm],
        out_shape=[
            jax.ShapeDtypeStruct((4, rows, half // 2), BF16),
            jax.ShapeDtypeStruct((2, 2, rows, half // 2), BF16),
        ],
        scratch_shapes=[
            pltpu.VMEM(w_up.shape, BF16),
            pltpu.VMEM(w_down.shape, BF16),
            pltpu.SemaphoreType.DMA((2,)),
        ],
        compiler_params=params(16),
        name="mlp",
    )(core, own, other, in_hbm(w_up), in_hbm(w_down))


def pair_kernel(place_ref, shares_ref, other_ref, kept_ref, sent_ref):
    high, core = place_ref[0], place_ref[1]
    for ref, index in ((kept_ref, high), (sent_ref, 1 - high)):
        ref[...] = shares_ref[core, index].astype(F32) + other_ref[index].astype(F32)


def close_kernel(place_ref, resid_ref, kept_ref, other_ref, out_ref):
    own = resid_ref[place_ref[0] * 2 + place_ref[1]]
    out_ref[...] = (own.astype(F32) + (kept_ref[...] + other_ref[...])).astype(BF16)


def along(value, axis, by):
    size = lax.axis_size(axis)
    return lax.ppermute(value, axis, [(i, (i + by) % size) for i in range(size)])


def swapped(value, axes, bits):
    size = lax.axis_size(axes)
    return lax.ppermute(value, axes, [(i, i ^ bits) for i in range(size)])


STEPS = (2, 1, 3)


def on_device(inputs, latent, w_query, w_key, w_value, w_out, w_up, w_down):
    queries = make_queries(latent, w_query)
    rows, columns = queries.shape
    count = lax.axis_size("z")
    both = jnp.concatenate([queries, swapped(queries, "ylo", 1)], axis=0)
    spread = jnp.broadcast_to(both[None], (count,) + both.shape)
    part = lax.all_to_all(spread, "z", 0, 0, tiled=True).reshape(count * 2 * rows, columns)
    arrived = [along(part, "x", by) for by in STEPS]
    inputs, part = lax.optimization_barrier((inputs, part))
    keys, values = make_keys_values(inputs, w_key, w_value)
    pieces = []
    for by, chunk in zip(STEPS, arrived):
        pieces.append(along(attend([chunk], keys, values)[0], "x", -by))
    pieces.append(attend([part], keys, values)[0])
    block = merge(pieces, under_levels, part.shape[0], 1)[0]
    block = lax.all_to_all(block.reshape(count, 2 * rows, -1), "z", 0, 0, tiled=True)
    own, others = merge([block], side_levels, 2 * rows, 2)
    pieces = [own, swapped(others, "ylo", 1)]
    high, core = lax.axis_index("yhi"), lax.axis_index("core")
    place = jnp.stack([high, core]).astype(jnp.int32)
    core_place = place[1:]
    width = latent.shape[1]
    half = jax.ShapeDtypeStruct((rows, width // 2), F32)
    quarter = jax.ShapeDtypeStruct((rows, width // 4), F32)
    halves = project(pieces, w_out)
    other = swapped(lax.dynamic_index_in_dim(halves, 1 - core, 0, keepdims=False), HEAD, 1)
    pair = placed_call(add_kernel, "pair_sum", half, core_place, halves, other)
    across = swapped(pair, HEAD, 2)
    resid_half = placed_call(
        residual_kernel,
        "residual",
        jax.ShapeDtypeStruct(half.shape, BF16),
        core_place,
        pair,
        across,
        latent,
    )
    resid, shares = mlp(core_place, resid_half, swapped(resid_half, HEAD, 1), w_up, w_down)
    other = swapped(lax.dynamic_index_in_dim(shares, 1 - core, 0, keepdims=False), HEAD, 1)
    kept, sent = placed_call(pair_kernel, "pair_shares", [quarter] * 2, place, shares, other)
    return placed_call(
        close_kernel,
        "close",
        jax.ShapeDtypeStruct(quarter.shape, BF16),
        place,
        resid,
        kept,
        swapped(sent, HEAD, 2),
    )


def solution(mesh):
    fine = Mesh(mesh.devices.reshape(4, 8, 2, 2, 2), SEQ + HEAD)
    placed = (
        P(SEQ, None),
        P(SEQ, None),
        P(None, HEAD),
        P(None, HEAD),
        P(None, HEAD),
        P(HEAD, None),
        P(None, HEAD),
        P(HEAD, None),
    )
    return jax.shard_map(
        on_device, mesh=fine, in_specs=placed, out_specs=P(SEQ, HEAD), check_vma=False
    )
```

```python
import functools

import jax
import jax.numpy as jnp
from jax import lax
from jax.experimental import pallas as pl
from jax.experimental.pallas import tpu as pltpu
from jax.sharding import Mesh
from jax.sharding import PartitionSpec as P

HEAD_DIM = 64
HEADS_HERE = 4
LEVEL_ROWS = 16
LANES = 128
SEQ = ("x", "z", "ylo")
HEAD = ("yhi", "core")
BF16 = jnp.bfloat16
F32 = jnp.float32
NT = (((1,), (1,)), ((), ()))
NN = (((1,), (0,)), ((), ()))
TN = (((0,), (0,)), ((), ()))


def product(left, right, numbers=NN):
    return lax.dot_general(left, right, numbers, preferred_element_type=F32)


def params(mib):
    return pltpu.CompilerParams(vmem_limit_bytes=mib * 2**20)


def norm_rows(widened):
    width = widened.shape[-1]
    row_mean = jnp.sum(widened, axis=-1, keepdims=True) / width
    row_square = jnp.sum(widened * widened, axis=-1, keepdims=True) / width
    row_var = row_square - row_mean * row_mean
    return (widened - row_mean) * lax.rsqrt(row_var + 1e-05)


def in_hbm(value):
    return pltpu.with_memory_space_constraint(value, pltpu.HBM)


def query_kernel(latent_hbm, w_hbm, out_ref, latent_ref, w_ref, sems):
    copies = [
        pltpu.make_async_copy(latent_hbm, latent_ref, sems.at[0]),
        pltpu.make_async_copy(w_hbm, w_ref, sems.at[1]),
    ]
    for copy in copies:
        copy.start()
    copies[0].wait()
    normed = norm_rows(latent_ref[...].astype(F32)).astype(BF16)
    copies[1].wait()
    out_ref[...] = (product(normed, w_ref[...]) * HEAD_DIM ** (-0.5)).astype(BF16)


def make_queries(latent, w_query):
    return pl.pallas_call(
        query_kernel,
        in_specs=[pl.BlockSpec(memory_space=pltpu.HBM)] * 2,
        out_shape=jax.ShapeDtypeStruct((latent.shape[0], w_query.shape[1]), BF16),
        scratch_shapes=[
            pltpu.VMEM(latent.shape, BF16),
            pltpu.VMEM(w_query.shape, BF16),
            pltpu.SemaphoreType.DMA((2,)),
        ],
        compiler_params=params(8),
        name="make_queries",
    )(in_hbm(latent), in_hbm(w_query))


def key_value_kernel(
    block, x_hbm, w_key_hbm, w_value_hbm, key_ref, value_ref, x_ref, w_key_ref, w_value_ref, sems
):
    tokens = x_ref.shape[0]
    weights = [
        pltpu.make_async_copy(w_key_hbm, w_key_ref, sems.at[0]),
        pltpu.make_async_copy(w_value_hbm, w_value_ref, sems.at[1]),
    ]
    spans = [slice(start, start + block) for start in range(0, tokens, block)]
    copies = [
        pltpu.make_async_copy(x_hbm.at[span], x_ref.at[span], sems.at[2 + i])
        for i, span in enumerate(spans)
    ]
    for copy in copies[:1] + weights + copies[1:]:
        copy.start()
    lane = lax.broadcasted_iota(jnp.int32, (block, LANES), 1)
    low = lane < HEAD_DIM
    for i, span in enumerate(spans):
        copies[i].wait()
        normed = norm_rows(x_ref[span].astype(F32)).astype(BF16)
        if i == 0:
            weights[0].wait()
            weights[1].wait()
        keys = product(normed, w_key_ref[...]).astype(BF16)
        vals = product(normed, w_value_ref[...])
        for head in range(HEADS_HERE):
            key_ref[head, span] = keys[:, head * HEAD_DIM : (head + 1) * HEAD_DIM]
            pair = vals[:, head // 2 * LANES : (head // 2 + 1) * LANES]
            one = jnp.where(lane == (HEAD_DIM if head % 2 == 0 else 0), 1.0, 0.0)
            kept = jnp.where(low, pair, one) if head % 2 == 0 else jnp.where(low, one, pair)
            value_ref[head, span] = kept.astype(BF16)


def make_keys_values(x, w_key, w_value):
    tokens = x.shape[0]
    block = 512
    return pl.pallas_call(
        functools.partial(key_value_kernel, block),
        in_specs=[pl.BlockSpec(memory_space=pltpu.HBM)] * 3,
        out_shape=[
            jax.ShapeDtypeStruct((HEADS_HERE, tokens, HEAD_DIM), BF16),
            jax.ShapeDtypeStruct((HEADS_HERE, tokens, LANES), BF16),
        ],
        scratch_shapes=[
            pltpu.VMEM(x.shape, BF16),
            pltpu.VMEM(w_key.shape, BF16),
            pltpu.VMEM(w_value.shape, BF16),
            pltpu.SemaphoreType.DMA((2 + tokens // block,)),
        ],
        compiler_params=params(16),
        name="make_keys_values",
    )(in_hbm(x), in_hbm(w_key), in_hbm(w_value))


def split_levels(levels, lane):
    first = levels.astype(BF16).astype(F32)
    rest = levels - first
    second = rest.astype(BF16).astype(F32)
    third = rest - second
    parts = jnp.where(lane < 4, first, jnp.where(lane < 8, second, third))
    return jnp.where(lane < 12, parts, 0.0)


def level_rows(rows):
    return rows // (2 * LANES) * LEVEL_ROWS


def attend_kernel(count, fetched, *refs):
    query_refs, (key_ref, value_ref) = refs[:count], refs[count : count + 2]
    out_refs = refs[count + 2 + fetched :][:count]
    copies = []
    if fetched:
        sems = refs[-1]
        sources, kept = refs[count + 2 :][:fetched], refs[2 * count + 2 + fetched :][:fetched]
        for i, (source, target) in enumerate(zip(sources, kept)):
            copies.append(pltpu.make_async_copy(source, target, sems.at[i]))
    for copy in copies:
        copy.start()
    rows = query_refs[0].shape[0]
    total_rows = rows * count

    def scores_of(head):
        columns = slice(head * HEAD_DIM, (head + 1) * HEAD_DIM)
        parts = [ref[:, columns] for ref in query_refs]
        part = parts[0] if count == 1 else jnp.concatenate(parts, axis=0)
        return product(part, key_ref[head], NT)

    lane = lax.broadcasted_iota(jnp.int32, (total_rows, LANES), 1)
    levels = jnp.zeros((total_rows, LANES), F32)
    following = scores_of(0)
    even = None
    for head in range(HEADS_HERE):
        scores = following
        if head + 1 < HEADS_HERE:
            following = scores_of(head + 1)
        highest = jnp.max(scores, axis=1, keepdims=True)
        weights = jnp.exp(scores - highest).astype(BF16)
        accum = product(weights, value_ref[head])
        place = HEAD_DIM if head % 2 == 0 else 0
        total = accum[:, place : place + 1]
        mean = accum * (1.0 / total)
        levels = jnp.where(lane % 4 == head, highest + jnp.log(total), levels)
        if head % 2 == 0:
            even = mean
        else:
            both = jnp.where(lane < HEAD_DIM, even, mean).astype(BF16)
            for i, ref in enumerate(out_refs):
                columns = slice(head // 2 * LANES, (head // 2 + 1) * LANES)
                ref[:rows, columns] = both[i * rows : (i + 1) * rows]
    packed = jnp.transpose(split_levels(levels, lane))[:LEVEL_ROWS].astype(BF16)
    for i, ref in enumerate(out_refs):
        for j in range(rows // (2 * LANES)):
            start = i * rows + j * 2 * LANES
            span = slice(rows + j * LEVEL_ROWS, rows + (j + 1) * LEVEL_ROWS)
            ref[span] = packed[:, start : start + 2 * LANES]
    for copy in copies:
        copy.wait()


def attend(chunks, keys, values, fetched=()):
    count = len(chunks)
    rows = chunks[0].shape[0]
    out = jax.ShapeDtypeStruct((rows + level_rows(rows), 2 * LANES), BF16)
    vmem, hbm = pl.BlockSpec(memory_space=pltpu.VMEM), pl.BlockSpec(memory_space=pltpu.HBM)
    return pl.pallas_call(
        functools.partial(attend_kernel, count, len(fetched)),
        in_specs=[vmem] * (count + 2) + [hbm] * len(fetched),
        out_shape=[out] * count + [jax.ShapeDtypeStruct(w.shape, BF16) for w in fetched],
        scratch_shapes=[pltpu.SemaphoreType.DMA((len(fetched),))] if fetched else [],
        compiler_params=params(24),
        name="attend",
    )(*chunks, keys, values, *[in_hbm(w) for w in fetched])


def spread_matrix(count):
    source = lax.broadcasted_iota(jnp.int32, (count, 2 * LANES), 0)
    target = lax.broadcasted_iota(jnp.int32, (count, 2 * LANES), 1)
    hit = (source < 12) & (source % 4 == target // HEAD_DIM)
    return jnp.where(hit, 1.0, 0.0).astype(BF16)


def side_levels(piece):
    return piece[:, : 2 * LANES], product(piece[:, 2 * LANES :], spread_matrix(LANES))


def under_levels(piece):
    rows = piece.shape[0] * 2 * LANES // (2 * LANES + LEVEL_ROWS)
    spread = spread_matrix(LEVEL_ROWS)
    levels = [
        product(piece[start : start + LEVEL_ROWS], spread, TN)
        for start in range(rows, piece.shape[0], LEVEL_ROWS)
    ]
    return piece[:rows], jnp.concatenate(levels, axis=0)


def merged(pieces, read):
    means, levels = zip(*[read(piece) for piece in pieces])
    highest = functools.reduce(jnp.maximum, levels)
    total, accum = None, None
    for mean, level in zip(means, levels):
        factor = jnp.exp(level - highest)
        term = factor * mean.astype(F32)
        total = factor if total is None else total + factor
        accum = term if accum is None else accum + term
    return accum / total, highest, total


def merge_kernel(count, read, targets, *refs):
    out_refs = refs[count:]
    pieces = [ref[...] for ref in refs[:count]]
    if count == 1:
        pieces = [pieces[0][i] for i in range(pieces[0].shape[0])]
    mean, highest, total = merged(pieces, read)
    levels = highest + jnp.log(total)
    lane = lax.broadcasted_iota(jnp.int32, (levels.shape[0], LANES), 1)
    one, two = levels[:, :LANES], levels[:, LANES:]
    one_other, two_other = pltpu.roll(one, HEAD_DIM, 1), pltpu.roll(two, HEAD_DIM, 1)
    head = lane % 4
    picked = jnp.where(
        head == 0, one, jnp.where(head == 1, one_other, jnp.where(head == 2, two, two_other))
    )
    packed = split_levels(picked, lane).astype(BF16)
    mean = mean.astype(BF16)
    for ref, index, source, rows in targets(out_refs):
        span = slice(source, source + rows)
        ref[index + (slice(None, 2 * LANES),)] = mean[span]
        ref[index + (slice(2 * LANES, None),)] = packed[span]


def in_turn(refs):
    rows = refs[0].shape[0]
    return [(ref, (slice(None),), i * rows, rows) for i, ref in enumerate(refs)]


def side_by_side(refs):
    count, pair, _ = refs[0].shape
    rows = pair // 2
    return [
        (refs[0], (i, slice(half * rows, (half + 1) * rows)), (half * count + i) * rows, rows)
        for half in range(2)
        for i in range(count)
    ]


def merge(pieces, read, targets, shapes):
    return pl.pallas_call(
        functools.partial(merge_kernel, len(pieces), read, targets),
        out_shape=[jax.ShapeDtypeStruct(shape, BF16) for shape in shapes],
        compiler_params=params(24),
        name="merge",
    )(*pieces)


def project_kernel(count, *refs):
    w_ref, out_ref = refs[count:]
    mean, highest, total = merged([ref[...] for ref in refs[:count]], side_levels)
    projected = product(mean.astype(BF16), w_ref[...])
    columns = out_ref.shape[2]
    for i in range(out_ref.shape[0]):
        out_ref[i] = projected[:, i * columns : (i + 1) * columns]


def project(pieces, w_out):
    rows, width = pieces[0].shape[0], w_out.shape[1]
    return pl.pallas_call(
        functools.partial(project_kernel, len(pieces)),
        out_shape=jax.ShapeDtypeStruct((2, rows, width // 2), F32),
        compiler_params=params(8),
        name="project",
    )(*pieces, w_out)


def placed_call(kernel, name, out_shape, place, *operands):
    return pl.pallas_call(
        kernel,
        in_specs=[pl.BlockSpec(memory_space=pltpu.SMEM)]
        + [pl.BlockSpec(memory_space=pltpu.VMEM)] * len(operands),
        out_shape=out_shape,
        compiler_params=params(8),
        name=name,
    )(place, *operands)


def add_kernel(place_ref, halves_ref, other_ref, out_ref):
    out_ref[...] = halves_ref[place_ref[0] % 2] + other_ref[...]


def residual_kernel(place_ref, one_ref, two_ref, latent_ref, out_ref):
    columns = out_ref.shape[1]
    own = latent_ref[:, pl.ds(pl.multiple_of(place_ref[0] % 2 * columns, LANES), columns)]
    out_ref[...] = (own.astype(F32) + (one_ref[...] + two_ref[...])).astype(BF16)


def mlp_kernel(
    place_ref, own_ref, other_ref, w_up_ref, w_down_hbm, resid_ref, share_ref, w_down_ref, sem
):
    copy = pltpu.make_async_copy(w_down_hbm, w_down_ref, sem)
    copy.start()
    columns = resid_ref.shape[2]
    own, other = own_ref[...], other_ref[...]
    low = place_ref[0] % 2 == 0
    residual = jnp.concatenate([jnp.where(low, own, other), jnp.where(low, other, own)], axis=1)
    normed = norm_rows(residual.astype(F32)).astype(BF16)
    raised = product(normed, w_up_ref[...])
    hidden = (0.5 * raised * (1.0 + lax.erf(raised * 0.5**0.5))).astype(BF16)
    copy.wait()
    share = product(hidden, w_down_ref[...]).astype(BF16)
    for high in range(2):
        for core in range(2):
            i = high * 2 + core
            resid_ref[i] = residual[:, i * columns : (i + 1) * columns]
            share_ref[core, high] = share[:, i * columns : (i + 1) * columns]


def mlp(place, own, other, w_up, w_down):
    rows, half = own.shape
    vmem, hbm = pl.BlockSpec(memory_space=pltpu.VMEM), pl.BlockSpec(memory_space=pltpu.HBM)
    return pl.pallas_call(
        mlp_kernel,
        in_specs=[pl.BlockSpec(memory_space=pltpu.SMEM), vmem, vmem, vmem, hbm],
        out_shape=[
            jax.ShapeDtypeStruct((4, rows, half // 2), BF16),
            jax.ShapeDtypeStruct((2, 2, rows, half // 2), BF16),
        ],
        scratch_shapes=[pltpu.VMEM(w_down.shape, BF16), pltpu.SemaphoreType.DMA],
        compiler_params=params(16),
        name="mlp",
    )(place, own, other, w_up, in_hbm(w_down))


def pair_kernel(place_ref, shares_ref, other_ref, kept_ref, sent_ref):
    high, core = place_ref[0] // 2, place_ref[0] % 2
    for ref, index in ((kept_ref, high), (sent_ref, 1 - high)):
        ref[...] = shares_ref[core, index].astype(F32) + other_ref[index].astype(F32)


def close_kernel(place_ref, resid_ref, kept_ref, other_ref, out_ref):
    own = resid_ref[place_ref[0]]
    out_ref[...] = (own.astype(F32) + (kept_ref[...] + other_ref[...])).astype(BF16)


def along(value, axis, by):
    size = lax.axis_size(axis)
    return lax.ppermute(value, axis, [(i, (i + by) % size) for i in range(size)])


def swapped(value, axes, bits):
    size = lax.axis_size(axes)
    return lax.ppermute(value, axes, [(i, i ^ bits) for i in range(size)])


STEPS = (2, 1, 3)


def on_device(inputs, latent, w_query, w_key, w_value, w_out, w_up, w_down):
    queries = make_queries(latent, w_query)
    rows, columns = queries.shape
    count = lax.axis_size("z")
    spread = jnp.broadcast_to(queries[None], (count,) + queries.shape)
    part = lax.all_to_all(spread, "z", 0, 0, tiled=True).reshape(count * rows, columns)
    part = jnp.concatenate([part, swapped(part, "ylo", 1)], axis=0)
    arrived = [along(part, "x", by) for by in STEPS]
    inputs, part = lax.optimization_barrier((inputs, part))
    keys, values = make_keys_values(inputs, w_key, w_value)
    pieces = []
    for by, chunk in zip(STEPS, arrived):
        pieces.append(along(attend([chunk], keys, values)[0], "x", -by))
    piece, w_up = attend([part], keys, values, (w_up,))
    pieces.append(piece)
    block = merge(pieces, under_levels, side_by_side, [(count, 2 * rows, 3 * LANES)])[0]
    block = lax.all_to_all(block, "z", 0, 0, tiled=True)
    own, others = merge([block], side_levels, in_turn, [(rows, 3 * LANES)] * 2)
    pieces = [own, swapped(others, "ylo", 1)]
    high, core = lax.axis_index("yhi"), lax.axis_index("core")
    place = (high * 2 + core).astype(jnp.int32).reshape(1)
    width = latent.shape[1]
    half = jax.ShapeDtypeStruct((rows, width // 2), F32)
    quarter = jax.ShapeDtypeStruct((rows, width // 4), F32)
    halves = project(pieces, w_out)
    other = swapped(lax.dynamic_index_in_dim(halves, 1 - core, 0, keepdims=False), HEAD, 1)
    pair = placed_call(add_kernel, "pair_sum", half, place, halves, other)
    across = swapped(pair, HEAD, 2)
    resid_half = placed_call(
        residual_kernel,
        "residual",
        jax.ShapeDtypeStruct(half.shape, BF16),
        place,
        pair,
        across,
        latent,
    )
    resid, shares = mlp(place, resid_half, swapped(resid_half, HEAD, 1), w_up, w_down)
    other = swapped(lax.dynamic_index_in_dim(shares, 1 - core, 0, keepdims=False), HEAD, 1)
    kept, sent = placed_call(pair_kernel, "pair_shares", [quarter] * 2, place, shares, other)
    return placed_call(
        close_kernel,
        "close",
        jax.ShapeDtypeStruct(quarter.shape, BF16),
        place,
        resid,
        kept,
        swapped(sent, HEAD, 2),
    )


def solution(mesh):
    fine = Mesh(mesh.devices.reshape(4, 8, 2, 2, 2), SEQ + HEAD)
    placed = (
        P(SEQ, None),
        P(SEQ, None),
        P(None, HEAD),
        P(None, HEAD),
        P(None, HEAD),
        P(HEAD, None),
        P(None, HEAD),
        P(HEAD, None),
    )
    return jax.shard_map(
        on_device, mesh=fine, in_specs=placed, out_specs=P(SEQ, HEAD), check_vma=False
    )
```

```python
import functools

import jax
import jax.numpy as jnp
from jax import lax
from jax.experimental import pallas as pl
from jax.experimental.pallas import tpu as pltpu
from jax.sharding import Mesh
from jax.sharding import PartitionSpec as P

HEAD_DIM = 64
HEADS_HERE = 4
LEVEL_ROWS = 16
LANES = 128
SEQ = ("x", "z", "ylo")
HEAD = ("yhi", "core")
BF16 = jnp.bfloat16
F32 = jnp.float32
NT = (((1,), (1,)), ((), ()))
NN = (((1,), (0,)), ((), ()))
TN = (((0,), (0,)), ((), ()))


def product(left, right, numbers=NN):
    return lax.dot_general(left, right, numbers, preferred_element_type=F32)


def params(mib):
    return pltpu.CompilerParams(vmem_limit_bytes=mib * 2**20)


def norm_rows(widened):
    width = widened.shape[-1]
    row_mean = jnp.sum(widened, axis=-1, keepdims=True) / width
    row_square = jnp.sum(widened * widened, axis=-1, keepdims=True) / width
    row_var = row_square - row_mean * row_mean
    return (widened - row_mean) * lax.rsqrt(row_var + 1e-05)


def in_hbm(value):
    return pltpu.with_memory_space_constraint(value, pltpu.HBM)


def query_kernel(latent_hbm, w_hbm, out_ref, latent_ref, w_ref, sems):
    copies = [
        pltpu.make_async_copy(latent_hbm, latent_ref, sems.at[0]),
        pltpu.make_async_copy(w_hbm, w_ref, sems.at[1]),
    ]
    for copy in copies:
        copy.start()
    copies[0].wait()
    normed = norm_rows(latent_ref[...].astype(F32)).astype(BF16)
    copies[1].wait()
    out_ref[...] = (product(normed, w_ref[...]) * HEAD_DIM ** (-0.5)).astype(BF16)


def make_queries(latent, w_query):
    return pl.pallas_call(
        query_kernel,
        in_specs=[pl.BlockSpec(memory_space=pltpu.HBM)] * 2,
        out_shape=jax.ShapeDtypeStruct((latent.shape[0], w_query.shape[1]), BF16),
        scratch_shapes=[
            pltpu.VMEM(latent.shape, BF16),
            pltpu.VMEM(w_query.shape, BF16),
            pltpu.SemaphoreType.DMA((2,)),
        ],
        compiler_params=params(8),
        name="make_queries",
    )(in_hbm(latent), in_hbm(w_query))


def key_value_kernel(
    block, x_hbm, w_key_hbm, w_value_hbm, key_ref, value_ref, x_ref, w_key_ref, w_value_ref, sems
):
    tokens = x_ref.shape[0]
    weights = [
        pltpu.make_async_copy(w_key_hbm, w_key_ref, sems.at[0]),
        pltpu.make_async_copy(w_value_hbm, w_value_ref, sems.at[1]),
    ]
    spans = [slice(start, start + block) for start in range(0, tokens, block)]
    copies = [
        pltpu.make_async_copy(x_hbm.at[span], x_ref.at[span], sems.at[2 + i])
        for i, span in enumerate(spans)
    ]
    for copy in copies[:1] + weights + copies[1:]:
        copy.start()
    lane = lax.broadcasted_iota(jnp.int32, (block, LANES), 1)
    low = lane < HEAD_DIM
    copies[0].wait()
    following = norm_rows(x_ref[spans[0]].astype(F32)).astype(BF16)
    weights[0].wait()
    weights[1].wait()
    for i, span in enumerate(spans):
        normed = following
        if i + 1 < len(spans):
            copies[i + 1].wait()
            following = norm_rows(x_ref[spans[i + 1]].astype(F32)).astype(BF16)
        keys = product(normed, w_key_ref[...]).astype(BF16)
        vals = product(normed, w_value_ref[...])
        for head in range(HEADS_HERE):
            key_ref[head, span] = keys[:, head * HEAD_DIM : (head + 1) * HEAD_DIM]
            pair = vals[:, head // 2 * LANES : (head // 2 + 1) * LANES]
            one = jnp.where(lane == (HEAD_DIM if head % 2 == 0 else 0), 1.0, 0.0)
            kept = jnp.where(low, pair, one) if head % 2 == 0 else jnp.where(low, one, pair)
            value_ref[head, span] = kept.astype(BF16)


def make_keys_values(x, w_key, w_value):
    tokens = x.shape[0]
    block = 512
    return pl.pallas_call(
        functools.partial(key_value_kernel, block),
        in_specs=[pl.BlockSpec(memory_space=pltpu.HBM)] * 3,
        out_shape=[
            jax.ShapeDtypeStruct((HEADS_HERE, tokens, HEAD_DIM), BF16),
            jax.ShapeDtypeStruct((HEADS_HERE, tokens, LANES), BF16),
        ],
        scratch_shapes=[
            pltpu.VMEM(x.shape, BF16),
            pltpu.VMEM(w_key.shape, BF16),
            pltpu.VMEM(w_value.shape, BF16),
            pltpu.SemaphoreType.DMA((2 + tokens // block,)),
        ],
        compiler_params=params(16),
        name="make_keys_values",
    )(in_hbm(x), in_hbm(w_key), in_hbm(w_value))


def split_levels(levels, lane):
    first = levels.astype(BF16).astype(F32)
    rest = levels - first
    second = rest.astype(BF16).astype(F32)
    third = rest - second
    parts = jnp.where(lane < 4, first, jnp.where(lane < 8, second, third))
    return jnp.where(lane < 12, parts, 0.0)


def level_rows(rows):
    return rows // (2 * LANES) * LEVEL_ROWS


def attend_kernel(count, fetched, *refs):
    query_refs, (key_ref, value_ref) = refs[:count], refs[count : count + 2]
    out_refs = refs[count + 2 + fetched :][:count]
    copies = []
    if fetched:
        sems = refs[-1]
        sources, kept = refs[count + 2 :][:fetched], refs[2 * count + 2 + fetched :][:fetched]
        for i, (source, target) in enumerate(zip(sources, kept)):
            copies.append(pltpu.make_async_copy(source, target, sems.at[i]))
    for copy in copies:
        copy.start()
    rows = query_refs[0].shape[0]
    total_rows = rows * count

    def scores_of(head):
        columns = slice(head * HEAD_DIM, (head + 1) * HEAD_DIM)
        parts = [ref[:, columns] for ref in query_refs]
        part = parts[0] if count == 1 else jnp.concatenate(parts, axis=0)
        return product(part, key_ref[head], NT)

    lane = lax.broadcasted_iota(jnp.int32, (total_rows, LANES), 1)
    levels = jnp.zeros((total_rows, LANES), F32)
    following = scores_of(0)
    even = None
    for head in range(HEADS_HERE):
        scores = following
        if head + 1 < HEADS_HERE:
            following = scores_of(head + 1)
        highest = jnp.max(scores, axis=1, keepdims=True)
        weights = jnp.exp(scores - highest).astype(BF16)
        accum = product(weights, value_ref[head])
        place = HEAD_DIM if head % 2 == 0 else 0
        total = accum[:, place : place + 1]
        mean = accum * (1.0 / total)
        levels = jnp.where(lane % 4 == head, highest + jnp.log(total), levels)
        if head % 2 == 0:
            even = mean
        else:
            both = jnp.where(lane < HEAD_DIM, even, mean).astype(BF16)
            for i, ref in enumerate(out_refs):
                columns = slice(head // 2 * LANES, (head // 2 + 1) * LANES)
                ref[:rows, columns] = both[i * rows : (i + 1) * rows]
    packed = jnp.transpose(split_levels(levels, lane))[:LEVEL_ROWS].astype(BF16)
    for i, ref in enumerate(out_refs):
        for j in range(rows // (2 * LANES)):
            start = i * rows + j * 2 * LANES
            span = slice(rows + j * LEVEL_ROWS, rows + (j + 1) * LEVEL_ROWS)
            ref[span] = packed[:, start : start + 2 * LANES]
    for copy in copies:
        copy.wait()


def attend(chunks, keys, values, fetched=()):
    count = len(chunks)
    rows = chunks[0].shape[0]
    out = jax.ShapeDtypeStruct((rows + level_rows(rows), 2 * LANES), BF16)
    vmem, hbm = pl.BlockSpec(memory_space=pltpu.VMEM), pl.BlockSpec(memory_space=pltpu.HBM)
    return pl.pallas_call(
        functools.partial(attend_kernel, count, len(fetched)),
        in_specs=[vmem] * (count + 2) + [hbm] * len(fetched),
        out_shape=[out] * count + [jax.ShapeDtypeStruct(w.shape, BF16) for w in fetched],
        scratch_shapes=[pltpu.SemaphoreType.DMA((len(fetched),))] if fetched else [],
        compiler_params=params(24),
        name="attend",
    )(*chunks, keys, values, *[in_hbm(w) for w in fetched])


def spread_matrix(count):
    source = lax.broadcasted_iota(jnp.int32, (count, 2 * LANES), 0)
    target = lax.broadcasted_iota(jnp.int32, (count, 2 * LANES), 1)
    hit = (source < 12) & (source % 4 == target // HEAD_DIM)
    return jnp.where(hit, 1.0, 0.0).astype(BF16)


def side_levels(piece):
    return piece[:, : 2 * LANES], product(piece[:, 2 * LANES :], spread_matrix(LANES))


def under_levels(piece):
    rows = piece.shape[0] * 2 * LANES // (2 * LANES + LEVEL_ROWS)
    spread = spread_matrix(LEVEL_ROWS)
    levels = [
        product(piece[start : start + LEVEL_ROWS], spread, TN)
        for start in range(rows, piece.shape[0], LEVEL_ROWS)
    ]
    return piece[:rows], jnp.concatenate(levels, axis=0)


def merged(pieces, read):
    means, levels = zip(*[read(piece) for piece in pieces])
    highest = functools.reduce(jnp.maximum, levels)
    total, accum = None, None
    for mean, level in zip(means, levels):
        factor = jnp.exp(level - highest)
        term = factor * mean.astype(F32)
        total = factor if total is None else total + factor
        accum = term if accum is None else accum + term
    return accum / total, highest, total


def merge_kernel(count, write, *refs):
    out_refs = refs[count:]
    mean, highest, total = merged([ref[...] for ref in refs[:count]], under_levels)
    levels = highest + jnp.log(total)
    lane = lax.broadcasted_iota(jnp.int32, (levels.shape[0], LANES), 1)
    one, two = levels[:, :LANES], levels[:, LANES:]
    one_other, two_other = pltpu.roll(one, HEAD_DIM, 1), pltpu.roll(two, HEAD_DIM, 1)
    head = lane % 4
    picked = jnp.where(
        head == 0, one, jnp.where(head == 1, one_other, jnp.where(head == 2, two, two_other))
    )
    write(out_refs, mean.astype(BF16), split_levels(picked, lane))


def write_halves(refs, mean, parts):
    rows = mean.shape[0] // len(refs)
    turned = jnp.transpose(parts)[:LEVEL_ROWS].astype(BF16)
    for i, ref in enumerate(refs):
        ref[:rows] = mean[i * rows : (i + 1) * rows]
        for j in range(rows // (2 * LANES)):
            start = i * rows + j * 2 * LANES
            span = slice(rows + j * LEVEL_ROWS, rows + (j + 1) * LEVEL_ROWS)
            ref[span] = turned[:, start : start + 2 * LANES]


def write_blocks(refs, mean, parts):
    count, rows, _ = refs[0].shape
    parts = parts.astype(BF16)
    for i in range(count):
        refs[0][i, :, : 2 * LANES] = mean[i * rows : (i + 1) * rows]
        refs[0][i, :, 2 * LANES :] = parts[i * rows : (i + 1) * rows]


def merge(pieces, write, shapes):
    return pl.pallas_call(
        functools.partial(merge_kernel, len(pieces), write),
        out_shape=[jax.ShapeDtypeStruct(shape, BF16) for shape in shapes],
        compiler_params=params(24),
        name="merge",
    )(*pieces)


def placed_call(kernel, name, out_shape, place, *operands):
    return pl.pallas_call(
        kernel,
        in_specs=[pl.BlockSpec(memory_space=pltpu.SMEM)]
        + [pl.BlockSpec(memory_space=pltpu.VMEM)] * len(operands),
        out_shape=out_shape,
        compiler_params=params(8),
        name=name,
    )(place, *operands)


def ordered(place_ref, low, high):
    first = place_ref[0] % 2 == 0
    return jnp.where(first, low, high), jnp.where(first, high, low)


def project_kernel(place_ref, pieces_ref, w_ref, kept_ref, sent_ref):
    pieces = [pieces_ref[i] for i in range(pieces_ref.shape[0])]
    mean, highest, total = merged(pieces, side_levels)
    projected = product(mean.astype(BF16), w_ref[...])
    columns = kept_ref.shape[1]
    halves = ordered(place_ref, projected[:, :columns], projected[:, columns:])
    kept_ref[...], sent_ref[...] = halves


def add_kernel(place_ref, kept_ref, other_ref, out_ref):
    out_ref[...] = kept_ref[...] + other_ref[...]


def residual_kernel(place_ref, one_ref, two_ref, latent_ref, out_ref):
    columns = out_ref.shape[1]
    own = latent_ref[:, pl.ds(pl.multiple_of(place_ref[0] % 2 * columns, LANES), columns)]
    out_ref[...] = (own.astype(F32) + (one_ref[...] + two_ref[...])).astype(BF16)


def mlp_kernel(
    place_ref,
    own_ref,
    other_ref,
    w_up_ref,
    w_down_hbm,
    resid_ref,
    kept_ref,
    sent_ref,
    w_down_ref,
    sem,
):
    copy = pltpu.make_async_copy(w_down_hbm, w_down_ref, sem)
    copy.start()
    columns = resid_ref.shape[2]
    halves = ordered(place_ref, own_ref[...], other_ref[...])
    residual = jnp.concatenate(halves, axis=1)
    normed = norm_rows(residual.astype(F32)).astype(BF16)
    raised = product(normed, w_up_ref[...])
    hidden = (0.5 * raised * (1.0 + lax.erf(raised * 0.5**0.5))).astype(BF16)
    copy.wait()
    share = product(hidden, w_down_ref[...]).astype(BF16)
    blocks = [share[:, i * columns : (i + 1) * columns] for i in range(4)]
    for i in range(4):
        resid_ref[i] = residual[:, i * columns : (i + 1) * columns]
    for high in range(2):
        pair = ordered(place_ref, blocks[2 * high], blocks[2 * high + 1])
        kept_ref[high], sent_ref[high] = pair


def mlp(place, own, other, w_up, w_down):
    rows, half = own.shape
    vmem, hbm = pl.BlockSpec(memory_space=pltpu.VMEM), pl.BlockSpec(memory_space=pltpu.HBM)
    return pl.pallas_call(
        mlp_kernel,
        in_specs=[pl.BlockSpec(memory_space=pltpu.SMEM), vmem, vmem, vmem, hbm],
        out_shape=[
            jax.ShapeDtypeStruct((4, rows, half // 2), BF16),
        ]
        + [jax.ShapeDtypeStruct((2, rows, half // 2), BF16)] * 2,
        scratch_shapes=[pltpu.VMEM(w_down.shape, BF16), pltpu.SemaphoreType.DMA],
        compiler_params=params(16),
        name="mlp",
    )(place, own, other, w_up, in_hbm(w_down))


def pair_kernel(place_ref, shares_ref, other_ref, kept_ref, sent_ref):
    high = place_ref[0] // 2
    for ref, index in ((kept_ref, high), (sent_ref, 1 - high)):
        ref[...] = shares_ref[index].astype(F32) + other_ref[index].astype(F32)


def close_kernel(place_ref, resid_ref, kept_ref, other_ref, out_ref):
    own = resid_ref[place_ref[0]]
    out_ref[...] = (own.astype(F32) + (kept_ref[...] + other_ref[...])).astype(BF16)


def along(value, axis, by):
    size = lax.axis_size(axis)
    return lax.ppermute(value, axis, [(i, (i + by) % size) for i in range(size)])


def swapped(value, axes, bits):
    size = lax.axis_size(axes)
    return lax.ppermute(value, axes, [(i, i ^ bits) for i in range(size)])


STEPS = (2, 1, 3)


def on_device(inputs, latent, w_query, w_key, w_value, w_out, w_up, w_down):
    queries = make_queries(latent, w_query)
    rows, columns = queries.shape
    count = lax.axis_size("z")
    spread = jnp.broadcast_to(queries[None], (count,) + queries.shape)
    part = lax.all_to_all(spread, "z", 0, 0, tiled=True).reshape(count * rows, columns)
    part = jnp.concatenate([part, swapped(part, "ylo", 1)], axis=0)
    arrived = [along(part, "x", by) for by in STEPS]
    inputs, part = lax.optimization_barrier((inputs, part))
    keys, values = make_keys_values(inputs, w_key, w_value)
    pieces = []
    for by, chunk in zip(STEPS, arrived):
        pieces.append(along(attend([chunk], keys, values)[0], "x", -by))
    piece, w_up = attend([part], keys, values, (w_up,))
    pieces.append(piece)
    half = (count * rows + level_rows(count * rows), columns)
    own, others = merge(pieces, write_halves, [half] * 2)
    block = merge([own, swapped(others, "ylo", 1)], write_blocks, [(count, rows, 3 * LANES)])[0]
    place = lax.axis_index(HEAD).astype(jnp.int32).reshape(1)
    block, place = lax.optimization_barrier((block, place))
    pieces = lax.all_to_all(block, "z", 0, 0, tiled=True)
    width = latent.shape[1]
    half = jax.ShapeDtypeStruct((rows, width // 2), F32)
    quarter = jax.ShapeDtypeStruct((rows, width // 4), F32)
    kept, sent = placed_call(project_kernel, "project", [half] * 2, place, pieces, w_out)
    other = swapped(sent, HEAD, 1)
    pair = placed_call(add_kernel, "pair_sum", half, place, kept, other)
    across = swapped(pair, HEAD, 2)
    resid_half = placed_call(
        residual_kernel,
        "residual",
        jax.ShapeDtypeStruct(half.shape, BF16),
        place,
        pair,
        across,
        latent,
    )
    resid, kept, sent = mlp(place, resid_half, swapped(resid_half, HEAD, 1), w_up, w_down)
    other = swapped(sent, HEAD, 1)
    kept, sent = placed_call(pair_kernel, "pair_shares", [quarter] * 2, place, kept, other)
    return placed_call(
        close_kernel,
        "close",
        jax.ShapeDtypeStruct(quarter.shape, BF16),
        place,
        resid,
        kept,
        swapped(sent, HEAD, 2),
    )


def solution(mesh):
    fine = Mesh(mesh.devices.reshape(4, 8, 2, 2, 2), SEQ + HEAD)
    placed = (
        P(SEQ, None),
        P(SEQ, None),
        P(None, HEAD),
        P(None, HEAD),
        P(None, HEAD),
        P(HEAD, None),
        P(None, HEAD),
        P(HEAD, None),
    )
    return jax.shard_map(
        on_device, mesh=fine, in_specs=placed, out_specs=P(SEQ, HEAD), check_vma=False
    )
```

```python
import functools

import jax
import jax.numpy as jnp
from jax import lax
from jax.experimental import pallas as pl
from jax.experimental.pallas import tpu as pltpu
from jax.sharding import Mesh
from jax.sharding import PartitionSpec as P

HEAD_DIM = 64
HEADS_HERE = 4
LEVEL_ROWS = 16
LANES = 128
SEQ = ("x", "z", "ylo")
HEAD = ("yhi", "core")
BF16 = jnp.bfloat16
F32 = jnp.float32
NT = (((1,), (1,)), ((), ()))
NN = (((1,), (0,)), ((), ()))
TN = (((0,), (0,)), ((), ()))


def product(left, right, numbers=NN):
    return lax.dot_general(left, right, numbers, preferred_element_type=F32)


def params(mib):
    return pltpu.CompilerParams(vmem_limit_bytes=mib * 2**20)


def norm_rows(widened):
    width = widened.shape[-1]
    row_mean = jnp.sum(widened, axis=-1, keepdims=True) / width
    row_square = jnp.sum(widened * widened, axis=-1, keepdims=True) / width
    row_var = row_square - row_mean * row_mean
    return (widened - row_mean) * lax.rsqrt(row_var + 1e-05)


def in_hbm(value):
    return pltpu.with_memory_space_constraint(value, pltpu.HBM)


def query_kernel(latent_hbm, w_hbm, out_ref, latent_ref, w_ref, sems):
    copies = [
        pltpu.make_async_copy(latent_hbm, latent_ref, sems.at[0]),
        pltpu.make_async_copy(w_hbm, w_ref, sems.at[1]),
    ]
    for copy in copies:
        copy.start()
    copies[0].wait()
    normed = norm_rows(latent_ref[...].astype(F32)).astype(BF16)
    copies[1].wait()
    out_ref[...] = (product(normed, w_ref[...]) * HEAD_DIM ** (-0.5)).astype(BF16)


def make_queries(latent, w_query):
    return pl.pallas_call(
        query_kernel,
        in_specs=[pl.BlockSpec(memory_space=pltpu.HBM)] * 2,
        out_shape=jax.ShapeDtypeStruct((latent.shape[0], w_query.shape[1]), BF16),
        scratch_shapes=[
            pltpu.VMEM(latent.shape, BF16),
            pltpu.VMEM(w_query.shape, BF16),
            pltpu.SemaphoreType.DMA((2,)),
        ],
        compiler_params=params(8),
        name="make_queries",
    )(in_hbm(latent), in_hbm(w_query))


def key_value_kernel(
    block, x_hbm, w_key_hbm, w_value_hbm, key_ref, value_ref, x_ref, w_key_ref, w_value_ref, sems
):
    tokens = x_ref.shape[0]
    weights = [
        pltpu.make_async_copy(w_key_hbm, w_key_ref, sems.at[0]),
        pltpu.make_async_copy(w_value_hbm, w_value_ref, sems.at[1]),
    ]
    spans = [slice(start, start + block) for start in range(0, tokens, block)]
    copies = [
        pltpu.make_async_copy(x_hbm.at[span], x_ref.at[span], sems.at[2 + i])
        for i, span in enumerate(spans)
    ]
    for copy in copies[:1] + weights + copies[1:]:
        copy.start()
    lane = lax.broadcasted_iota(jnp.int32, (block, LANES), 1)
    low = lane < HEAD_DIM
    copies[0].wait()
    following = norm_rows(x_ref[spans[0]].astype(F32)).astype(BF16)
    weights[0].wait()
    weights[1].wait()
    for i, span in enumerate(spans):
        normed = following
        if i + 1 < len(spans):
            copies[i + 1].wait()
            following = norm_rows(x_ref[spans[i + 1]].astype(F32)).astype(BF16)
        keys = product(normed, w_key_ref[...]).astype(BF16)
        vals = product(normed, w_value_ref[...])
        for head in range(HEADS_HERE):
            key_ref[head, span] = keys[:, head * HEAD_DIM : (head + 1) * HEAD_DIM]
            pair = vals[:, head // 2 * LANES : (head // 2 + 1) * LANES]
            one = jnp.where(lane == (HEAD_DIM if head % 2 == 0 else 0), 1.0, 0.0)
            kept = jnp.where(low, pair, one) if head % 2 == 0 else jnp.where(low, one, pair)
            value_ref[head, span] = kept.astype(BF16)


def make_keys_values(x, w_key, w_value):
    tokens = x.shape[0]
    block = 512
    return pl.pallas_call(
        functools.partial(key_value_kernel, block),
        in_specs=[pl.BlockSpec(memory_space=pltpu.HBM)] * 3,
        out_shape=[
            jax.ShapeDtypeStruct((HEADS_HERE, tokens, HEAD_DIM), BF16),
            jax.ShapeDtypeStruct((HEADS_HERE, tokens, LANES), BF16),
        ],
        scratch_shapes=[
            pltpu.VMEM(x.shape, BF16),
            pltpu.VMEM(w_key.shape, BF16),
            pltpu.VMEM(w_value.shape, BF16),
            pltpu.SemaphoreType.DMA((2 + tokens // block,)),
        ],
        compiler_params=params(16),
        name="make_keys_values",
    )(in_hbm(x), in_hbm(w_key), in_hbm(w_value))


def split_levels(levels, lane):
    first = levels.astype(BF16).astype(F32)
    rest = levels - first
    second = rest.astype(BF16).astype(F32)
    third = rest - second
    parts = jnp.where(lane < 4, first, jnp.where(lane < 8, second, third))
    return jnp.where(lane < 12, parts, 0.0)


def level_rows(rows):
    return rows // (2 * LANES) * LEVEL_ROWS


def block_places(refs, total_rows):
    block = 2 * LANES
    per_ref = total_rows // len(refs)
    return [
        (ref, start // block * (block + LEVEL_ROWS), i * per_ref + start)
        for i, ref in enumerate(refs)
        for start in range(0, per_ref, block)
    ]


def attend_kernel(spans, outs, fetched, *refs):
    count = len(spans)
    query_refs, (key_ref, value_ref) = refs[:count], refs[count : count + 2]
    out_refs = refs[count + 2 + fetched :][:outs]
    copies = []
    if fetched:
        sems = refs[-1]
        sources, kept = refs[count + 2 :][:fetched], refs[count + 2 + fetched + outs :][:fetched]
        for i, (source, target) in enumerate(zip(sources, kept)):
            copies.append(pltpu.make_async_copy(source, target, sems.at[i]))
    for copy in copies:
        copy.start()
    total_rows = sum(rows for _, rows in spans)
    block = 2 * LANES

    def scores_of(head):
        columns = slice(head * HEAD_DIM, (head + 1) * HEAD_DIM)
        parts = [
            ref[start : start + rows, columns] for ref, (start, rows) in zip(query_refs, spans)
        ]
        part = parts[0] if count == 1 else jnp.concatenate(parts, axis=0)
        return product(part, key_ref[head], NT)

    lane = lax.broadcasted_iota(jnp.int32, (total_rows, LANES), 1)
    levels = jnp.zeros((total_rows, LANES), F32)
    following = scores_of(0)
    even = None
    for head in range(HEADS_HERE):
        scores = following
        if head + 1 < HEADS_HERE:
            following = scores_of(head + 1)
        highest = jnp.max(scores, axis=1, keepdims=True)
        weights = jnp.exp(scores - highest).astype(BF16)
        accum = product(weights, value_ref[head])
        place = HEAD_DIM if head % 2 == 0 else 0
        total = accum[:, place : place + 1]
        mean = accum * (1.0 / total)
        levels = jnp.where(lane % 4 == head, highest + jnp.log(total), levels)
        if head % 2 == 0:
            even = mean
        else:
            both = jnp.where(lane < HEAD_DIM, even, mean).astype(BF16)
            columns = slice(head // 2 * LANES, (head // 2 + 1) * LANES)
            for ref, place, start in block_places(out_refs, total_rows):
                ref[place : place + block, columns] = both[start : start + block]
    packed = jnp.transpose(split_levels(levels, lane))[:LEVEL_ROWS].astype(BF16)
    for ref, place, start in block_places(out_refs, total_rows):
        ref[place + block : place + block + LEVEL_ROWS] = packed[:, start : start + block]
    for copy in copies:
        copy.wait()


def attend(chunks, outs, keys, values, fetched=()):
    spans = tuple((start, rows) for _, start, rows in chunks)
    rows = sum(rows for _, rows in spans) // outs
    out = jax.ShapeDtypeStruct((rows + level_rows(rows), 2 * LANES), BF16)
    vmem, hbm = pl.BlockSpec(memory_space=pltpu.VMEM), pl.BlockSpec(memory_space=pltpu.HBM)
    return pl.pallas_call(
        functools.partial(attend_kernel, spans, outs, len(fetched)),
        in_specs=[vmem] * (len(chunks) + 2) + [hbm] * len(fetched),
        out_shape=[out] * outs + [jax.ShapeDtypeStruct(w.shape, BF16) for w in fetched],
        scratch_shapes=[pltpu.SemaphoreType.DMA((len(fetched),))] if fetched else [],
        compiler_params=params(24),
        name="attend",
    )(*[chunk for chunk, _, _ in chunks], keys, values, *[in_hbm(w) for w in fetched])


def spread_matrix(count):
    source = lax.broadcasted_iota(jnp.int32, (count, 2 * LANES), 0)
    target = lax.broadcasted_iota(jnp.int32, (count, 2 * LANES), 1)
    hit = (source < 12) & (source % 4 == target // HEAD_DIM)
    return jnp.where(hit, 1.0, 0.0).astype(BF16)


def side_levels(piece):
    return piece[:, : 2 * LANES], product(piece[:, 2 * LANES :], spread_matrix(LANES))


def under_levels(piece):
    block = 2 * LANES
    spread = spread_matrix(LEVEL_ROWS)
    means, levels = [], []
    for start in range(0, piece.shape[0], block + LEVEL_ROWS):
        means.append(piece[start : start + block])
        parts = piece[start + block : start + block + LEVEL_ROWS]
        levels.append(product(parts, spread, TN))
    return jnp.concatenate(means, axis=0), jnp.concatenate(levels, axis=0)


def merged(pieces, read):
    means, levels = zip(*[read(piece) for piece in pieces])
    highest = functools.reduce(jnp.maximum, levels)
    total, accum = None, None
    for mean, level in zip(means, levels):
        factor = jnp.exp(level - highest)
        term = factor * mean.astype(F32)
        total = factor if total is None else total + factor
        accum = term if accum is None else accum + term
    return accum / total, highest, total


def merge_kernel(count, write, *refs):
    out_refs = refs[count:]
    mean, highest, total = merged([ref[...] for ref in refs[:count]], under_levels)
    levels = highest + jnp.log(total)
    lane = lax.broadcasted_iota(jnp.int32, (levels.shape[0], LANES), 1)
    one, two = levels[:, :LANES], levels[:, LANES:]
    one_other, two_other = pltpu.roll(one, HEAD_DIM, 1), pltpu.roll(two, HEAD_DIM, 1)
    head = lane % 4
    picked = jnp.where(
        head == 0, one, jnp.where(head == 1, one_other, jnp.where(head == 2, two, two_other))
    )
    write(out_refs, mean.astype(BF16), split_levels(picked, lane))


def write_halves(refs, mean, parts):
    block = 2 * LANES
    turned = jnp.transpose(parts)[:LEVEL_ROWS].astype(BF16)
    for ref, place, start in block_places(refs, mean.shape[0]):
        ref[place : place + block] = mean[start : start + block]
        ref[place + block : place + block + LEVEL_ROWS] = turned[:, start : start + block]


def write_blocks(refs, mean, parts):
    count, rows, _ = refs[0].shape
    parts = parts.astype(BF16)
    for i in range(count):
        refs[0][i, :, : 2 * LANES] = mean[i * rows : (i + 1) * rows]
        refs[0][i, :, 2 * LANES :] = parts[i * rows : (i + 1) * rows]


def merge(pieces, write, shapes):
    return pl.pallas_call(
        functools.partial(merge_kernel, len(pieces), write),
        out_shape=[jax.ShapeDtypeStruct(shape, BF16) for shape in shapes],
        compiler_params=params(24),
        name="merge",
    )(*pieces)


def placed_call(kernel, name, out_shape, place, *operands):
    return pl.pallas_call(
        kernel,
        in_specs=[pl.BlockSpec(memory_space=pltpu.SMEM)]
        + [pl.BlockSpec(memory_space=pltpu.VMEM)] * len(operands),
        out_shape=out_shape,
        compiler_params=params(8),
        name=name,
    )(place, *operands)


def ordered(place_ref, low, high):
    first = place_ref[0] % 2 == 0
    return jnp.where(first, low, high), jnp.where(first, high, low)


def project_kernel(place_ref, pieces_ref, w_ref, kept_ref, sent_ref):
    pieces = [pieces_ref[i] for i in range(pieces_ref.shape[0])]
    mean, highest, total = merged(pieces, side_levels)
    projected = product(mean.astype(BF16), w_ref[...])
    columns = kept_ref.shape[1]
    halves = ordered(place_ref, projected[:, :columns], projected[:, columns:])
    kept_ref[...], sent_ref[...] = halves


def add_kernel(place_ref, kept_ref, other_ref, out_ref):
    out_ref[...] = kept_ref[...] + other_ref[...]


def residual_kernel(place_ref, one_ref, two_ref, latent_ref, out_ref):
    columns = out_ref.shape[1]
    own = latent_ref[:, pl.ds(pl.multiple_of(place_ref[0] % 2 * columns, LANES), columns)]
    out_ref[...] = (own.astype(F32) + (one_ref[...] + two_ref[...])).astype(BF16)


def mlp_kernel(
    place_ref,
    own_ref,
    other_ref,
    w_up_ref,
    w_down_hbm,
    resid_ref,
    kept_ref,
    sent_ref,
    w_down_ref,
    sem,
):
    copy = pltpu.make_async_copy(w_down_hbm, w_down_ref, sem)
    copy.start()
    columns = resid_ref.shape[2]
    halves = ordered(place_ref, own_ref[...], other_ref[...])
    residual = jnp.concatenate(halves, axis=1)
    normed = norm_rows(residual.astype(F32)).astype(BF16)
    raised = product(normed, w_up_ref[...])
    hidden = (0.5 * raised * (1.0 + lax.erf(raised * 0.5**0.5))).astype(BF16)
    copy.wait()
    share = product(hidden, w_down_ref[...]).astype(BF16)
    blocks = [share[:, i * columns : (i + 1) * columns] for i in range(4)]
    for i in range(4):
        resid_ref[i] = residual[:, i * columns : (i + 1) * columns]
    for high in range(2):
        pair = ordered(place_ref, blocks[2 * high], blocks[2 * high + 1])
        kept_ref[high], sent_ref[high] = pair


def mlp(place, own, other, w_up, w_down):
    rows, half = own.shape
    vmem, hbm = pl.BlockSpec(memory_space=pltpu.VMEM), pl.BlockSpec(memory_space=pltpu.HBM)
    return pl.pallas_call(
        mlp_kernel,
        in_specs=[pl.BlockSpec(memory_space=pltpu.SMEM), vmem, vmem, vmem, hbm],
        out_shape=[
            jax.ShapeDtypeStruct((4, rows, half // 2), BF16),
        ]
        + [jax.ShapeDtypeStruct((2, rows, half // 2), BF16)] * 2,
        scratch_shapes=[pltpu.VMEM(w_down.shape, BF16), pltpu.SemaphoreType.DMA],
        compiler_params=params(16),
        name="mlp",
    )(place, own, other, w_up, in_hbm(w_down))


def pair_kernel(place_ref, shares_ref, other_ref, kept_ref, sent_ref):
    high = place_ref[0] // 2
    for ref, index in ((kept_ref, high), (sent_ref, 1 - high)):
        ref[...] = shares_ref[index].astype(F32) + other_ref[index].astype(F32)


def close_kernel(place_ref, resid_ref, kept_ref, other_ref, out_ref):
    own = resid_ref[place_ref[0]]
    out_ref[...] = (own.astype(F32) + (kept_ref[...] + other_ref[...])).astype(BF16)


def along(value, axis, by):
    size = lax.axis_size(axis)
    return lax.ppermute(value, axis, [(i, (i + by) % size) for i in range(size)])


def swapped(value, axes, bits):
    size = lax.axis_size(axes)
    return lax.ppermute(value, axes, [(i, i ^ bits) for i in range(size)])


STEPS = (2, 1, 3)


def on_device(inputs, latent, w_query, w_key, w_value, w_out, w_up, w_down):
    queries = make_queries(latent, w_query)
    rows, columns = queries.shape
    count = lax.axis_size("z")
    spread = jnp.broadcast_to(queries[None], (count,) + queries.shape)
    part = lax.all_to_all(spread, "z", 0, 0, tiled=True).reshape(count * rows, columns)
    size = count * rows
    two, one, three = [along(part, "x", by) for by in STEPS]
    inputs, part = lax.optimization_barrier((inputs, part))
    keys, values = make_keys_values(inputs, w_key, w_value)
    keys, first = lax.optimization_barrier((keys, jnp.concatenate([two, one], axis=0)))
    first_pair = swapped(first, "ylo", 1)
    own_side = attend([(first, 0, 2 * size)], 2, keys, values)
    own_side, three, part = lax.optimization_barrier((own_side, three, part))
    second = jnp.concatenate([three, part], axis=0)
    second_pair = swapped(second, "ylo", 1)
    pair_side = attend([(first_pair, 0, 2 * size)], 2, keys, values)
    pair_side, second_pair = lax.optimization_barrier((pair_side, second_pair))
    pieces = [
        along(jnp.concatenate(sides, axis=0), "x", -by)
        for by, sides in zip(STEPS, zip(own_side, pair_side))
    ]
    chunks = [(second, 0, size), (second_pair, 0, size)]
    pieces.append(along(attend(chunks, 1, keys, values)[0], "x", -STEPS[2]))
    chunks = [(second, size, size), (second_pair, size, size)]
    piece, w_up = attend(chunks, 1, keys, values, (w_up,))
    pieces.append(piece)
    half = (count * rows + level_rows(count * rows), columns)
    own, others = merge(pieces, write_halves, [half] * 2)
    block = merge([own, swapped(others, "ylo", 1)], write_blocks, [(count, rows, 3 * LANES)])[0]
    place = lax.axis_index(HEAD).astype(jnp.int32).reshape(1)
    block, place = lax.optimization_barrier((block, place))
    pieces = lax.all_to_all(block, "z", 0, 0, tiled=True)
    width = latent.shape[1]
    half = jax.ShapeDtypeStruct((rows, width // 2), F32)
    quarter = jax.ShapeDtypeStruct((rows, width // 4), F32)
    kept, sent = placed_call(project_kernel, "project", [half] * 2, place, pieces, w_out)
    other = swapped(sent, HEAD, 1)
    pair = placed_call(add_kernel, "pair_sum", half, place, kept, other)
    across = swapped(pair, HEAD, 2)
    resid_half = placed_call(
        residual_kernel,
        "residual",
        jax.ShapeDtypeStruct(half.shape, BF16),
        place,
        pair,
        across,
        latent,
    )
    resid, kept, sent = mlp(place, resid_half, swapped(resid_half, HEAD, 1), w_up, w_down)
    other = swapped(sent, HEAD, 1)
    kept, sent = placed_call(pair_kernel, "pair_shares", [quarter] * 2, place, kept, other)
    return placed_call(
        close_kernel,
        "close",
        jax.ShapeDtypeStruct(quarter.shape, BF16),
        place,
        resid,
        kept,
        swapped(sent, HEAD, 2),
    )


def solution(mesh):
    fine = Mesh(mesh.devices.reshape(4, 8, 2, 2, 2), SEQ + HEAD)
    placed = (
        P(SEQ, None),
        P(SEQ, None),
        P(None, HEAD),
        P(None, HEAD),
        P(None, HEAD),
        P(HEAD, None),
        P(None, HEAD),
        P(HEAD, None),
    )
    return jax.shard_map(
        on_device, mesh=fine, in_specs=placed, out_specs=P(SEQ, HEAD), check_vma=False
    )
```

```python
import functools

import jax
import jax.numpy as jnp
from jax import lax
from jax.experimental import pallas as pl
from jax.experimental.pallas import tpu as pltpu
from jax.sharding import Mesh
from jax.sharding import PartitionSpec as P

HEAD_DIM = 64
HEADS_HERE = 4
LEVEL_ROWS = 16
LANES = 128
SEQ = ("x", "z", "ylo")
HEAD = ("yhi", "core")
BF16 = jnp.bfloat16
F32 = jnp.float32
NT = (((1,), (1,)), ((), ()))
NN = (((1,), (0,)), ((), ()))
TN = (((0,), (0,)), ((), ()))


def product(left, right, numbers=NN):
    return lax.dot_general(left, right, numbers, preferred_element_type=F32)


def params(mib):
    return pltpu.CompilerParams(vmem_limit_bytes=mib * 2**20)


def norm_rows(widened):
    width = widened.shape[-1]
    row_mean = jnp.sum(widened, axis=-1, keepdims=True) / width
    row_square = jnp.sum(widened * widened, axis=-1, keepdims=True) / width
    row_var = row_square - row_mean * row_mean
    return (widened - row_mean) * lax.rsqrt(row_var + 1e-05)


def in_hbm(value):
    return pltpu.with_memory_space_constraint(value, pltpu.HBM)


def query_kernel(latent_hbm, w_hbm, out_ref, latent_ref, w_ref, sems):
    copies = [
        pltpu.make_async_copy(latent_hbm, latent_ref, sems.at[0]),
        pltpu.make_async_copy(w_hbm, w_ref, sems.at[1]),
    ]
    for copy in copies:
        copy.start()
    copies[0].wait()
    normed = norm_rows(latent_ref[...].astype(F32)).astype(BF16)
    copies[1].wait()
    out_ref[...] = (product(normed, w_ref[...]) * HEAD_DIM ** (-0.5)).astype(BF16)


def make_queries(latent, w_query):
    return pl.pallas_call(
        query_kernel,
        in_specs=[pl.BlockSpec(memory_space=pltpu.HBM)] * 2,
        out_shape=jax.ShapeDtypeStruct((latent.shape[0], w_query.shape[1]), BF16),
        scratch_shapes=[
            pltpu.VMEM(latent.shape, BF16),
            pltpu.VMEM(w_query.shape, BF16),
            pltpu.SemaphoreType.DMA((2,)),
        ],
        compiler_params=params(8),
        name="make_queries",
    )(in_hbm(latent), in_hbm(w_query))


def key_value_kernel(
    block, x_hbm, w_key_hbm, w_value_hbm, key_ref, value_ref, x_ref, w_key_ref, w_value_ref, sems
):
    tokens = x_ref.shape[0]
    weights = [
        pltpu.make_async_copy(w_key_hbm, w_key_ref, sems.at[0]),
        pltpu.make_async_copy(w_value_hbm, w_value_ref, sems.at[1]),
    ]
    spans = [slice(start, start + block) for start in range(0, tokens, block)]
    copies = [
        pltpu.make_async_copy(x_hbm.at[span], x_ref.at[span], sems.at[2 + i])
        for i, span in enumerate(spans)
    ]
    for copy in copies[:1] + weights + copies[1:]:
        copy.start()
    lane = lax.broadcasted_iota(jnp.int32, (block, LANES), 1)
    low = lane < HEAD_DIM
    copies[0].wait()
    following = norm_rows(x_ref[spans[0]].astype(F32)).astype(BF16)
    weights[0].wait()
    weights[1].wait()
    for i, span in enumerate(spans):
        normed = following
        if i + 1 < len(spans):
            copies[i + 1].wait()
            following = norm_rows(x_ref[spans[i + 1]].astype(F32)).astype(BF16)
        keys = product(normed, w_key_ref[...]).astype(BF16)
        vals = product(normed, w_value_ref[...])
        for head in range(HEADS_HERE):
            key_ref[head, span] = keys[:, head * HEAD_DIM : (head + 1) * HEAD_DIM]
            pair = vals[:, head // 2 * LANES : (head // 2 + 1) * LANES]
            one = jnp.where(lane == (HEAD_DIM if head % 2 == 0 else 0), 1.0, 0.0)
            kept = jnp.where(low, pair, one) if head % 2 == 0 else jnp.where(low, one, pair)
            value_ref[head, span] = kept.astype(BF16)


def make_keys_values(x, w_key, w_value):
    tokens = x.shape[0]
    block = 1024
    return pl.pallas_call(
        functools.partial(key_value_kernel, block),
        in_specs=[pl.BlockSpec(memory_space=pltpu.HBM)] * 3,
        out_shape=[
            jax.ShapeDtypeStruct((HEADS_HERE, tokens, HEAD_DIM), BF16),
            jax.ShapeDtypeStruct((HEADS_HERE, tokens, LANES), BF16),
        ],
        scratch_shapes=[
            pltpu.VMEM(x.shape, BF16),
            pltpu.VMEM(w_key.shape, BF16),
            pltpu.VMEM(w_value.shape, BF16),
            pltpu.SemaphoreType.DMA((2 + tokens // block,)),
        ],
        compiler_params=params(24),
        name="make_keys_values",
    )(in_hbm(x), in_hbm(w_key), in_hbm(w_value))


def split_levels(levels, lane):
    first = levels.astype(BF16).astype(F32)
    rest = levels - first
    second = rest.astype(BF16).astype(F32)
    third = rest - second
    parts = jnp.where(lane < 4, first, jnp.where(lane < 8, second, third))
    return jnp.where(lane < 12, parts, 0.0)


def level_rows(rows):
    return rows // (2 * LANES) * LEVEL_ROWS


def block_places(refs, total_rows):
    block = 2 * LANES
    per_ref = total_rows // len(refs)
    return [
        (ref, start // block * (block + LEVEL_ROWS), i * per_ref + start)
        for i, ref in enumerate(refs)
        for start in range(0, per_ref, block)
    ]


def attend_kernel(spans, outs, fetched, *refs):
    count = len(spans)
    query_refs, (key_ref, value_ref) = refs[:count], refs[count : count + 2]
    out_refs = refs[count + 2 + fetched :][:outs]
    copies = []
    if fetched:
        sems = refs[-1]
        sources, kept = refs[count + 2 :][:fetched], refs[count + 2 + fetched + outs :][:fetched]
        for i, (source, target) in enumerate(zip(sources, kept)):
            copies.append(pltpu.make_async_copy(source, target, sems.at[i]))
    for copy in copies:
        copy.start()
    total_rows = sum(rows for _, rows in spans)
    block = 2 * LANES

    def scores_of(head):
        columns = slice(head * HEAD_DIM, (head + 1) * HEAD_DIM)
        parts = [
            ref[start : start + rows, columns] for ref, (start, rows) in zip(query_refs, spans)
        ]
        part = parts[0] if count == 1 else jnp.concatenate(parts, axis=0)
        return product(part, key_ref[head], NT)

    lane = lax.broadcasted_iota(jnp.int32, (total_rows, LANES), 1)
    levels = jnp.zeros((total_rows, LANES), F32)
    following = scores_of(0)
    even = None
    for head in range(HEADS_HERE):
        scores = following
        if head + 1 < HEADS_HERE:
            following = scores_of(head + 1)
        highest = jnp.max(scores, axis=1, keepdims=True)
        weights = jnp.exp(scores - highest).astype(BF16)
        accum = product(weights, value_ref[head])
        place = HEAD_DIM if head % 2 == 0 else 0
        total = accum[:, place : place + 1]
        mean = accum * (1.0 / total)
        levels = jnp.where(lane % 4 == head, highest + jnp.log(total), levels)
        if head % 2 == 0:
            even = mean
        else:
            both = jnp.where(lane < HEAD_DIM, even, mean).astype(BF16)
            columns = slice(head // 2 * LANES, (head // 2 + 1) * LANES)
            for ref, place, start in block_places(out_refs, total_rows):
                ref[place : place + block, columns] = both[start : start + block]
    packed = jnp.transpose(split_levels(levels, lane))[:LEVEL_ROWS].astype(BF16)
    for ref, place, start in block_places(out_refs, total_rows):
        ref[place + block : place + block + LEVEL_ROWS] = packed[:, start : start + block]
    for copy in copies:
        copy.wait()


def attend(chunks, outs, keys, values, fetched=()):
    spans = tuple((start, rows) for _, start, rows in chunks)
    rows = sum(rows for _, rows in spans) // outs
    out = jax.ShapeDtypeStruct((rows + level_rows(rows), 2 * LANES), BF16)
    vmem, hbm = pl.BlockSpec(memory_space=pltpu.VMEM), pl.BlockSpec(memory_space=pltpu.HBM)
    return pl.pallas_call(
        functools.partial(attend_kernel, spans, outs, len(fetched)),
        in_specs=[vmem] * (len(chunks) + 2) + [hbm] * len(fetched),
        out_shape=[out] * outs + [jax.ShapeDtypeStruct(w.shape, BF16) for w in fetched],
        scratch_shapes=[pltpu.SemaphoreType.DMA((len(fetched),))] if fetched else [],
        compiler_params=params(24),
        name="attend",
    )(*[chunk for chunk, _, _ in chunks], keys, values, *[in_hbm(w) for w in fetched])


def spread_matrix(count):
    source = lax.broadcasted_iota(jnp.int32, (count, 2 * LANES), 0)
    target = lax.broadcasted_iota(jnp.int32, (count, 2 * LANES), 1)
    hit = (source < 12) & (source % 4 == target // HEAD_DIM)
    return jnp.where(hit, 1.0, 0.0).astype(BF16)


def side_levels(piece):
    return piece[:, : 2 * LANES], product(piece[:, 2 * LANES :], spread_matrix(LANES))


def under_levels(piece):
    block = 2 * LANES
    spread = spread_matrix(LEVEL_ROWS)
    means, levels = [], []
    for start in range(0, piece.shape[0], block + LEVEL_ROWS):
        means.append(piece[start : start + block])
        parts = piece[start + block : start + block + LEVEL_ROWS]
        levels.append(product(parts, spread, TN))
    return jnp.concatenate(means, axis=0), jnp.concatenate(levels, axis=0)


def merged(pieces, read):
    means, levels = zip(*[read(piece) for piece in pieces])
    highest = functools.reduce(jnp.maximum, levels)
    total, accum = None, None
    for mean, level in zip(means, levels):
        factor = jnp.exp(level - highest)
        term = factor * mean.astype(F32)
        total = factor if total is None else total + factor
        accum = term if accum is None else accum + term
    return accum / total, highest, total


def merge_kernel(count, write, *refs):
    out_refs = refs[count:]
    mean, highest, total = merged([ref[...] for ref in refs[:count]], under_levels)
    levels = highest + jnp.log(total)
    lane = lax.broadcasted_iota(jnp.int32, (levels.shape[0], LANES), 1)
    one, two = levels[:, :LANES], levels[:, LANES:]
    one_other, two_other = pltpu.roll(one, HEAD_DIM, 1), pltpu.roll(two, HEAD_DIM, 1)
    head = lane % 4
    picked = jnp.where(
        head == 0, one, jnp.where(head == 1, one_other, jnp.where(head == 2, two, two_other))
    )
    write(out_refs, mean.astype(BF16), split_levels(picked, lane))


def write_halves(refs, mean, parts):
    block = 2 * LANES
    turned = jnp.transpose(parts)[:LEVEL_ROWS].astype(BF16)
    for ref, place, start in block_places(refs, mean.shape[0]):
        ref[place : place + block] = mean[start : start + block]
        ref[place + block : place + block + LEVEL_ROWS] = turned[:, start : start + block]


def write_blocks(refs, mean, parts):
    count, rows, _ = refs[0].shape
    parts = parts.astype(BF16)
    for i in range(count):
        refs[0][i, :, : 2 * LANES] = mean[i * rows : (i + 1) * rows]
        refs[0][i, :, 2 * LANES :] = parts[i * rows : (i + 1) * rows]


def merge(pieces, write, shapes):
    return pl.pallas_call(
        functools.partial(merge_kernel, len(pieces), write),
        out_shape=[jax.ShapeDtypeStruct(shape, BF16) for shape in shapes],
        compiler_params=params(24),
        name="merge",
    )(*pieces)


def placed_call(kernel, name, out_shape, place, *operands):
    return pl.pallas_call(
        kernel,
        in_specs=[pl.BlockSpec(memory_space=pltpu.SMEM)]
        + [pl.BlockSpec(memory_space=pltpu.VMEM)] * len(operands),
        out_shape=out_shape,
        compiler_params=params(8),
        name=name,
    )(place, *operands)


def ordered(place_ref, low, high):
    first = place_ref[0] % 2 == 0
    return jnp.where(first, low, high), jnp.where(first, high, low)


def project_kernel(place_ref, pieces_ref, w_ref, kept_ref, sent_ref):
    pieces = [pieces_ref[i] for i in range(pieces_ref.shape[0])]
    mean, highest, total = merged(pieces, side_levels)
    projected = product(mean.astype(BF16), w_ref[...])
    columns = kept_ref.shape[1]
    halves = ordered(place_ref, projected[:, :columns], projected[:, columns:])
    kept_ref[...], sent_ref[...] = halves


def add_kernel(place_ref, kept_ref, other_ref, out_ref):
    out_ref[...] = kept_ref[...] + other_ref[...]


def residual_kernel(place_ref, one_ref, two_ref, latent_ref, out_ref):
    columns = out_ref.shape[1]
    own = latent_ref[:, pl.ds(pl.multiple_of(place_ref[0] % 2 * columns, LANES), columns)]
    out_ref[...] = (own.astype(F32) + (one_ref[...] + two_ref[...])).astype(BF16)


def mlp_kernel(
    place_ref,
    own_ref,
    other_ref,
    w_up_ref,
    w_down_hbm,
    resid_ref,
    kept_ref,
    sent_ref,
    w_down_ref,
    sem,
):
    copy = pltpu.make_async_copy(w_down_hbm, w_down_ref, sem)
    copy.start()
    columns = resid_ref.shape[2]
    halves = ordered(place_ref, own_ref[...], other_ref[...])
    residual = jnp.concatenate(halves, axis=1)
    normed = norm_rows(residual.astype(F32)).astype(BF16)
    raised = product(normed, w_up_ref[...])
    hidden = (0.5 * raised * (1.0 + lax.erf(raised * 0.5**0.5))).astype(BF16)
    copy.wait()
    share = product(hidden, w_down_ref[...]).astype(BF16)
    blocks = [share[:, i * columns : (i + 1) * columns] for i in range(4)]
    for i in range(4):
        resid_ref[i] = residual[:, i * columns : (i + 1) * columns]
    for high in range(2):
        pair = ordered(place_ref, blocks[2 * high], blocks[2 * high + 1])
        kept_ref[high], sent_ref[high] = pair


def mlp(place, own, other, w_up, w_down):
    rows, half = own.shape
    vmem, hbm = pl.BlockSpec(memory_space=pltpu.VMEM), pl.BlockSpec(memory_space=pltpu.HBM)
    return pl.pallas_call(
        mlp_kernel,
        in_specs=[pl.BlockSpec(memory_space=pltpu.SMEM), vmem, vmem, vmem, hbm],
        out_shape=[
            jax.ShapeDtypeStruct((4, rows, half // 2), BF16),
        ]
        + [jax.ShapeDtypeStruct((2, rows, half // 2), BF16)] * 2,
        scratch_shapes=[pltpu.VMEM(w_down.shape, BF16), pltpu.SemaphoreType.DMA],
        compiler_params=params(16),
        name="mlp",
    )(place, own, other, w_up, in_hbm(w_down))


def pair_kernel(place_ref, shares_ref, other_ref, kept_ref, sent_ref):
    high = place_ref[0] // 2
    for ref, index in ((kept_ref, high), (sent_ref, 1 - high)):
        ref[...] = shares_ref[index].astype(F32) + other_ref[index].astype(F32)


def close_kernel(place_ref, resid_ref, kept_ref, other_ref, out_ref):
    own = resid_ref[place_ref[0]]
    out_ref[...] = (own.astype(F32) + (kept_ref[...] + other_ref[...])).astype(BF16)


def along(value, axis, by):
    size = lax.axis_size(axis)
    return lax.ppermute(value, axis, [(i, (i + by) % size) for i in range(size)])


def swapped(value, axes, bits):
    size = lax.axis_size(axes)
    return lax.ppermute(value, axes, [(i, i ^ bits) for i in range(size)])


STEPS = (2, 1, 3)


def on_device(inputs, latent, w_query, w_key, w_value, w_out, w_up, w_down):
    queries = make_queries(latent, w_query)
    rows, columns = queries.shape
    count = lax.axis_size("z")
    spread = jnp.broadcast_to(queries[None], (count,) + queries.shape)
    part = lax.all_to_all(spread, "z", 0, 0, tiled=True).reshape(count * rows, columns)
    size = count * rows
    two, one, three = [along(part, "x", by) for by in STEPS]
    inputs, part = lax.optimization_barrier((inputs, part))
    keys, values = make_keys_values(inputs, w_key, w_value)
    keys, first = lax.optimization_barrier((keys, jnp.concatenate([two, one], axis=0)))
    first_pair = swapped(first, "ylo", 1)
    own_side = attend([(first, 0, 2 * size)], 2, keys, values)
    own_side, three, part = lax.optimization_barrier((own_side, three, part))
    second = jnp.concatenate([three, part], axis=0)
    second_pair = swapped(second, "ylo", 1)
    side = attend([(first_pair, 0, size)], 1, keys, values)[0]
    pieces = [along(jnp.concatenate([own_side[0], side], axis=0), "x", -STEPS[0])]
    side, first_pair = lax.optimization_barrier((side, first_pair))
    side = attend([(first_pair, size, size)], 1, keys, values)[0]
    side, second_pair = lax.optimization_barrier((side, second_pair))
    pieces.append(along(jnp.concatenate([own_side[1], side], axis=0), "x", -STEPS[1]))
    chunks = [(second, 0, size), (second_pair, 0, size)]
    pieces.append(along(attend(chunks, 1, keys, values)[0], "x", -STEPS[2]))
    chunks = [(second, size, size), (second_pair, size, size)]
    piece, w_up = attend(chunks, 1, keys, values, (w_up,))
    pieces.append(piece)
    half = (count * rows + level_rows(count * rows), columns)
    own, others = merge(pieces, write_halves, [half] * 2)
    block = merge([own, swapped(others, "ylo", 1)], write_blocks, [(count, rows, 3 * LANES)])[0]
    place = lax.axis_index(HEAD).astype(jnp.int32).reshape(1)
    block, place = lax.optimization_barrier((block, place))
    pieces = lax.all_to_all(block, "z", 0, 0, tiled=True)
    width = latent.shape[1]
    half = jax.ShapeDtypeStruct((rows, width // 2), F32)
    quarter = jax.ShapeDtypeStruct((rows, width // 4), F32)
    kept, sent = placed_call(project_kernel, "project", [half] * 2, place, pieces, w_out)
    other = swapped(sent, HEAD, 1)
    pair = placed_call(add_kernel, "pair_sum", half, place, kept, other)
    across = swapped(pair, HEAD, 2)
    resid_half = placed_call(
        residual_kernel,
        "residual",
        jax.ShapeDtypeStruct(half.shape, BF16),
        place,
        pair,
        across,
        latent,
    )
    resid, kept, sent = mlp(place, resid_half, swapped(resid_half, HEAD, 1), w_up, w_down)
    other = swapped(sent, HEAD, 1)
    kept, sent = placed_call(pair_kernel, "pair_shares", [quarter] * 2, place, kept, other)
    return placed_call(
        close_kernel,
        "close",
        jax.ShapeDtypeStruct(quarter.shape, BF16),
        place,
        resid,
        kept,
        swapped(sent, HEAD, 2),
    )


def solution(mesh):
    fine = Mesh(mesh.devices.reshape(4, 8, 2, 2, 2), SEQ + HEAD)
    placed = (
        P(SEQ, None),
        P(SEQ, None),
        P(None, HEAD),
        P(None, HEAD),
        P(None, HEAD),
        P(HEAD, None),
        P(None, HEAD),
        P(HEAD, None),
    )
    return jax.shard_map(
        on_device, mesh=fine, in_specs=placed, out_specs=P(SEQ, HEAD), check_vma=False
    )
```

```python
import functools

import jax
import jax.numpy as jnp
from jax import lax
from jax.experimental import pallas as pl
from jax.experimental.pallas import tpu as pltpu
from jax.sharding import Mesh
from jax.sharding import PartitionSpec as P

HEAD_DIM = 64
HEADS_HERE = 4
LEVEL_ROWS = 16
LANES = 128
SEQ = ("x", "z", "ylo")
HEAD = ("yhi", "core")
BF16 = jnp.bfloat16
F32 = jnp.float32
NT = (((1,), (1,)), ((), ()))
NN = (((1,), (0,)), ((), ()))
TN = (((0,), (0,)), ((), ()))


def product(left, right, numbers=NN):
    return lax.dot_general(left, right, numbers, preferred_element_type=F32)


def params(mib):
    return pltpu.CompilerParams(vmem_limit_bytes=mib * 2**20)


def norm_rows(widened):
    width = widened.shape[-1]
    row_mean = jnp.sum(widened, axis=-1, keepdims=True) / width
    row_square = jnp.sum(widened * widened, axis=-1, keepdims=True) / width
    row_var = row_square - row_mean * row_mean
    return (widened - row_mean) * lax.rsqrt(row_var + 1e-05)


def in_hbm(value):
    return pltpu.with_memory_space_constraint(value, pltpu.HBM)


def query_kernel(latent_hbm, w_hbm, out_ref, latent_ref, w_ref, sems):
    copies = [
        pltpu.make_async_copy(latent_hbm, latent_ref, sems.at[0]),
        pltpu.make_async_copy(w_hbm, w_ref, sems.at[1]),
    ]
    for copy in copies:
        copy.start()
    copies[0].wait()
    normed = norm_rows(latent_ref[...].astype(F32)).astype(BF16)
    copies[1].wait()
    out_ref[...] = (product(normed, w_ref[...]) * HEAD_DIM ** (-0.5)).astype(BF16)


def make_queries(latent, w_query):
    return pl.pallas_call(
        query_kernel,
        in_specs=[pl.BlockSpec(memory_space=pltpu.HBM)] * 2,
        out_shape=jax.ShapeDtypeStruct((latent.shape[0], w_query.shape[1]), BF16),
        scratch_shapes=[
            pltpu.VMEM(latent.shape, BF16),
            pltpu.VMEM(w_query.shape, BF16),
            pltpu.SemaphoreType.DMA((2,)),
        ],
        compiler_params=params(8),
        name="make_queries",
    )(in_hbm(latent), in_hbm(w_query))


def key_value_kernel(
    block, x_hbm, w_key_hbm, w_value_hbm, key_ref, value_ref, x_ref, w_key_ref, w_value_ref, sems
):
    tokens = x_ref.shape[0]
    weights = [
        pltpu.make_async_copy(w_key_hbm, w_key_ref, sems.at[0]),
        pltpu.make_async_copy(w_value_hbm, w_value_ref, sems.at[1]),
    ]
    spans = [slice(start, start + block) for start in range(0, tokens, block)]
    copies = [
        pltpu.make_async_copy(x_hbm.at[span], x_ref.at[span], sems.at[2 + i])
        for i, span in enumerate(spans)
    ]
    for copy in copies[:1] + weights + copies[1:]:
        copy.start()
    lane = lax.broadcasted_iota(jnp.int32, (block, LANES), 1)
    low = lane < HEAD_DIM
    copies[0].wait()
    following = norm_rows(x_ref[spans[0]].astype(F32)).astype(BF16)
    weights[0].wait()
    weights[1].wait()
    for i, span in enumerate(spans):
        normed = following
        if i + 1 < len(spans):
            copies[i + 1].wait()
            following = norm_rows(x_ref[spans[i + 1]].astype(F32)).astype(BF16)
        keys = product(normed, w_key_ref[...]).astype(BF16)
        vals = product(normed, w_value_ref[...])
        for head in range(HEADS_HERE):
            key_ref[head, span] = keys[:, head * HEAD_DIM : (head + 1) * HEAD_DIM]
            pair = vals[:, head // 2 * LANES : (head // 2 + 1) * LANES]
            one = jnp.where(lane == (HEAD_DIM if head % 2 == 0 else 0), 1.0, 0.0)
            kept = jnp.where(low, pair, one) if head % 2 == 0 else jnp.where(low, one, pair)
            value_ref[head, span] = kept.astype(BF16)


def make_keys_values(x, w_key, w_value):
    tokens = x.shape[0]
    block = 1024
    return pl.pallas_call(
        functools.partial(key_value_kernel, block),
        in_specs=[pl.BlockSpec(memory_space=pltpu.HBM)] * 3,
        out_shape=[
            jax.ShapeDtypeStruct((HEADS_HERE, tokens, HEAD_DIM), BF16),
            jax.ShapeDtypeStruct((HEADS_HERE, tokens, LANES), BF16),
        ],
        scratch_shapes=[
            pltpu.VMEM(x.shape, BF16),
            pltpu.VMEM(w_key.shape, BF16),
            pltpu.VMEM(w_value.shape, BF16),
            pltpu.SemaphoreType.DMA((2 + tokens // block,)),
        ],
        compiler_params=params(24),
        name="make_keys_values",
    )(in_hbm(x), in_hbm(w_key), in_hbm(w_value))


def split_levels(levels, lane):
    first = levels.astype(BF16).astype(F32)
    rest = levels - first
    second = rest.astype(BF16).astype(F32)
    third = rest - second
    parts = jnp.where(lane < 4, first, jnp.where(lane < 8, second, third))
    return jnp.where(lane < 12, parts, 0.0)


def level_rows(rows):
    return rows // (2 * LANES) * LEVEL_ROWS


def attend_kernel(count, fetched, *refs):
    query_refs, (key_ref, value_ref) = refs[:count], refs[count : count + 2]
    out_refs = refs[count + 2 + fetched :][:count]
    copies = []
    if fetched:
        sems = refs[-1]
        sources, kept = refs[count + 2 :][:fetched], refs[2 * count + 2 + fetched :][:fetched]
        for i, (source, target) in enumerate(zip(sources, kept)):
            copies.append(pltpu.make_async_copy(source, target, sems.at[i]))
    for copy in copies:
        copy.start()
    rows = query_refs[0].shape[0]
    total_rows = rows * count

    def scores_of(head):
        columns = slice(head * HEAD_DIM, (head + 1) * HEAD_DIM)
        parts = [ref[:, columns] for ref in query_refs]
        part = parts[0] if count == 1 else jnp.concatenate(parts, axis=0)
        return product(part, key_ref[head], NT)

    lane = lax.broadcasted_iota(jnp.int32, (total_rows, LANES), 1)
    levels = jnp.zeros((total_rows, LANES), F32)
    following = scores_of(0)
    even = None
    for head in range(HEADS_HERE):
        scores = following
        if head + 1 < HEADS_HERE:
            following = scores_of(head + 1)
        highest = jnp.max(scores, axis=1, keepdims=True)
        weights = jnp.exp(scores - highest).astype(BF16)
        accum = product(weights, value_ref[head])
        place = HEAD_DIM if head % 2 == 0 else 0
        total = accum[:, place : place + 1]
        mean = accum * (1.0 / total)
        levels = jnp.where(lane % 4 == head, highest + jnp.log(total), levels)
        if head % 2 == 0:
            even = mean
        else:
            both = jnp.where(lane < HEAD_DIM, even, mean).astype(BF16)
            for i, ref in enumerate(out_refs):
                columns = slice(head // 2 * LANES, (head // 2 + 1) * LANES)
                ref[:rows, columns] = both[i * rows : (i + 1) * rows]
    packed = jnp.transpose(split_levels(levels, lane))[:LEVEL_ROWS].astype(BF16)
    for i, ref in enumerate(out_refs):
        for j in range(rows // (2 * LANES)):
            start = i * rows + j * 2 * LANES
            span = slice(rows + j * LEVEL_ROWS, rows + (j + 1) * LEVEL_ROWS)
            ref[span] = packed[:, start : start + 2 * LANES]
    for copy in copies:
        copy.wait()


def attend(chunks, keys, values, fetched=()):
    count = len(chunks)
    rows = chunks[0].shape[0]
    out = jax.ShapeDtypeStruct((rows + level_rows(rows), 2 * LANES), BF16)
    vmem, hbm = pl.BlockSpec(memory_space=pltpu.VMEM), pl.BlockSpec(memory_space=pltpu.HBM)
    return pl.pallas_call(
        functools.partial(attend_kernel, count, len(fetched)),
        in_specs=[vmem] * (count + 2) + [hbm] * len(fetched),
        out_shape=[out] * count + [jax.ShapeDtypeStruct(w.shape, BF16) for w in fetched],
        scratch_shapes=[pltpu.SemaphoreType.DMA((len(fetched),))] if fetched else [],
        compiler_params=params(24),
        name="attend",
    )(*chunks, keys, values, *[in_hbm(w) for w in fetched])


def spread_matrix(count):
    source = lax.broadcasted_iota(jnp.int32, (count, 2 * LANES), 0)
    target = lax.broadcasted_iota(jnp.int32, (count, 2 * LANES), 1)
    hit = (source < 12) & (source % 4 == target // HEAD_DIM)
    return jnp.where(hit, 1.0, 0.0).astype(BF16)


def side_levels(piece):
    return piece[:, : 2 * LANES], product(piece[:, 2 * LANES :], spread_matrix(LANES))


def under_levels(piece):
    rows = piece.shape[0] * 2 * LANES // (2 * LANES + LEVEL_ROWS)
    spread = spread_matrix(LEVEL_ROWS)
    levels = [
        product(piece[start : start + LEVEL_ROWS], spread, TN)
        for start in range(rows, piece.shape[0], LEVEL_ROWS)
    ]
    return piece[:rows], jnp.concatenate(levels, axis=0)


def merged(pieces, read):
    means, levels = zip(*[read(piece) for piece in pieces])
    highest = functools.reduce(jnp.maximum, levels)
    total, accum = None, None
    for mean, level in zip(means, levels):
        factor = jnp.exp(level - highest)
        term = factor * mean.astype(F32)
        total = factor if total is None else total + factor
        accum = term if accum is None else accum + term
    return accum / total, highest, total


def merge_kernel(count, write, *refs):
    out_refs = refs[count:]
    mean, highest, total = merged([ref[...] for ref in refs[:count]], under_levels)
    levels = highest + jnp.log(total)
    lane = lax.broadcasted_iota(jnp.int32, (levels.shape[0], LANES), 1)
    one, two = levels[:, :LANES], levels[:, LANES:]
    one_other, two_other = pltpu.roll(one, HEAD_DIM, 1), pltpu.roll(two, HEAD_DIM, 1)
    head = lane % 4
    picked = jnp.where(
        head == 0, one, jnp.where(head == 1, one_other, jnp.where(head == 2, two, two_other))
    )
    write(out_refs, mean.astype(BF16), split_levels(picked, lane))


def write_halves(refs, mean, parts):
    rows = mean.shape[0] // len(refs)
    turned = jnp.transpose(parts)[:LEVEL_ROWS].astype(BF16)
    for i, ref in enumerate(refs):
        ref[:rows] = mean[i * rows : (i + 1) * rows]
        for j in range(rows // (2 * LANES)):
            start = i * rows + j * 2 * LANES
            span = slice(rows + j * LEVEL_ROWS, rows + (j + 1) * LEVEL_ROWS)
            ref[span] = turned[:, start : start + 2 * LANES]


def write_blocks(refs, mean, parts):
    count, rows, _ = refs[0].shape
    parts = parts.astype(BF16)
    for i in range(count):
        refs[0][i, :, : 2 * LANES] = mean[i * rows : (i + 1) * rows]
        refs[0][i, :, 2 * LANES :] = parts[i * rows : (i + 1) * rows]


def merge(pieces, write, shapes):
    return pl.pallas_call(
        functools.partial(merge_kernel, len(pieces), write),
        out_shape=[jax.ShapeDtypeStruct(shape, BF16) for shape in shapes],
        compiler_params=params(24),
        name="merge",
    )(*pieces)


def placed_call(kernel, name, out_shape, place, *operands):
    return pl.pallas_call(
        kernel,
        in_specs=[pl.BlockSpec(memory_space=pltpu.SMEM)]
        + [pl.BlockSpec(memory_space=pltpu.VMEM)] * len(operands),
        out_shape=out_shape,
        compiler_params=params(8),
        name=name,
    )(place, *operands)


def ordered(place_ref, low, high):
    first = place_ref[0] % 2 == 0
    return jnp.where(first, low, high), jnp.where(first, high, low)


def project_kernel(place_ref, pieces_ref, w_ref, kept_ref, sent_ref):
    pieces = [pieces_ref[i] for i in range(pieces_ref.shape[0])]
    mean, highest, total = merged(pieces, side_levels)
    projected = product(mean.astype(BF16), w_ref[...])
    columns = kept_ref.shape[1]
    halves = ordered(place_ref, projected[:, :columns], projected[:, columns:])
    kept_ref[...], sent_ref[...] = halves


def add_kernel(place_ref, kept_ref, other_ref, out_ref):
    out_ref[...] = kept_ref[...] + other_ref[...]


def residual_kernel(place_ref, one_ref, two_ref, latent_ref, out_ref):
    columns = out_ref.shape[1]
    own = latent_ref[:, pl.ds(pl.multiple_of(place_ref[0] % 2 * columns, LANES), columns)]
    out_ref[...] = (own.astype(F32) + (one_ref[...] + two_ref[...])).astype(BF16)


def mlp_kernel(
    place_ref,
    own_ref,
    other_ref,
    w_up_ref,
    w_down_hbm,
    resid_ref,
    kept_ref,
    sent_ref,
    w_down_ref,
    sem,
):
    copy = pltpu.make_async_copy(w_down_hbm, w_down_ref, sem)
    copy.start()
    columns = resid_ref.shape[2]
    halves = ordered(place_ref, own_ref[...], other_ref[...])
    residual = jnp.concatenate(halves, axis=1)
    normed = norm_rows(residual.astype(F32)).astype(BF16)
    raised = product(normed, w_up_ref[...])
    hidden = (0.5 * raised * (1.0 + lax.erf(raised * 0.5**0.5))).astype(BF16)
    copy.wait()
    share = product(hidden, w_down_ref[...]).astype(BF16)
    blocks = [share[:, i * columns : (i + 1) * columns] for i in range(4)]
    for i in range(4):
        resid_ref[i] = residual[:, i * columns : (i + 1) * columns]
    for high in range(2):
        pair = ordered(place_ref, blocks[2 * high], blocks[2 * high + 1])
        kept_ref[high], sent_ref[high] = pair


def mlp(place, own, other, w_up, w_down):
    rows, half = own.shape
    vmem, hbm = pl.BlockSpec(memory_space=pltpu.VMEM), pl.BlockSpec(memory_space=pltpu.HBM)
    return pl.pallas_call(
        mlp_kernel,
        in_specs=[pl.BlockSpec(memory_space=pltpu.SMEM), vmem, vmem, vmem, hbm],
        out_shape=[
            jax.ShapeDtypeStruct((4, rows, half // 2), BF16),
        ]
        + [jax.ShapeDtypeStruct((2, rows, half // 2), BF16)] * 2,
        scratch_shapes=[pltpu.VMEM(w_down.shape, BF16), pltpu.SemaphoreType.DMA],
        compiler_params=params(16),
        name="mlp",
    )(place, own, other, w_up, in_hbm(w_down))


def pair_kernel(place_ref, shares_ref, other_ref, kept_ref, sent_ref):
    high = place_ref[0] // 2
    for ref, index in ((kept_ref, high), (sent_ref, 1 - high)):
        ref[...] = shares_ref[index].astype(F32) + other_ref[index].astype(F32)


def close_kernel(place_ref, resid_ref, kept_ref, other_ref, out_ref):
    own = resid_ref[place_ref[0]]
    out_ref[...] = (own.astype(F32) + (kept_ref[...] + other_ref[...])).astype(BF16)


def along(value, axis, by):
    size = lax.axis_size(axis)
    return lax.ppermute(value, axis, [(i, (i + by) % size) for i in range(size)])


def swapped(value, axes, bits):
    size = lax.axis_size(axes)
    return lax.ppermute(value, axes, [(i, i ^ bits) for i in range(size)])


STEPS = (2, 1, 3)


def on_device(inputs, latent, w_query, w_key, w_value, w_out, w_up, w_down):
    queries = make_queries(latent, w_query)
    rows, columns = queries.shape
    count = lax.axis_size("z")
    spread = jnp.broadcast_to(queries[None], (count,) + queries.shape)
    part = lax.all_to_all(spread, "z", 0, 0, tiled=True).reshape(count * rows, columns)
    part = jnp.concatenate([part, swapped(part, "ylo", 1)], axis=0)
    arrived = [along(part, "x", by) for by in STEPS]
    inputs, part = lax.optimization_barrier((inputs, part))
    keys, values = make_keys_values(inputs, w_key, w_value)
    pieces = []
    for by, chunk in zip(STEPS, arrived):
        pieces.append(along(attend([chunk], keys, values)[0], "x", -by))
    piece, w_up = attend([part], keys, values, (w_up,))
    pieces.append(piece)
    half = (count * rows + level_rows(count * rows), columns)
    own, others = merge(pieces, write_halves, [half] * 2)
    block = merge([own, swapped(others, "ylo", 1)], write_blocks, [(count, rows, 3 * LANES)])[0]
    place = lax.axis_index(HEAD).astype(jnp.int32).reshape(1)
    block, place = lax.optimization_barrier((block, place))
    pieces = lax.all_to_all(block, "z", 0, 0, tiled=True)
    width = latent.shape[1]
    half = jax.ShapeDtypeStruct((rows, width // 2), F32)
    quarter = jax.ShapeDtypeStruct((rows, width // 4), F32)
    kept, sent = placed_call(project_kernel, "project", [half] * 2, place, pieces, w_out)
    other = swapped(sent, HEAD, 1)
    pair = placed_call(add_kernel, "pair_sum", half, place, kept, other)
    across = swapped(pair, HEAD, 2)
    resid_half = placed_call(
        residual_kernel,
        "residual",
        jax.ShapeDtypeStruct(half.shape, BF16),
        place,
        pair,
        across,
        latent,
    )
    resid, kept, sent = mlp(place, resid_half, swapped(resid_half, HEAD, 1), w_up, w_down)
    other = swapped(sent, HEAD, 1)
    kept, sent = placed_call(pair_kernel, "pair_shares", [quarter] * 2, place, kept, other)
    return placed_call(
        close_kernel,
        "close",
        jax.ShapeDtypeStruct(quarter.shape, BF16),
        place,
        resid,
        kept,
        swapped(sent, HEAD, 2),
    )


def solution(mesh):
    fine = Mesh(mesh.devices.reshape(4, 8, 2, 2, 2), SEQ + HEAD)
    placed = (
        P(SEQ, None),
        P(SEQ, None),
        P(None, HEAD),
        P(None, HEAD),
        P(None, HEAD),
        P(HEAD, None),
        P(None, HEAD),
        P(HEAD, None),
    )
    return jax.shard_map(
        on_device, mesh=fine, in_specs=placed, out_specs=P(SEQ, HEAD), check_vma=False
    )
```
